128 devices in a mesh: psg: 32 (over x, y_lo, z), mp: 4 (over y_hi, core).
Axes of the slice: x: 4, y: 4 (y_hi: 2, y_lo: 2; y = y_hi * 2 + y_lo), z: 4, core: 2. Of those that a mesh axis runs over, the one named last changes fastest.
Arguments:
- tokens: bfloat16 [32768, 4096], P('psg'), may hold values from -6 to 6
- lengths: int32 [128], P('psg'), may hold values from 32 to 256, as said below
- assignment: int32 [128], P('psg'), may hold values from 0 to 3, as said below
- retrieval: float32 [128], P('psg'), may hold values from -8 to 306
- enc_gain: float32 [4096], replicated, may hold values from 0.25 to 1.75
- enc_qkv: bfloat16 [3, 4096, 2048], P(None, 'psg', 'mp'), may hold values from -0.09375 to 0.09375
- position_bias: float32 [32, 32], P('mp'), may hold values from -6 to 306
- enc_output: bfloat16 [2048, 4096], P('mp', 'psg'), may hold values from -0.125 to 0.125
- final_gain: float32 [4096], replicated, may hold values from 0.25 to 1.75
- embedding: bfloat16 [32128, 4096], P('mp', 'psg'), may hold values from -18 to 18
- dec_tokens: int32 [4, 2], replicated, may hold values from 0 to 32127
- dec_gain: float32 [4096], P('psg'), may hold values from 0.25 to 1.75
- cross_query: bfloat16 [4096, 2048], P('psg', 'mp'), may hold values from -0.0234375 to 0.0234375
- cross_keyval: bfloat16 [2, 4096, 2048], P(None, 'psg', 'mp'), may hold values from -0.09375 to 0.09375
- cross_output: bfloat16 [2048, 4096], P('mp', 'psg'), may hold values from -0.25 to 0.25
Outputs:
- encoded: bfloat16 [32768, 4096], P('psg', 'mp')
- decoded: bfloat16 [4, 2, 4096], P(None, None, ('psg', 'mp'))
The draws below stay inside these ranges and needn't reach their ends.
Inputs may be any that keep to these rules, and one draw needn't show every extreme that they name: Passage p holds real tokens in its first lengths[p] slots and padding after them; in every draw all passages of some index of psg have 256 real tokens. `assignment`: every claim has exactly 32 passages.
All inputs are finite; a program needn't handle non-finite values.
Results may differ from the reference program's by a relative error of at most 0.013.
The reference program's roundings to bfloat16 on the way count: a program that leaves them out, or rounds other values in their place, can miss the bound.
Values may be sent and summed in bfloat16 or wider, within the bound.
A program may use at most 128 MiB of HBM per device.

```python
import math
import jax
import jax.numpy as jnp
import numpy as np
from jax import lax

D = 4096
HEAD_DIM = 64
VOCAB = 32128
BUCKETS = 32
MAXDIST = 128
HEADS = 32
SEQ = 256
CLAIMS = 4
POS = 2
PSG_DEV = 4
PASSAGES = 128
TOKENS = 32768
PSG_CLAIM = 32
INNER = 2048
N_MP = 4


def claim_table(key):
    order = jax.random.permutation(jax.random.fold_in(key, 11), PASSAGES)
    return (order // PSG_CLAIM).astype(jnp.int32)


def draw_assignment(key, part):
    return claim_table(key)


def draw_retrieval(key, part):
    noise = jax.random.normal(jax.random.fold_in(key, 12), (PASSAGES,), jnp.float32)
    return jnp.clip(2.0 * noise, -8.0, 8.0)


def draw_lengths(key, part):
    lengths = jax.random.randint(jax.random.fold_in(key, 21), (PASSAGES,), SEQ // 8, SEQ + 1)
    devices = PASSAGES // PSG_DEV
    full_device = jax.random.randint(jax.random.fold_in(key, 22), (), 0, devices)
    position = jnp.arange(PASSAGES)
    lengths = jnp.where(position // PSG_DEV == full_device, SEQ, lengths)
    shortest = (full_device + 1) % devices * PSG_DEV
    lengths = jnp.where(position == shortest, SEQ // 8, lengths)
    return lengths.astype(jnp.int32)


def draw_position_bias(key, part):
    noise = jax.random.normal(jax.random.fold_in(key, 31), (HEADS, BUCKETS), jnp.float32)
    return jnp.clip(noise, -4.0, 4.0)


def draw_embedding(key, part):
    column = jnp.arange(D, dtype=jnp.float32)[None, :] / D
    col_scale = jnp.exp(column * jnp.log(3.0)) * jnp.exp(jax.random.uniform(jax.random.fold_in(key, 41), (1, D), jnp.float32, 0.0, jnp.log(3.0)))
    row_scale = jnp.exp(jax.random.uniform(jax.random.fold_in(key, 42), (VOCAB, 1), jnp.float32, 0.0, jnp.log(4.0)))
    base = jnp.clip(jax.random.normal(jax.random.fold_in(key, 45), (VOCAB, D), jnp.float32), -4.0, 4.0)
    return (0.12 * base * row_scale * col_scale).astype(jnp.bfloat16)


def plant(drawn, rng, least, high):
    extent = drawn.shape
    place = [jax.random.randint(jax.random.fold_in(rng, axis), (), 0, extent[axis]) for axis in range(len(extent))]
    drawn = drawn.at[tuple(place)].set(least)
    longest = extent.index(max(extent))
    place[longest] = (place[longest] + 1) % extent[longest]
    return drawn.at[tuple(place)].set(high)


def shard_levels(key, shape, shards, least, high):
    factor_of = 1.0
    for axis_at, shards_of in shards:
        draws = jax.random.uniform(jax.random.fold_in(jax.random.fold_in(key, 6), axis_at), (shards_of,), jnp.float32, least / len(shards), high / len(shards))
        factor_of = factor_of * jnp.repeat(jnp.exp(draws), shape[axis_at] // shards_of).reshape((-1,) + (1,) * (len(shape) - 1 - axis_at))
    return factor_of


def cumulative_ranks(count, lean):
    loads = [(1 << 20) // math.isqrt(standing ** lean) + 1 for standing in range(1, count + 1)]
    deviation = 1 + sum(loads) // (1 << 30)
    return np.cumsum(np.array([max(1, weight // deviation) for weight in loads]))


def ranked_ids(stream_key, dims, count, skew):
    grid = cumulative_ranks(count, skew)
    lot = jax.random.randint(jax.random.fold_in(stream_key, 1), dims, 0, int(grid[count - 1]))
    rank = jnp.searchsorted(jnp.asarray(grid, jnp.int32), lot, side="right")
    return jax.random.permutation(jax.random.fold_in(stream_key, 2), count)[rank].astype(jnp.int32)


def scatter_about(rng, shape, scale, reach, shards=(), kind=jnp.bfloat16):
    values = jax.random.normal(rng, shape, jnp.float32) * scale
    if len(shards) > 0:
        values = shard_levels(rng, shape, shards, -0.22, 0.18) * values
    return jnp.clip(values, min=-reach, max=reach).astype(kind)


def setup_inputs(seed: int = 0) -> dict:
    seeds = jax.random.split(jax.random.key(seed), 16)
    tokens = scatter_about(seeds[0], (TOKENS, D), 1.0, 6.0, ((0, 32),))
    lengths = draw_lengths(jax.random.fold_in(seeds[15], 71), 0)
    assignment = draw_assignment(jax.random.fold_in(seeds[15], 71), 0)
    retrieval = draw_retrieval(jax.random.fold_in(seeds[15], 71), 0)
    enc_gain = jnp.clip(1.0 + 0.15 * jax.random.normal(seeds[4], (D,), jnp.float32), 0.25, 1.75)
    enc_qkv = scatter_about(seeds[5], (3, D, INNER), D ** -0.5, 0.09375, ((1, 32), (2, 4)))
    position_bias = draw_position_bias(jax.random.fold_in(seeds[15], 71), 0)
    enc_output = scatter_about(seeds[7], (INNER, D), INNER ** -0.5, 0.125, ((0, 4), (1, 32)))
    final_gain = jnp.clip(1.0 + 0.15 * jax.random.normal(seeds[8], (D,), jnp.float32), 0.25, 1.75)
    embedding = draw_embedding(jax.random.fold_in(seeds[15], 71), 0)
    dec_tokens = plant(ranked_ids(seeds[10], (CLAIMS, POS), VOCAB, 2), jax.random.fold_in(seeds[10], 3), 0, VOCAB - 1).astype(jnp.int32)
    dec_gain = jnp.clip(1.0 + 0.15 * jax.random.normal(seeds[11], (D,), jnp.float32), 0.25, 1.75)
    cross_query = scatter_about(seeds[12], (D, INNER), (16 * D) ** -0.5, 0.0234375, ((0, 32), (1, 4)))
    cross_keyval = scatter_about(seeds[13], (2, D, INNER), D ** -0.5, 0.09375, ((1, 32), (2, 4)))
    cross_output = scatter_about(seeds[14], (INNER, D), (INNER // 4) ** -0.5, 0.25, ((0, 4), (1, 32)))
    return {"tokens": tokens, "lengths": lengths, "assignment": assignment, "retrieval": retrieval, "enc_gain": enc_gain, "enc_qkv": enc_qkv, "position_bias": position_bias, "enc_output": enc_output, "final_gain": final_gain, "embedding": embedding, "dec_tokens": dec_tokens, "dec_gain": dec_gain, "cross_query": cross_query, "cross_keyval": cross_keyval, "cross_output": cross_output}


EPSILON = 1e-06
MASKED = -1e+30
HIGHEST = lax.Precision.HIGHEST

def bucket_onehot(length, buckets, max_distance):
    halfway = buckets // 2
    exact_max = halfway // 2
    relative_list = list(range(-(length - 1), length))
    beyond_list = [min(halfway - 1, exact_max + math.floor(math.log(max(abs(shift), 1) / exact_max) / math.log(max_distance / exact_max) * (halfway - exact_max))) for shift in relative_list]
    relative = np.array(relative_list)
    beyond = np.array(beyond_list)
    distance = np.abs(relative)
    bucket_ids = np.where(relative > 0, halfway, 0) + np.where(distance < exact_max, distance, beyond)
    return (bucket_ids[None, :] == np.arange(buckets)[:, None]).astype(np.float32)

def toeplitz(vectors):
    heads_count, width_all = vectors.shape
    length = (width_all + 1) // 2
    padded = jnp.concatenate([vectors, jnp.zeros((heads_count, 1), vectors.dtype)], axis=1)
    rolled = jnp.roll(padded, -(length - 1), axis=1)
    repeated = jnp.tile(rolled, (1, length))[:, :length * (2 * length - 1)]
    return repeated.reshape(heads_count, length, 2 * length - 1)[:, :, :length]

def rms_norm(values, norm_gain):
    values = values.astype(jnp.float32)
    inverse = lax.rsqrt(lax.optimization_barrier(jnp.mean(values * values, axis=-1, keepdims=True)) + EPSILON)
    return values * inverse * norm_gain

def rounded(values):
    return lax.optimization_barrier(values.astype(jnp.bfloat16))

def reference(tokens, lengths, assignment, retrieval, enc_gain, enc_qkv, position_bias, enc_output, final_gain, embedding, dec_tokens, dec_gain, cross_query, cross_keyval, cross_output):
    query_rows = CLAIMS * POS
    group_cols = INNER // N_MP
    bias_table = jnp.dot(position_bias, jnp.asarray(bucket_onehot(SEQ, BUCKETS, MAXDIST)), precision=HIGHEST)
    pair_bias = toeplitz(bias_table)
    out_groups = enc_output.astype(jnp.float32).reshape(N_MP, group_cols, D)
    embedded = embedding[dec_tokens.reshape(-1)]
    dquery = rms_norm(embedded, dec_gain)
    cquery = jnp.dot(dquery, cross_query.astype(jnp.float32), precision=HIGHEST).reshape(query_rows, HEADS, HEAD_DIM)
    row_claim = jnp.arange(query_rows) // POS
    positions = jnp.arange(SEQ)

    def passage_step(state_in, inputs):
        run_max, run_total, run_acc = state_in
        passage, length, owner_claim, score_bias = inputs
        normed = rms_norm(passage, enc_gain).astype(jnp.bfloat16)
        query_heads = rounded(jnp.dot(normed, enc_qkv[0], preferred_element_type=jnp.float32)).astype(jnp.float32).reshape(SEQ, HEADS, HEAD_DIM)
        key_heads = rounded(jnp.dot(normed, enc_qkv[1], preferred_element_type=jnp.float32)).astype(jnp.float32).reshape(SEQ, HEADS, HEAD_DIM)
        value_heads = rounded(jnp.dot(normed, enc_qkv[2], preferred_element_type=jnp.float32)).astype(jnp.float32).reshape(SEQ, HEADS, HEAD_DIM)
        scores = jnp.einsum('ihd,jhd->hij', query_heads, key_heads, precision=HIGHEST) + pair_bias
        valid_keys = positions < length
        scores = jnp.where(valid_keys[None, None, :], scores, MASKED)
        weights = jnp.exp(scores - lax.optimization_barrier(jnp.max(scores, axis=-1, keepdims=True)))
        probabilities = rounded(weights / lax.optimization_barrier(jnp.sum(weights, axis=-1, keepdims=True))).astype(jnp.float32)
        attended = rounded(jnp.einsum('hij,jhd->ihd', probabilities, value_heads, precision=HIGHEST)).astype(jnp.float32)
        attended = attended.reshape(SEQ, N_MP, group_cols)
        partials = rounded(jnp.einsum('sgc,gcd->gsd', attended, out_groups, precision=HIGHEST)).astype(jnp.float32)
        encoded = (passage.astype(jnp.float32) + lax.optimization_barrier(jnp.sum(partials, axis=0))).astype(jnp.bfloat16)
        memory = rms_norm(encoded, final_gain).astype(jnp.bfloat16)
        cross_keys = jnp.dot(memory, cross_keyval[0], preferred_element_type=jnp.float32).reshape(SEQ, HEADS, HEAD_DIM)
        cross_values = jnp.dot(memory, cross_keyval[1], preferred_element_type=jnp.float32).reshape(SEQ, HEADS, HEAD_DIM)
        cross_scores = jnp.einsum('rhd,jhd->rhj', cquery, cross_keys, precision=HIGHEST) + score_bias
        usable = ((positions[None, :] < length) & (row_claim[:, None] == owner_claim))[:, None, :]
        masked = jnp.where(usable, cross_scores, MASKED)
        new_max = jnp.maximum(run_max, lax.optimization_barrier(jnp.max(masked, axis=-1)))
        shrink = jnp.exp(run_max - new_max)
        weights_c = jnp.where(usable, jnp.exp(masked - new_max[..., None]), 0.0)
        run_total = run_total * shrink + lax.optimization_barrier(jnp.sum(weights_c, axis=-1))
        run_acc = run_acc * shrink[..., None] + jnp.einsum('rhj,jhd->rhd', weights_c, cross_values, precision=HIGHEST)
        return ((new_max, run_total, run_acc), encoded)
    start_state = (jnp.full((query_rows, HEADS), MASKED, jnp.float32), jnp.zeros((query_rows, HEADS), jnp.float32), jnp.zeros((query_rows, HEADS, HEAD_DIM), jnp.float32))
    final_state, encoded = lax.scan(passage_step, start_state, (tokens.reshape(PASSAGES, SEQ, D), lengths, assignment, retrieval))
    cross_attn = (final_state[2] / final_state[1][..., None]).reshape(query_rows, INNER)
    decoded = (embedded.astype(jnp.float32) + jnp.dot(cross_attn, cross_output.astype(jnp.float32), precision=HIGHEST)).astype(jnp.bfloat16)
    return (encoded.reshape(TOKENS, D), decoded.reshape(CLAIMS, POS, D))
```

```python
import functools
import math

import jax
import jax.numpy as jnp
import numpy as np
from jax import lax
from jax.experimental import pallas as pl
from jax.experimental.pallas import tpu as pltpu
from jax.sharding import PartitionSpec as P

D = 4096
HEAD_DIM = 64
BUCKETS = 32
MAXDIST = 128
SEQ = 256
CLAIMS = 4
POS = 2
NPSG = 32
NMP = 4
EPSILON = 1e-06
MASKED = -1e30
HIGHEST = lax.Precision.HIGHEST
MESH = pl.DeviceIdType.MESH
ANY = pl.BlockSpec(memory_space=pl.ANY)
VMEM = pl.BlockSpec(memory_space=pltpu.VMEM)


def bucket_onehot(length, buckets, max_distance):
    halfway = buckets // 2
    exact_max = halfway // 2
    relative_list = list(range(-(length - 1), length))
    beyond_list = [
        min(
            halfway - 1,
            exact_max
            + math.floor(
                math.log(max(abs(shift), 1) / exact_max)
                / math.log(max_distance / exact_max)
                * (halfway - exact_max)
            ),
        )
        for shift in relative_list
    ]
    relative = np.array(relative_list)
    beyond = np.array(beyond_list)
    distance = np.abs(relative)
    bucket_ids = np.where(relative > 0, halfway, 0) + np.where(
        distance < exact_max, distance, beyond
    )
    return (bucket_ids[None, :] == np.arange(buckets)[:, None]).astype(np.float32)


def toeplitz(vectors):
    heads_count, width_all = vectors.shape
    length = (width_all + 1) // 2
    padded = jnp.concatenate([vectors, jnp.zeros((heads_count, 1), vectors.dtype)], axis=1)
    rolled = jnp.roll(padded, -(length - 1), axis=1)
    repeated = jnp.tile(rolled, (1, length))[:, : length * (2 * length - 1)]
    return repeated.reshape(heads_count, length, 2 * length - 1)[:, :, :length]


def rms_norm(values, norm_gain):
    values = values.astype(jnp.float32)
    inverse = lax.rsqrt(jnp.mean(values * values, axis=-1, keepdims=True) + EPSILON)
    return values * inverse * norm_gain


def place():
    psg = lax.axis_index("psg")
    mp = lax.axis_index("mp")
    return psg // 8, (psg // 4) % 2, psg % 4, mp // 2, mp % 2


def psg_of(x, yl, z):
    return x * 8 + yl * 4 + z


def remote(src, dst, send_sem, recv_sem, device):
    return pltpu.make_async_remote_copy(
        src_ref=src,
        dst_ref=dst,
        send_sem=send_sem,
        recv_sem=recv_sem,
        device_id=device,
        device_id_type=MESH,
    )


def signal(device):
    pl.semaphore_signal(
        pltpu.get_barrier_semaphore(), inc=1, device_id=device, device_id_type=MESH
    )


def psg_gather_kernel(src, out, send_sem, recv_sem, own_sem):
    me = lax.axis_index("psg")
    mp = lax.axis_index("mp")

    def greet(k, c):
        signal((lax.rem(me + k, NPSG), mp))
        return c

    lax.fori_loop(1, NPSG, greet, 0)
    own = pltpu.make_async_copy(src, out.at[me], own_sem)
    own.start()
    pl.semaphore_wait(pltpu.get_barrier_semaphore(), NPSG - 1)

    def copy(k):
        return remote(
            src, out.at[me], send_sem.at[k], recv_sem.at[k], (lax.rem(me + k, NPSG), mp)
        )

    def start(k, c):
        copy(k).start()
        return c

    lax.fori_loop(1, NPSG, start, 0)

    def finish(k, c):
        copy(k).wait()
        return c

    lax.fori_loop(1, NPSG, finish, 0)
    own.wait()


def psg_gather(x, collective_id):
    return pl.pallas_call(
        psg_gather_kernel,
        out_shape=jax.ShapeDtypeStruct((NPSG,) + x.shape, x.dtype),
        in_specs=[VMEM],
        out_specs=VMEM,
        scratch_shapes=[
            pltpu.SemaphoreType.DMA((NPSG,)),
            pltpu.SemaphoreType.DMA((NPSG,)),
            pltpu.SemaphoreType.DMA,
        ],
        compiler_params=pltpu.CompilerParams(
            collective_id=collective_id, has_side_effects=True
        ),
    )(x)


def mp_exchange_kernel(split, src, out, send_sem, recv_sem, own_sem):
    psg = lax.axis_index("psg")
    me = lax.axis_index("mp")
    for k in range(1, NMP):
        signal((psg, lax.rem(me + k, NMP)))
    own = pltpu.make_async_copy(src.at[me] if split else src, out.at[me], own_sem)
    own.start()
    pl.semaphore_wait(pltpu.get_barrier_semaphore(), NMP - 1)
    copies = []
    for k in range(1, NMP):
        to = lax.rem(me + k, NMP)
        copies.append(
            remote(
                src.at[to] if split else src,
                out.at[me],
                send_sem.at[k],
                recv_sem.at[k],
                (psg, to),
            )
        )
        copies[-1].start()
    for copy in copies:
        copy.wait()
    own.wait()


def mp_exchange(x, collective_id, split):
    shape = x.shape if split else (NMP,) + x.shape
    return pl.pallas_call(
        functools.partial(mp_exchange_kernel, split),
        out_shape=jax.ShapeDtypeStruct(shape, x.dtype),
        in_specs=[VMEM],
        out_specs=VMEM,
        scratch_shapes=[
            pltpu.SemaphoreType.DMA((NMP,)),
            pltpu.SemaphoreType.DMA((NMP,)),
            pltpu.SemaphoreType.DMA,
        ],
        compiler_params=pltpu.CompilerParams(
            collective_id=collective_id, has_side_effects=True
        ),
    )(x)


def spread_kernel(src, out, send_sem, recv_sem, own_sem):
    psg = lax.axis_index("psg")
    mp = lax.axis_index("mp")
    x = psg // 8
    mine = x == mp

    def greet(k, c):
        frm = lax.rem(psg + k, NPSG)

        @pl.when(jnp.logical_or(k > 0, jnp.logical_not(mine)))
        def _():
            signal((frm, x))

        return c

    lax.fori_loop(0, NPSG, greet, 0)
    first = lax.rem(psg, 8) * 4 + mp

    def copy(k):
        t = lax.rem(first + k, NPSG)
        c, m = t // 4, lax.rem(t, 4)
        return remote(src.at[c, m], out.at[psg], send_sem.at[k], recv_sem.at[psg], (mp * 8 + c, m))

    @pl.when(mine)
    def _():
        own = pltpu.make_async_copy(src.at[lax.rem(psg, 8), mp], out.at[psg], own_sem)
        own.start()
        own.wait()
        pl.semaphore_wait(pltpu.get_barrier_semaphore(), NPSG - 1)

    @pl.when(jnp.logical_not(mine))
    def _():
        pl.semaphore_wait(pltpu.get_barrier_semaphore(), NPSG)
        copy(0).start()

    def start(k, c):
        copy(k).start()
        return c

    lax.fori_loop(1, NPSG, start, 0)

    def arrived(k, c):
        frm = lax.rem(psg + k, NPSG)
        remote(src.at[0, 0], out.at[frm], send_sem.at[0], recv_sem.at[frm], (frm, x)).wait_recv()
        return c

    def sent(k, c):
        copy(k).wait_send()
        return c

    @pl.when(jnp.logical_not(mine))
    def _():
        arrived(0, 0)
        copy(0).wait_send()

    lax.fori_loop(1, NPSG, arrived, 0)
    lax.fori_loop(1, NPSG, sent, 0)


def spread(x, collective_id):
    return pl.pallas_call(
        spread_kernel,
        out_shape=jax.ShapeDtypeStruct((NPSG,) + x.shape[2:], x.dtype),
        in_specs=[VMEM],
        out_specs=VMEM,
        scratch_shapes=[
            pltpu.SemaphoreType.DMA((NPSG,)),
            pltpu.SemaphoreType.DMA((NPSG,)),
            pltpu.SemaphoreType.DMA,
        ],
        compiler_params=pltpu.CompilerParams(
            collective_id=collective_id, has_side_effects=True
        ),
    )(x)


ROWS_A = (0, 16)
ROWS_B = (16, 16)
ROWS_D = (32, 48)
ROWS_E = (80, 48)
ALL = slice(None)


def weights_kernel(w_ref, b_ref, g_ref, e_ref, send_sem, recv_sem, own_sem):
    x, yl, z, yh, core = place()
    psg = lax.axis_index("psg")
    mp = lax.axis_index("mp")
    y_dev = (psg_of(x, 1 - yl, z), mp)

    def dev(axis, step):
        if axis == "x":
            return (psg_of(lax.rem(x + step, 4), yl, z), mp)
        return (psg_of(x, yl, lax.rem(z + step, 4)), mp)

    same_half = (x // 2) == yh
    yl_to = jnp.where(same_half, yl, 1 - yl)

    def block_to(k):
        return (psg_of(lax.rem(x + k, 4), yl_to, z), x)

    mine = x == mp

    for axis in ("x", "z"):
        signal(dev(axis, 1))
        signal(dev(axis, 3))
    signal(y_dev)
    for m in range(NMP):
        own_half = (m // 2) == yh
        frm = psg_of(mp, jnp.where(own_half, yl, 1 - yl), z)

        @pl.when(jnp.logical_not(jnp.logical_and(mine, m == mp)))
        def _():
            signal((frm, m))

    own = pltpu.make_async_copy(w_ref, g_ref.at[:, x, yl, z], own_sem.at[0])
    own.start()

    def g(xs, ys, zs, rows, cols=None):
        c = ALL if cols is None else pl.ds(cols * 256, 256)
        return g_ref.at[:, xs, ys, zs, pl.ds(rows[0], rows[1]), c]

    def send(t, src, dst, device):
        copy = remote(src, dst, send_sem.at[t], recv_sem.at[t], device)
        copy.start()
        return copy

    sent = []

    class Ring:
        def __init__(self, t, axis, piece, first=None):
            self.t, self.axis, self.piece = t, axis, piece
            at = x if axis == "x" else z
            self.at = at
            src = piece(at) if first is None else first
            self.up = send(t, src, piece(at), dev(axis, 1))
            self.down = send(t + 1, src, piece(at), dev(axis, 3))
            sent.extend([self.up, self.down])

        def forward(self):
            below = lax.rem(self.at + 3, 4)
            above = lax.rem(self.at + 1, 4)
            self.up.wait_recv()
            self.f_up = send(
                self.t + 2, self.piece(below, 0), self.piece(below, 0), dev(self.axis, 1)
            )
            self.down.wait_recv()
            self.f_down = send(
                self.t + 3, self.piece(above, 1), self.piece(above, 1), dev(self.axis, 3)
            )
            sent.extend([self.f_up, self.f_down])

        def end(self):
            self.f_up.wait_recv()
            self.f_down.wait_recv()

    def w(rows):
        return w_ref.at[:, pl.ds(rows[0], rows[1]), :]

    pl.semaphore_wait(pltpu.get_barrier_semaphore(), jnp.where(mine, 8, 9))

    yd = send(0, w(ROWS_D), g(x, yl, z, ROWS_D), y_dev)
    ye = send(1, w(ROWS_E), g(x, yl, z, ROWS_E), y_dev)
    sent.extend([yd, ye])
    a1 = Ring(4, "x", lambda v, c=None: g(v, yl, z, ROWS_A, c), w(ROWS_A))
    b1 = Ring(8, "z", lambda v, c=None: g(x, yl, v, ROWS_B, c), w(ROWS_B))
    own.wait()
    a1.forward()
    b1.forward()
    a1.end()
    b1.end()
    a2 = Ring(12, "z", lambda v, c=None: g(ALL, yl, v, ROWS_A, c))
    b2 = Ring(16, "x", lambda v, c=None: g(v, yl, ALL, ROWS_B, c))
    yd.wait_recv()
    ye.wait_recv()
    d2 = Ring(20, "x", lambda v, c=None: g(v, ALL, z, ROWS_D, c))
    e2 = Ring(24, "z", lambda v, c=None: g(x, ALL, v, ROWS_E, c))
    a2.forward()
    b2.forward()
    a2.end()
    b2.end()
    ya = send(2, g(ALL, yl, ALL, ROWS_A), g(ALL, yl, ALL, ROWS_A), y_dev)
    yb = send(3, g(ALL, yl, ALL, ROWS_B), g(ALL, yl, ALL, ROWS_B), y_dev)
    sent.extend([ya, yb])
    d2.forward()
    e2.forward()
    d2.end()
    e2.end()
    d3 = Ring(28, "z", lambda v, c=None: g(ALL, ALL, v, ROWS_D, c))
    e3 = Ring(32, "x", lambda v, c=None: g(v, ALL, ALL, ROWS_E, c))

    def e(ms, yls, zs):
        col = pl.multiple_of((yls * 4 + zs) * 128, 128)
        return e_ref.at[ms, :, pl.ds(col, 128)]

    for k in range(4):
        def remote_send():
            remote(
                b_ref, e(mp, yl, z), send_sem.at[36 + k], recv_sem.at[40 + mp], block_to(k)
            ).start()

        if k == 0:

            @pl.when(mine)
            def _():
                pltpu.make_async_copy(b_ref, e(mp, yl, z), own_sem.at[1]).start()

            pl.when(jnp.logical_not(mine))(remote_send)
        else:
            remote_send()
    for m in range(NMP):
        got = remote(b_ref, e(m, yl, z), send_sem.at[36], recv_sem.at[40 + m], y_dev)
        self_block = jnp.logical_and(mine, m == mp)
        pl.when(jnp.logical_not(self_block))(got.wait_recv)

    @pl.when(mine)
    def _():
        pltpu.make_async_copy(b_ref, e(mp, yl, z), own_sem.at[1]).wait()

    near = pl.ds(yh * 2, 2)
    far = pl.ds(2 - yh * 2, 2)
    y1 = send(44, e(near, yl, z), e(near, yl, z), y_dev)
    y2 = send(45, e(far, 1 - yl, z), e(far, 1 - yl, z), y_dev)
    sent.extend([y1, y2])
    y1.wait_recv()
    y2.wait_recv()

    d3.forward()
    e3.forward()

    def e_piece(v, c=None):
        return e(ALL, c, v)

    rings = []
    for i in range(2):
        up = send(46 + i, e(ALL, i, z), e(ALL, i, z), dev("z", 1))
        down = send(48 + i, e(ALL, i, z), e(ALL, i, z), dev("z", 3))
        rings.append((up, down))
        sent.extend([up, down])
    below = lax.rem(z + 3, 4)
    above = lax.rem(z + 1, 4)
    rings[0][0].wait_recv()
    f_up = send(50, e(ALL, 0, below), e(ALL, 0, below), dev("z", 1))
    rings[1][1].wait_recv()
    f_down = send(51, e(ALL, 1, above), e(ALL, 1, above), dev("z", 3))
    sent.extend([f_up, f_down])
    rings[1][0].wait_recv()
    rings[0][1].wait_recv()
    ya.wait_recv()
    yb.wait_recv()
    d3.end()
    e3.end()
    f_up.wait_recv()
    f_down.wait_recv()
    for copy in sent:
        copy.wait_send()
    for k in range(4):
        done = remote(b_ref, e(mp, yl, z), send_sem.at[36 + k], recv_sem.at[40], y_dev)
        if k == 0:
            pl.when(jnp.logical_not(mine))(done.wait_send)
        else:
            done.wait_send()


def gather_weights(enc_qkv, block):
    return pl.pallas_call(
        weights_kernel,
        out_shape=(
            jax.ShapeDtypeStruct((3, 4, 2, 4, 128, 512), jnp.bfloat16),
            jax.ShapeDtypeStruct((NMP, block.shape[0], 1024), jnp.bfloat16),
        ),
        in_specs=[ANY, ANY],
        out_specs=(ANY, ANY),
        scratch_shapes=[
            pltpu.SemaphoreType.DMA((52,)),
            pltpu.SemaphoreType.DMA((52,)),
            pltpu.SemaphoreType.DMA((2,)),
        ],
        compiler_params=pltpu.CompilerParams(collective_id=1, has_side_effects=True),
    )(enc_qkv, block)


def attended_kernel(src, out, transit, send_sem, recv_sem, own_sem):
    x, yl, z, yh, core = place()
    psg = lax.axis_index("psg")
    mp = lax.axis_index("mp")
    half = src.shape[0] // 2
    y = yh * 2 + yl

    def dev(step, other_core=False):
        t = lax.rem(y + step, 4)
        c = 1 - core if other_core else core
        return (psg_of(x, lax.rem(t, 2), z), (t // 2) * 2 + c)

    for step in (1, 3):
        signal(dev(step))
    signal(dev(0, True))
    own = pltpu.make_async_copy(src, out.at[mp], own_sem)
    own.start()
    pl.semaphore_wait(pltpu.get_barrier_semaphore(), 3)
    far = (1 - yh) * 2 + core
    quarter = half // 2
    sent = []

    def send(t, s, d, device):
        copy = remote(s, d, send_sem.at[t], recv_sem.at[t], device)
        copy.start()
        sent.append(copy)
        return copy

    hops = []
    for q in range(2):
        for up in range(2):
            rows = pl.ds(up * half + q * quarter, quarter)
            hops.append(
                send(
                    q * 2 + up, src.at[rows], transit.at[up, pl.ds(q * quarter, quarter)],
                    dev(1 if up == 0 else 3),
                )
            )
    chip = send(8, src, out.at[mp], dev(0, True))
    ends = []
    y_src = [lax.rem(y + 3, 4), lax.rem(y + 1, 4)]
    for q in range(2):
        for up in range(2):
            hops[q * 2 + up].wait_recv()
            rows = pl.ds(up * half + q * quarter, quarter)
            slot = (y_src[up] // 2) * 2 + core
            ends.append(
                send(
                    4 + q * 2 + up, transit.at[up, pl.ds(q * quarter, quarter)],
                    out.at[slot, rows], dev(1 if up == 0 else 3),
                )
            )
    last = []
    for q in range(2):
        for up in range(2):
            ends[q * 2 + up].wait_recv()
            rows = pl.ds(up * half + q * quarter, quarter)
            last.append(
                send(9 + q * 2 + up, out.at[far, rows], out.at[far, rows], dev(0, True))
            )
    chip.wait_recv()
    for copy in last:
        copy.wait_recv()
    for copy in sent:
        copy.wait_send()
    own.wait()


def gather_attended(x):
    rows, cols = x.shape
    return pl.pallas_call(
        attended_kernel,
        out_shape=jax.ShapeDtypeStruct((NMP, rows, cols), x.dtype),
        in_specs=[VMEM],
        out_specs=VMEM,
        scratch_shapes=[
            pltpu.VMEM((2, rows // 2, cols), x.dtype),
            pltpu.SemaphoreType.DMA((13,)),
            pltpu.SemaphoreType.DMA((13,)),
            pltpu.SemaphoreType.DMA,
        ],
        compiler_params=pltpu.CompilerParams(
            collective_id=2, has_side_effects=True, vmem_limit_bytes=32 << 20
        ),
    )(x)


def high_low(values):
    high = values.astype(jnp.bfloat16)
    low = (values - high.astype(jnp.float32)).astype(jnp.bfloat16)
    return high, low


def shards(
    tokens,
    lengths,
    assignment,
    retrieval,
    enc_gain,
    enc_qkv,
    position_bias,
    enc_output,
    final_gain,
    embedding,
    dec_tokens,
    dec_gain,
    cross_query,
    cross_keyval,
    cross_output,
):
    f32 = jnp.float32
    psg = lax.axis_index("psg")
    mp = lax.axis_index("mp")
    tok_rows = tokens.shape[0]
    passages_here = lengths.shape[0]
    heads_here = enc_qkv.shape[2] // HEAD_DIM
    query_rows = CLAIMS * POS
    positions = jnp.arange(SEQ)

    vocab_here = embedding.shape[0]
    token_ids = dec_tokens.reshape(-1) - mp * vocab_here
    held = (token_ids >= 0) & (token_ids < vocab_here)
    row_ids = jnp.clip(token_ids, 0, vocab_here - 1)
    rows = [lax.dynamic_slice_in_dim(embedding, row_ids[i], 1, 0) for i in range(query_rows)]
    found = jnp.where(held[:, None], jnp.concatenate(rows, axis=0).astype(f32), 0.0)
    embedded = jnp.sum(mp_exchange(found, 3, False), axis=0)
    part = jnp.dot(embedded * dec_gain, cross_query.astype(f32), precision=HIGHEST)
    squares = jnp.sum(embedded * embedded, axis=1, keepdims=True)
    part = jnp.concatenate([part, jnp.broadcast_to(squares, (query_rows, 128))], axis=1)
    joined = jnp.sum(psg_gather(part, 4), axis=0)
    cquery = joined[:, :512] * lax.rsqrt(joined[:, 512:513] / D + EPSILON)
    folded = jnp.einsum(
        "rhd,chd->rhc",
        cquery.reshape(query_rows, heads_here, HEAD_DIM),
        cross_keyval[0].astype(f32).reshape(128, heads_here, HEAD_DIM),
        precision=HIGHEST,
    ).reshape(query_rows * heads_here, 128)
    gain_here = lax.dynamic_slice_in_dim(final_gain, psg * 128, 128, 0)
    high, low = high_low(folded * gain_here)
    block = jnp.concatenate([enc_output, high, low], axis=0)

    qkv_all, blocks = gather_weights(enc_qkv, block)
    qkv_all = qkv_all.reshape(3, D, 512)

    normed = rms_norm(tokens, enc_gain).astype(jnp.bfloat16)
    projected = jnp.einsum("td,kdc->ktc", normed, qkv_all, preferred_element_type=f32)
    shaped = projected.astype(jnp.bfloat16).reshape(3, passages_here, SEQ, heads_here, HEAD_DIM)
    bias_table = jnp.dot(
        position_bias, jnp.asarray(bucket_onehot(SEQ, BUCKETS, MAXDIST)), precision=HIGHEST
    )
    pair_bias = toeplitz(bias_table)
    scores = (
        jnp.einsum("pihd,pjhd->phij", shaped[0], shaped[1], preferred_element_type=f32)
        + pair_bias[None]
    )
    valid_keys = positions[None, :] < lengths[:, None]
    scores = jnp.where(valid_keys[:, None, None, :], scores, MASKED)
    weights = jnp.exp(scores - jnp.max(scores, axis=-1, keepdims=True))
    probabilities = (weights / jnp.sum(weights, axis=-1, keepdims=True)).astype(jnp.bfloat16)
    attended = jnp.einsum("phij,pjhd->pihd", probabilities, shaped[2], preferred_element_type=f32)
    attended = attended.astype(jnp.bfloat16).reshape(tok_rows, 512)

    groups = gather_attended(attended)
    width = blocks.shape[2]
    summed = jnp.zeros((tok_rows, width), f32)
    for m in range(NMP):
        summed = summed + jnp.dot(
            groups[m], blocks[m, :512], preferred_element_type=f32
        ).astype(jnp.bfloat16).astype(f32)
    tokens_here = lax.dynamic_slice_in_dim(tokens, mp * width, width, 1)
    encoded = (tokens_here.astype(f32) + summed).astype(jnp.bfloat16)
    encoded_f = encoded.astype(f32)
    squares = jnp.sum(encoded_f * encoded_f, axis=1).reshape(passages_here, SEQ)

    rows_u = blocks[:, 512:].reshape(NMP, 2, CLAIMS, POS * heads_here, width)
    claim_u = jnp.stack(
        [lax.dynamic_index_in_dim(rows_u, assignment[i], 2, False) for i in range(passages_here)],
        axis=2,
    )
    per_psg = encoded.reshape(passages_here, SEQ, width)
    partial = jnp.einsum("mapnd,pkd->mapnk", claim_u, per_psg, preferred_element_type=f32)
    partial = (partial[:, 0] + partial[:, 1]).reshape(NMP, passages_here * POS * heads_here, SEQ)
    extra = jnp.broadcast_to(
        jnp.concatenate([squares, jnp.zeros_like(squares)], axis=0)[None],
        (NMP, 2 * passages_here, SEQ),
    )
    raw = jnp.sum(mp_exchange(jnp.concatenate([partial, extra], axis=1), 5, True), axis=0)
    n_rows = passages_here * POS * heads_here
    inverse = lax.rsqrt(raw[n_rows : n_rows + passages_here] / D + EPSILON)
    cross = raw[:n_rows].reshape(passages_here, POS * heads_here, SEQ)
    cross = cross * inverse[:, None, :] + retrieval[:, None, None]
    usable = (positions[None, :] < lengths[:, None])[:, None, :]
    masked = jnp.where(usable, cross, MASKED)
    onehot = assignment[None, :] == jnp.arange(CLAIMS)[:, None]
    psg_max = jnp.max(masked, axis=-1)
    local_max = jnp.max(jnp.where(onehot[:, :, None], psg_max[None], MASKED), axis=1)
    chosen_max = jnp.max(jnp.where(onehot[:, :, None], local_max[:, None], MASKED), axis=0)
    weights_c = jnp.where(
        usable, jnp.exp(masked - chosen_max[:, :, None]), 0.0
    )
    local_total = jnp.sum(
        jnp.where(onehot[:, :, None], jnp.sum(weights_c, axis=-1)[None], 0.0), axis=1
    )
    stats = jnp.stack([local_max.reshape(-1), local_total.reshape(-1)])
    stats = jnp.pad(stats, ((0, 6), (0, SEQ - stats.shape[1])))
    sent = jnp.concatenate(
        [(weights_c * inverse[:, None, :]).reshape(n_rows, SEQ), stats], axis=0
    )
    all_w = mp_exchange(sent, 6, False)
    spread_w = jnp.where(
        onehot[None, :, :, None, None],
        all_w[:, :n_rows].reshape(NMP, 1, passages_here, POS * heads_here, SEQ),
        0.0,
    )
    w_high, w_low = high_low(spread_w)
    weighted = jnp.einsum(
        "mcpnk,pkd->mcnd", w_high, per_psg, preferred_element_type=f32
    ) + jnp.einsum("mcpnk,pkd->mcnd", w_low, per_psg, preferred_element_type=f32)
    weighted = weighted.reshape(NMP, query_rows * heads_here, 8, 128).transpose(2, 0, 1, 3)
    both = jnp.concatenate([all_w[:, n_rows, :64], all_w[:, n_rows + 1, :64]], axis=1)
    both = jnp.broadcast_to(
        jnp.pad(both[:, None, :], ((0, 0), (0, 7), (0, 0)))[None], (8, NMP, 8, 128)
    )
    got = spread(jnp.concatenate([weighted, both], axis=2), 7)
    each_max = got[:, 64, :64]
    each_total = got[:, 64, 64:]
    joint_max = jnp.max(each_max, axis=0)
    scale = jnp.exp(each_max - joint_max[None])
    total = jnp.sum(scale * each_total, axis=0)
    mean_rows = jnp.sum(got[:, :64] * scale[:, :, None], axis=0) / total[:, None] * gain_here
    attn_part = jnp.einsum(
        "rhc,chd->rhd",
        mean_rows.reshape(query_rows, heads_here, 128),
        cross_keyval[1].astype(f32).reshape(128, heads_here, HEAD_DIM),
        precision=HIGHEST,
    ).reshape(query_rows, 512)
    cross_attn = jnp.sum(psg_gather(attn_part, 8), axis=0)
    out_part = jnp.dot(cross_attn, cross_output.astype(f32), precision=HIGHEST)
    out_sum = jnp.sum(mp_exchange(out_part, 9, False), axis=0) + embedded
    decoded = lax.dynamic_slice_in_dim(out_sum, mp * 32, 32, 1)
    return (encoded, decoded.astype(jnp.bfloat16).reshape(CLAIMS, POS, 32))


def solution(mesh):
    in_specs = (
        P("psg", None),
        P("psg"),
        P("psg"),
        P("psg"),
        P(),
        P(None, "psg", "mp"),
        P("mp", None),
        P("mp", "psg"),
        P(),
        P("mp", "psg"),
        P(),
        P("psg"),
        P("psg", "mp"),
        P(None, "psg", "mp"),
        P("mp", "psg"),
    )
    out_specs = (P("psg", "mp"), P(None, None, ("psg", "mp")))
    return jax.shard_map(shards, mesh=mesh, in_specs=in_specs, out_specs=out_specs, check_vma=False)
```

```python
import functools
import math

import jax
import jax.numpy as jnp
import numpy as np
from jax import lax
from jax.experimental import pallas as pl
from jax.experimental.pallas import tpu as pltpu
from jax.sharding import PartitionSpec as P

D = 4096
HEAD_DIM = 64
BUCKETS = 32
MAXDIST = 128
SEQ = 256
CLAIMS = 4
POS = 2
NPSG = 32
NMP = 4
EPSILON = 1e-06
MASKED = -1e30
HIGHEST = lax.Precision.HIGHEST
MESH = pl.DeviceIdType.MESH
ANY = pl.BlockSpec(memory_space=pl.ANY)
VMEM = pl.BlockSpec(memory_space=pltpu.VMEM)


def bucket_onehot(length, buckets, max_distance):
    halfway = buckets // 2
    exact_max = halfway // 2
    relative_list = list(range(-(length - 1), length))
    beyond_list = [
        min(
            halfway - 1,
            exact_max
            + math.floor(
                math.log(max(abs(shift), 1) / exact_max)
                / math.log(max_distance / exact_max)
                * (halfway - exact_max)
            ),
        )
        for shift in relative_list
    ]
    relative = np.array(relative_list)
    beyond = np.array(beyond_list)
    distance = np.abs(relative)
    bucket_ids = np.where(relative > 0, halfway, 0) + np.where(
        distance < exact_max, distance, beyond
    )
    return (bucket_ids[None, :] == np.arange(buckets)[:, None]).astype(np.float32)


def place():
    psg = lax.axis_index("psg")
    mp = lax.axis_index("mp")
    return psg // 8, (psg // 4) % 2, psg % 4, mp // 2, mp % 2


def psg_of(x, yl, z):
    return x * 8 + yl * 4 + z


def remote(src, dst, send_sem, recv_sem, device):
    return pltpu.make_async_remote_copy(
        src_ref=src,
        dst_ref=dst,
        send_sem=send_sem,
        recv_sem=recv_sem,
        device_id=device,
        device_id_type=MESH,
    )


def signal(device):
    pl.semaphore_signal(
        pltpu.get_barrier_semaphore(), inc=1, device_id=device, device_id_type=MESH
    )


def psg_gather_kernel(src, out, send_sem, recv_sem, own_sem):
    me = lax.axis_index("psg")
    mp = lax.axis_index("mp")

    def greet(k, c):
        signal((lax.rem(me + k, NPSG), mp))
        return c

    lax.fori_loop(1, NPSG, greet, 0)
    own = pltpu.make_async_copy(src, out.at[me], own_sem)
    own.start()
    pl.semaphore_wait(pltpu.get_barrier_semaphore(), NPSG - 1)

    def copy(k):
        return remote(
            src, out.at[me], send_sem.at[k], recv_sem.at[k], (lax.rem(me + k, NPSG), mp)
        )

    def start(k, c):
        copy(k).start()
        return c

    lax.fori_loop(1, NPSG, start, 0)

    def finish(k, c):
        copy(k).wait()
        return c

    lax.fori_loop(1, NPSG, finish, 0)
    own.wait()


def psg_gather(x, collective_id):
    return pl.pallas_call(
        psg_gather_kernel,
        out_shape=jax.ShapeDtypeStruct((NPSG,) + x.shape, x.dtype),
        in_specs=[VMEM],
        out_specs=VMEM,
        scratch_shapes=[
            pltpu.SemaphoreType.DMA((NPSG,)),
            pltpu.SemaphoreType.DMA((NPSG,)),
            pltpu.SemaphoreType.DMA,
        ],
        compiler_params=pltpu.CompilerParams(
            collective_id=collective_id, has_side_effects=True
        ),
    )(x)


def mp_exchange_kernel(split, src, out, send_sem, recv_sem, own_sem):
    psg = lax.axis_index("psg")
    me = lax.axis_index("mp")
    for k in range(1, NMP):
        signal((psg, lax.rem(me + k, NMP)))
    own = pltpu.make_async_copy(src.at[me] if split else src, out.at[me], own_sem)
    own.start()
    pl.semaphore_wait(pltpu.get_barrier_semaphore(), NMP - 1)
    copies = []
    for k in range(1, NMP):
        to = lax.rem(me + k, NMP)
        copies.append(
            remote(
                src.at[to] if split else src,
                out.at[me],
                send_sem.at[k],
                recv_sem.at[k],
                (psg, to),
            )
        )
        copies[-1].start()
    for copy in copies:
        copy.wait()
    own.wait()


def mp_exchange(x, collective_id, split):
    shape = x.shape if split else (NMP,) + x.shape
    return pl.pallas_call(
        functools.partial(mp_exchange_kernel, split),
        out_shape=jax.ShapeDtypeStruct(shape, x.dtype),
        in_specs=[VMEM],
        out_specs=VMEM,
        scratch_shapes=[
            pltpu.SemaphoreType.DMA((NMP,)),
            pltpu.SemaphoreType.DMA((NMP,)),
            pltpu.SemaphoreType.DMA,
        ],
        compiler_params=pltpu.CompilerParams(
            collective_id=collective_id, has_side_effects=True
        ),
    )(x)


def spread_kernel(src, out, send_sem, recv_sem, own_sem):
    psg = lax.axis_index("psg")
    mp = lax.axis_index("mp")
    x = psg // 8
    mine = x == mp

    def greet(k, c):
        frm = lax.rem(psg + k, NPSG)

        @pl.when(jnp.logical_or(k > 0, jnp.logical_not(mine)))
        def _():
            signal((frm, x))

        return c

    lax.fori_loop(0, NPSG, greet, 0)
    first = lax.rem(psg, 8) * 4 + mp

    def copy(k):
        t = lax.rem(first + k, NPSG)
        c, m = t // 4, lax.rem(t, 4)
        return remote(src.at[c, m], out.at[psg], send_sem.at[k], recv_sem.at[psg], (mp * 8 + c, m))

    @pl.when(mine)
    def _():
        own = pltpu.make_async_copy(src.at[lax.rem(psg, 8), mp], out.at[psg], own_sem)
        own.start()
        own.wait()
        pl.semaphore_wait(pltpu.get_barrier_semaphore(), NPSG - 1)

    @pl.when(jnp.logical_not(mine))
    def _():
        pl.semaphore_wait(pltpu.get_barrier_semaphore(), NPSG)
        copy(0).start()

    def start(k, c):
        copy(k).start()
        return c

    lax.fori_loop(1, NPSG, start, 0)

    def arrived(k, c):
        frm = lax.rem(psg + k, NPSG)
        remote(src.at[0, 0], out.at[frm], send_sem.at[0], recv_sem.at[frm], (frm, x)).wait_recv()
        return c

    def sent(k, c):
        copy(k).wait_send()
        return c

    @pl.when(jnp.logical_not(mine))
    def _():
        arrived(0, 0)
        copy(0).wait_send()

    lax.fori_loop(1, NPSG, arrived, 0)
    lax.fori_loop(1, NPSG, sent, 0)


def spread(x, collective_id):
    return pl.pallas_call(
        spread_kernel,
        out_shape=jax.ShapeDtypeStruct((NPSG,) + x.shape[2:], x.dtype),
        in_specs=[VMEM],
        out_specs=VMEM,
        scratch_shapes=[
            pltpu.SemaphoreType.DMA((NPSG,)),
            pltpu.SemaphoreType.DMA((NPSG,)),
            pltpu.SemaphoreType.DMA,
        ],
        compiler_params=pltpu.CompilerParams(
            collective_id=collective_id, has_side_effects=True
        ),
    )(x)


def lookup_kernel(ids, base, table, out, rows, sems):
    copies = []
    held = []
    for i in range(CLAIMS * POS):
        local = ids[i] - base[0]
        inside = jnp.logical_and(local >= 0, local < table.shape[0])
        local = jnp.clip(local, 0, table.shape[0] - 1)
        start = pl.multiple_of((local // 16) * 16, 16)
        held.append(jnp.where(inside, local - start, -1))
        copies.append(
            pltpu.make_async_copy(table.at[pl.ds(start, 16), :], rows.at[i], sems.at[i])
        )
        copies[-1].start()
    at = lax.broadcasted_iota(jnp.int32, (16, 128), 0)
    for i in range(CLAIMS * POS):
        copies[i].wait()
        picked = jnp.where(at == held[i], rows[i].astype(jnp.float32), 0.0)
        out[pl.ds(i, 1), :] = jnp.sum(picked, axis=0, keepdims=True)


def lookup(ids, base, table):
    smem = pl.BlockSpec(memory_space=pltpu.SMEM)
    return pl.pallas_call(
        lookup_kernel,
        out_shape=jax.ShapeDtypeStruct((CLAIMS * POS, 128), jnp.float32),
        in_specs=[smem, smem, ANY],
        out_specs=VMEM,
        scratch_shapes=[
            pltpu.VMEM((CLAIMS * POS, 16, 128), jnp.bfloat16),
            pltpu.SemaphoreType.DMA((CLAIMS * POS,)),
        ],
    )(ids, base, table)


def split3(values):
    high = values.astype(jnp.bfloat16)
    rest = values - high.astype(jnp.float32)
    middle = rest.astype(jnp.bfloat16)
    low = (rest - middle.astype(jnp.float32)).astype(jnp.bfloat16)
    return jnp.concatenate([high, middle, low], axis=0)


def dot3(values, weights, contract=0):
    n = values.shape[0]
    parts = lax.dot_general(
        split3(values),
        weights,
        (((1,), (contract,)), ((), ())),
        preferred_element_type=jnp.float32,
    )
    return parts[:n] + parts[n : 2 * n] + parts[2 * n :]


ALL = slice(None)


def encoder_kernel(
    tokens,
    enc_gain,
    w_ref,
    bias_in,
    onehot,
    mask_add,
    enc_output,
    final_gain,
    found,
    dec_gain,
    cross_query,
    cross_keyval,
    enc_out,
    u_out,
    emb_out,
    g_ref,
    normed,
    acc,
    qkv,
    e_ref,
    att,
    transit,
    bias,
    tok_here,
    block,
    mp_buf,
    x_buf,
    yz_buf,
    send_sem,
    recv_sem,
    own_sem,
):
    f32 = jnp.float32
    bf16 = jnp.bfloat16
    x, yl, z, yh, core = place()
    psg = lax.axis_index("psg")
    mp = lax.axis_index("mp")
    y = yh * 2 + yl
    y_dev = (psg_of(x, 1 - yl, z), mp)

    def dev(axis, step):
        if axis == "x":
            return (psg_of(lax.rem(x + step, 4), yl, z), mp)
        return (psg_of(x, yl, lax.rem(z + step, 4)), mp)

    def yz_dev(k):
        t = lax.rem(yl * 4 + z + k, 8)
        return (x * 8 + t, mp)

    def mp_dev(k):
        return (psg, lax.rem(mp + k, NMP))

    def y_step(step):
        t = lax.rem(y + step, 4)
        return (psg_of(x, lax.rem(t, 2), z), (t // 2) * 2 + core)

    other_core = (psg, yh * 2 + 1 - core)
    same_half = (x // 2) == yh
    yl_to = jnp.where(same_half, yl, 1 - yl)

    def block_to(k):
        return (psg_of(lax.rem(x + k, 4), yl_to, z), x)

    mine = x == mp

    load_tokens = pltpu.make_async_copy(tokens, normed, own_sem.at[0])
    load_tokens.start()
    own = pltpu.make_async_copy(
        w_ref, g_ref.at[:, x, z, pl.ds(pl.multiple_of(yl * 128, 128), 128), :], own_sem.at[1]
    )
    own.start()
    load_here = pltpu.make_async_copy(
        tokens.at[:, pl.ds(pl.multiple_of(mp * 1024, 128), 1024)], tok_here, own_sem.at[2]
    )
    load_here.start()
    load_block = pltpu.make_async_copy(enc_output, block.at[pl.ds(0, 512)], own_sem.at[3])
    load_block.start()

    for k in range(1, 4):
        signal(dev("x", k))
        signal(mp_dev(k))
    for k in range(1, 8):
        signal(yz_dev(k))
    signal(y_step(1))
    signal(y_step(3))
    for m in range(NMP):
        frm = psg_of(mp, jnp.where((m // 2) == yh, yl, 1 - yl), z)

        @pl.when(jnp.logical_not(jnp.logical_and(mine, m == mp)))
        def _():
            signal((frm, m))

    def g(k, xs, zs, yls, cols=None):
        rows = ALL if yls is None else pl.ds(pl.multiple_of(yls * 128, 128), 128)
        c = ALL if cols is None else pl.ds(cols[0], cols[1])
        return g_ref.at[k, xs, zs, rows, c]

    def wide(c):
        return None if c is None else (c * 256, 256)

    def low_cols(c):
        return (0, 256) if c is None else (c * 128, 128)

    def high_cols(c):
        return (256, 256) if c is None else (256 + c * 128, 128)

    sent = []

    def send(t, src, dst, device):
        copy = remote(src, dst, send_sem.at[t], recv_sem.at[t], device)
        copy.start()
        sent.append(copy)
        return copy

    class Ring:
        def __init__(self, t, axis, piece, first=None):
            self.t, self.axis, self.piece = t, axis, piece
            self.at = x if axis == "x" else z
            src = piece(self.at) if first is None else first
            self.up = send(t, src, piece(self.at), dev(axis, 1))
            self.down = send(t + 1, src, piece(self.at), dev(axis, 3))

        def forward(self):
            below = lax.rem(self.at + 3, 4)
            above = lax.rem(self.at + 1, 4)
            self.up.wait_recv()
            up = self.piece(below, 0)
            self.f_up = send(self.t + 2, up, up, dev(self.axis, 1))
            self.down.wait_recv()
            down = self.piece(above, 1)
            self.f_down = send(self.t + 3, down, down, dev(self.axis, 3))

        def end(self):
            self.f_up.wait_recv()
            self.f_down.wait_recv()

    pl.semaphore_wait(pltpu.get_barrier_semaphore(), jnp.where(mine, 18, 19))

    yd = send(0, w_ref.at[0], g(0, x, z, yl), y_dev)
    ye = send(1, w_ref.at[1], g(1, x, z, yl), y_dev)
    a1 = Ring(
        4, "x", lambda v, c=None: g(2, v, z, yl, low_cols(c)), w_ref.at[2, :, pl.ds(0, 256)]
    )
    b1 = Ring(
        8, "z", lambda v, c=None: g(2, x, v, yl, high_cols(c)), w_ref.at[2, :, pl.ds(256, 256)]
    )
    mp_buf[mp] = found[...]
    mps = [send(52 + k, found, mp_buf.at[mp], mp_dev(k)) for k in range(1, 4)]
    own.wait()
    yd.wait_recv()
    d2 = Ring(20, "x", lambda v, c=None: g(0, v, z, None, wide(c)))
    ye.wait_recv()
    e2 = Ring(24, "z", lambda v, c=None: g(1, x, v, None, wide(c)))
    a1.forward()
    b1.forward()

    for copy in mps:
        copy.wait_recv()
    emb = mp_buf[0] + mp_buf[1] + mp_buf[2] + mp_buf[3]
    emb_out[...] = emb
    terms = dot3(emb * dec_gain[...], cross_query[...])
    squares = jnp.sum(emb * emb, axis=1, keepdims=True)
    x_buf[x, :, pl.ds(0, 512)] = terms
    x_buf[x, :, pl.ds(512, 128)] = jnp.broadcast_to(squares, (8, 128))
    xs = [send(56 + k, x_buf.at[x], x_buf.at[x], dev("x", k)) for k in range(1, 4)]

    a1.end()
    a2 = Ring(12, "z", lambda v, c=None: g(2, ALL, v, yl, low_cols(c)))
    b1.end()
    b2 = Ring(16, "x", lambda v, c=None: g(2, v, ALL, yl, high_cols(c)))

    load_tokens.wait()

    def norm_rows(first, count):
        def body(i, c):
            rows = pl.ds(pl.multiple_of(i * 16, 16), 16)
            values = normed[rows, :].astype(f32)
            mean = jnp.sum(values * values, axis=1, keepdims=True) / D
            inverse = lax.rsqrt(mean + EPSILON)
            scaled = (values * inverse * enc_gain[...]).astype(bf16)
            for p in range(NPSG):
                to = ((p // 8) * 4 + p % 4) * 2 + (p // 4) % 2
                normed[rows, pl.ds(to * 128, 128)] = scaled[:, p * 128 : (p + 1) * 128]
            return c

        lax.fori_loop(first, first + count, body, 0)

    norm_rows(0, 24)

    for copy in xs:
        copy.wait_recv()
    yz = yl * 4 + z
    yz_buf[yz] = x_buf[0] + x_buf[1] + x_buf[2] + x_buf[3]
    yzs = [send(60 + k, yz_buf.at[yz], yz_buf.at[yz], yz_dev(k)) for k in range(1, 8)]

    d2.forward()
    e2.forward()
    norm_rows(24, 20)
    d2.end()
    d3 = Ring(28, "z", lambda v, c=None: g(0, ALL, v, None, wide(c)))
    e2.end()
    e3 = Ring(32, "x", lambda v, c=None: g(1, v, ALL, None, wide(c)))
    a2.forward()
    b2.forward()
    norm_rows(44, 20)

    for copy in yzs:
        copy.wait_recv()
    joined = yz_buf[0]
    for k in range(1, 8):
        joined = joined + yz_buf[k]
    cquery = joined[:, :512] * lax.rsqrt(joined[:, 512:513] / D + EPSILON)
    spread_q = jnp.broadcast_to(cquery[:, None, :], (8, 8, 512)).reshape(64, 512)
    head_of_row = lax.rem(lax.broadcasted_iota(jnp.int32, (64, 512), 0), 8)
    head_of_lane = lax.broadcasted_iota(jnp.int32, (64, 512), 1) // HEAD_DIM
    spread_q = jnp.where(head_of_row == head_of_lane, spread_q, 0.0)
    folded = dot3(spread_q, cross_keyval[0], 1)
    folded = folded * final_gain[:, pl.ds(pl.multiple_of(psg * 128, 128), 128)]
    high = folded.astype(bf16)
    load_block.wait()
    block[pl.ds(512, 64), :] = high
    block[pl.ds(576, 64), :] = (folded - high.astype(f32)).astype(bf16)

    def e(ms, yls, zs):
        col = pl.multiple_of((yls * 4 + zs) * 128, 128)
        return e_ref.at[ms, :, pl.ds(col, 128)]

    def block_copy(k):
        return remote(block, e(mp, yl, z), send_sem.at[36 + k], recv_sem.at[40 + mp], block_to(k))

    keep = pltpu.make_async_copy(block, e(mp, yl, z), own_sem.at[4])

    @pl.when(mine)
    def _():
        keep.start()

    @pl.when(jnp.logical_not(mine))
    def _():
        block_copy(0).start()

    for k in range(1, 4):
        block_copy(k).start()

    a2.end()
    low = g(2, ALL, ALL, yl, low_cols(None))
    ya = send(2, low, low, y_dev)
    b2.end()
    hi = g(2, ALL, ALL, yl, high_cols(None))
    yb = send(3, hi, hi, y_dev)

    table = dot3(bias_in[...], onehot[...])
    for h in range(8):
        row = jnp.broadcast_to(table[h : h + 1], (SEQ, 512))
        bias[h] = pltpu.roll(row, 0, 1, stride=1, stride_axis=0)[:, :SEQ]

    for m in range(NMP):
        got = remote(block, e(m, yl, z), send_sem.at[36], recv_sem.at[40 + m], y_dev)
        pl.when(jnp.logical_not(jnp.logical_and(mine, m == mp)))(got.wait_recv)

    @pl.when(mine)
    def _():
        keep.wait()

    near = pl.ds(yh * 2, 2)
    far_half = pl.ds(2 - yh * 2, 2)
    y1 = send(44, e(near, yl, z), e(near, yl, z), y_dev)
    y2 = send(45, e(far_half, 1 - yl, z), e(far_half, 1 - yl, z), y_dev)

    d3.forward()
    e3.forward()

    def product(k, rows, xi, zi):
        at = pl.multiple_of((xi * 4 + zi) * 256, 256)
        return jnp.dot(
            normed[rows, pl.ds(at, 256)], g_ref[k, xi, zi], preferred_element_type=f32
        )

    def project(step):
        def body(i, c):
            step(pl.ds(pl.multiple_of(i * 256, 256), 256))
            return c

        lax.fori_loop(0, 4, body, 0)

    def first_q(rows):
        total = None
        for xi in range(4):
            for dz in (0, 1, 3):
                term = product(0, rows, xi, lax.rem(z + dz, 4))
                total = term if total is None else total + term
        acc[0, rows, :] = total

    def first_k(rows):
        total = None
        for zi in range(4):
            for dx in (0, 1, 3):
                term = product(1, rows, lax.rem(x + dx, 4), zi)
                total = term if total is None else total + term
        acc[1, rows, :] = total

    def all_v(rows):
        total = None
        for xi in range(4):
            for zi in range(4):
                term = product(2, rows, xi, zi)
                total = term if total is None else total + term
        qkv[2, rows, :] = total.astype(bf16)

    def last_q(rows):
        total = acc[0, rows, :]
        for xi in range(4):
            total = total + product(0, rows, xi, lax.rem(z + 2, 4))
        qkv[0, rows, :] = total.astype(bf16)

    def last_k(rows):
        total = acc[1, rows, :]
        for zi in range(4):
            total = total + product(1, rows, lax.rem(x + 2, 4), zi)
        qkv[1, rows, :] = total.astype(bf16)

    project(first_q)
    y1.wait_recv()
    y2.wait_recv()
    e_up = [send(46 + i, e(ALL, i, z), e(ALL, i, z), dev("z", 1)) for i in range(2)]
    e_down = [send(48 + i, e(ALL, i, z), e(ALL, i, z), dev("z", 3)) for i in (1, 0)]
    project(first_k)
    ya.wait_recv()
    yb.wait_recv()
    project(all_v)
    d3.end()
    project(last_q)
    e3.end()
    project(last_k)

    lane = lax.broadcasted_iota(jnp.int32, (SEQ, 128), 1)

    def attend(p):
        rows = pl.ds(p * SEQ, SEQ)

        def body(j, c):
            lanes = pl.ds(pl.multiple_of(j * 128, 128), 128)
            q2 = qkv[0, rows, lanes]
            k2 = qkv[1, rows, lanes]
            v2 = qkv[2, rows, lanes]
            outs = []
            for t in range(2):
                qt = jnp.where((lane // HEAD_DIM) == t, q2, jnp.zeros_like(q2))
                s = lax.dot_general(
                    qt, k2, (((1,), (1,)), ((), ())), preferred_element_type=f32
                )
                s = s + bias[2 * j + t] + mask_add[pl.ds(p, 1), :]
                wts = jnp.exp(s - jnp.max(s, axis=1, keepdims=True))
                scale = 1.0 / jnp.sum(wts, axis=1, keepdims=True)
                outs.append(
                    jnp.dot((wts * scale).astype(bf16), v2, preferred_element_type=f32)
                )
            att[mp, rows, lanes] = jnp.where(lane < HEAD_DIM, outs[0], outs[1]).astype(bf16)
            return c

        lax.fori_loop(0, 4, body, 0)

    hops, ends, cores, lasts = [], [], [], []
    far = (1 - yh) * 2 + core

    def hand_out(p):
        rows = pl.ds(p * SEQ, SEQ)
        cores.append(send(68 + p, att.at[mp, rows], att.at[mp, rows], other_core))
        hops.append(
            send(72 + p, att.at[mp, rows], transit.at[p], y_step(1 if p % 2 == 0 else 3))
        )

    def hand_on(p):
        rows = pl.ds(p * SEQ, SEQ)
        hops[p].wait_recv()
        frm = lax.rem(y + (3 if p % 2 == 0 else 1), 4)
        slot = (frm // 2) * 2 + core
        ends.append(
            send(76 + p, transit.at[p], att.at[slot, rows], y_step(1 if p % 2 == 0 else 3))
        )

    def hand_over(p):
        rows = pl.ds(p * SEQ, SEQ)
        ends[p].wait_recv()
        lasts.append(send(80 + p, att.at[far, rows], att.at[far, rows], other_core))

    attend(0)
    hand_out(0)
    attend(1)
    hand_out(1)
    hand_on(0)
    e_up[0].wait_recv()
    piece = e(ALL, 0, lax.rem(z + 3, 4))
    ef_up = send(50, piece, piece, dev("z", 1))
    e_down[0].wait_recv()
    piece = e(ALL, 1, lax.rem(z + 1, 4))
    ef_down = send(51, piece, piece, dev("z", 3))
    attend(2)
    hand_out(2)
    hand_on(1)
    hand_over(0)
    attend(3)
    hand_out(3)
    hand_on(2)
    hand_over(1)
    hand_on(3)
    load_here.wait()
    e_up[1].wait_recv()
    e_down[1].wait_recv()
    ef_up.wait_recv()
    ef_down.wait_recv()
    hand_over(2)
    hand_over(3)
    u_copy = pltpu.make_async_copy(e_ref.at[:, pl.ds(512, 128), :], u_out, own_sem.at[5])
    u_copy.start()
    for p in range(4):
        cores[p].wait_recv()
        lasts[p].wait_recv()
        rows = pl.ds(p * SEQ, SEQ)

        def out_cols(i, c):
            cols = pl.ds(pl.multiple_of(i * 512, 512), 512)
            total = None
            for m in range(NMP):
                term = jnp.dot(
                    att[m, rows, :], e_ref[m, pl.ds(0, 512), cols], preferred_element_type=f32
                ).astype(bf16).astype(f32)
                total = term if total is None else total + term
            enc_out[rows, cols] = (tok_here[rows, cols].astype(f32) + total).astype(bf16)
            return c

        lax.fori_loop(0, 2, out_cols, 0)

    u_copy.wait()
    for copy in sent:
        copy.wait_send()
    for k in range(1, 4):
        block_copy(k).wait_send()

    @pl.when(jnp.logical_not(mine))
    def _():
        block_copy(0).wait_send()


def encoder(args):
    tok_rows = args[0].shape[0]
    bf16 = jnp.bfloat16
    return pl.pallas_call(
        encoder_kernel,
        out_shape=(
            jax.ShapeDtypeStruct((tok_rows, 1024), bf16),
            jax.ShapeDtypeStruct((NMP, 128, 1024), bf16),
            jax.ShapeDtypeStruct((CLAIMS * POS, 128), jnp.float32),
        ),
        in_specs=[ANY, VMEM, ANY, VMEM, VMEM, VMEM, ANY] + [VMEM] * 5,
        out_specs=(VMEM, ANY, VMEM),
        scratch_shapes=[
            pltpu.VMEM((3, 4, 4, 256, 512), bf16),
            pltpu.VMEM((tok_rows, D), bf16),
            pltpu.VMEM((2, tok_rows, 512), jnp.float32),
            pltpu.VMEM((3, tok_rows, 512), bf16),
            pltpu.VMEM((NMP, 640, 1024), bf16),
            pltpu.VMEM((NMP, tok_rows, 512), bf16),
            pltpu.VMEM((4, SEQ, 512), bf16),
            pltpu.VMEM((8, SEQ, SEQ), jnp.float32),
            pltpu.VMEM((tok_rows, 1024), bf16),
            pltpu.VMEM((640, 128), bf16),
            pltpu.VMEM((NMP, 8, 128), jnp.float32),
            pltpu.VMEM((4, 8, 640), jnp.float32),
            pltpu.VMEM((8, 8, 640), jnp.float32),
            pltpu.SemaphoreType.DMA((84,)),
            pltpu.SemaphoreType.DMA((84,)),
            pltpu.SemaphoreType.DMA((6,)),
        ],
        compiler_params=pltpu.CompilerParams(
            collective_id=1, has_side_effects=True, vmem_limit_bytes=58 << 20
        ),
    )(*args)


def high_low(values):
    high = values.astype(jnp.bfloat16)
    low = (values - high.astype(jnp.float32)).astype(jnp.bfloat16)
    return high, low


def shards(
    tokens,
    lengths,
    assignment,
    retrieval,
    enc_gain,
    enc_qkv,
    position_bias,
    enc_output,
    final_gain,
    embedding,
    dec_tokens,
    dec_gain,
    cross_query,
    cross_keyval,
    cross_output,
):
    f32 = jnp.float32
    psg = lax.axis_index("psg")
    mp = lax.axis_index("mp")
    tok_rows = tokens.shape[0]
    passages_here = lengths.shape[0]
    heads_here = enc_qkv.shape[2] // HEAD_DIM
    query_rows = CLAIMS * POS
    positions = jnp.arange(SEQ)

    vocab_here = embedding.shape[0]
    found = lookup(dec_tokens.reshape(-1), (mp * vocab_here).reshape(1), embedding)
    onehot = bucket_onehot(SEQ, BUCKETS, MAXDIST)
    onehot = np.concatenate([onehot[:, 255:], np.zeros((BUCKETS, 1)), onehot[:, :255]], axis=1)
    mask_add = jnp.where(positions[None, :] < lengths[:, None], 0.0, MASKED)
    encoded, u_all, embedded = encoder(
        (
            tokens,
            enc_gain.reshape(1, D),
            enc_qkv,
            position_bias,
            jnp.asarray(onehot, jnp.bfloat16),
            mask_add,
            enc_output,
            final_gain.reshape(1, D),
            found,
            dec_gain.reshape(1, 128),
            cross_query,
            cross_keyval,
        )
    )
    width = encoded.shape[1]
    gain_here = lax.dynamic_slice_in_dim(final_gain, psg * 128, 128, 0)
    encoded_f = encoded.astype(f32)
    squares = jnp.sum(encoded_f * encoded_f, axis=1).reshape(passages_here, SEQ)

    rows_u = u_all.reshape(NMP, 2, CLAIMS, POS * heads_here, width)
    claim_u = jnp.stack(
        [lax.dynamic_index_in_dim(rows_u, assignment[i], 2, False) for i in range(passages_here)],
        axis=2,
    )
    per_psg = encoded.reshape(passages_here, SEQ, width)
    partial = jnp.einsum("mapnd,pkd->mapnk", claim_u, per_psg, preferred_element_type=f32)
    partial = (partial[:, 0] + partial[:, 1]).reshape(NMP, passages_here * POS * heads_here, SEQ)
    extra = jnp.broadcast_to(
        jnp.concatenate([squares, jnp.zeros_like(squares)], axis=0)[None],
        (NMP, 2 * passages_here, SEQ),
    )
    raw = jnp.sum(mp_exchange(jnp.concatenate([partial, extra], axis=1), 5, True), axis=0)
    n_rows = passages_here * POS * heads_here
    inverse = lax.rsqrt(raw[n_rows : n_rows + passages_here] / D + EPSILON)
    cross = raw[:n_rows].reshape(passages_here, POS * heads_here, SEQ)
    cross = cross * inverse[:, None, :] + retrieval[:, None, None]
    usable = (positions[None, :] < lengths[:, None])[:, None, :]
    masked = jnp.where(usable, cross, MASKED)
    onehot = assignment[None, :] == jnp.arange(CLAIMS)[:, None]
    psg_max = jnp.max(masked, axis=-1)
    local_max = jnp.max(jnp.where(onehot[:, :, None], psg_max[None], MASKED), axis=1)
    chosen_max = jnp.max(jnp.where(onehot[:, :, None], local_max[:, None], MASKED), axis=0)
    weights_c = jnp.where(
        usable, jnp.exp(masked - chosen_max[:, :, None]), 0.0
    )
    local_total = jnp.sum(
        jnp.where(onehot[:, :, None], jnp.sum(weights_c, axis=-1)[None], 0.0), axis=1
    )
    stats = jnp.stack([local_max.reshape(-1), local_total.reshape(-1)])
    stats = jnp.pad(stats, ((0, 6), (0, SEQ - stats.shape[1])))
    sent = jnp.concatenate(
        [(weights_c * inverse[:, None, :]).reshape(n_rows, SEQ), stats], axis=0
    )
    all_w = mp_exchange(sent, 6, False)
    spread_w = jnp.where(
        onehot[None, :, :, None, None],
        all_w[:, :n_rows].reshape(NMP, 1, passages_here, POS * heads_here, SEQ),
        0.0,
    )
    w_high, w_low = high_low(spread_w)
    weighted = jnp.einsum(
        "mcpnk,pkd->mcnd", w_high, per_psg, preferred_element_type=f32
    ) + jnp.einsum("mcpnk,pkd->mcnd", w_low, per_psg, preferred_element_type=f32)
    weighted = weighted.reshape(NMP, query_rows * heads_here, 8, 128).transpose(2, 0, 1, 3)
    both = jnp.concatenate([all_w[:, n_rows, :64], all_w[:, n_rows + 1, :64]], axis=1)
    both = jnp.broadcast_to(
        jnp.pad(both[:, None, :], ((0, 0), (0, 7), (0, 0)))[None], (8, NMP, 8, 128)
    )
    got = spread(jnp.concatenate([weighted, both], axis=2), 7)
    each_max = got[:, 64, :64]
    each_total = got[:, 64, 64:]
    joint_max = jnp.max(each_max, axis=0)
    scale = jnp.exp(each_max - joint_max[None])
    total = jnp.sum(scale * each_total, axis=0)
    mean_rows = jnp.sum(got[:, :64] * scale[:, :, None], axis=0) / total[:, None] * gain_here
    attn_part = jnp.einsum(
        "rhc,chd->rhd",
        mean_rows.reshape(query_rows, heads_here, 128),
        cross_keyval[1].astype(f32).reshape(128, heads_here, HEAD_DIM),
        precision=HIGHEST,
    ).reshape(query_rows, 512)
    cross_attn = jnp.sum(psg_gather(attn_part, 8), axis=0)
    out_part = jnp.dot(cross_attn, cross_output.astype(f32), precision=HIGHEST)
    out_sum = jnp.sum(mp_exchange(out_part, 9, False), axis=0) + embedded
    decoded = lax.dynamic_slice_in_dim(out_sum, mp * 32, 32, 1)
    return (encoded, decoded.astype(jnp.bfloat16).reshape(CLAIMS, POS, 32))


def solution(mesh):
    in_specs = (
        P("psg", None),
        P("psg"),
        P("psg"),
        P("psg"),
        P(),
        P(None, "psg", "mp"),
        P("mp", None),
        P("mp", "psg"),
        P(),
        P("mp", "psg"),
        P(),
        P("psg"),
        P("psg", "mp"),
        P(None, "psg", "mp"),
        P("mp", "psg"),
    )
    out_specs = (P("psg", "mp"), P(None, None, ("psg", "mp")))
    return jax.shard_map(shards, mesh=mesh, in_specs=in_specs, out_specs=out_specs, check_vma=False)
```

```python
import functools
import math

import jax
import jax.numpy as jnp
import numpy as np
from jax import lax
from jax.experimental import pallas as pl
from jax.experimental.pallas import tpu as pltpu
from jax.sharding import PartitionSpec as P

D = 4096
HEAD_DIM = 64
BUCKETS = 32
MAXDIST = 128
SEQ = 256
CLAIMS = 4
POS = 2
NPSG = 32
NMP = 4
EPSILON = 1e-06
MASKED = -1e30
MESH = pl.DeviceIdType.MESH
ANY = pl.BlockSpec(memory_space=pl.ANY)
VMEM = pl.BlockSpec(memory_space=pltpu.VMEM)


def bucket_onehot(length, buckets, max_distance):
    halfway = buckets // 2
    exact_max = halfway // 2
    relative_list = list(range(-(length - 1), length))
    beyond_list = [
        min(
            halfway - 1,
            exact_max
            + math.floor(
                math.log(max(abs(shift), 1) / exact_max)
                / math.log(max_distance / exact_max)
                * (halfway - exact_max)
            ),
        )
        for shift in relative_list
    ]
    relative = np.array(relative_list)
    beyond = np.array(beyond_list)
    distance = np.abs(relative)
    bucket_ids = np.where(relative > 0, halfway, 0) + np.where(
        distance < exact_max, distance, beyond
    )
    return (bucket_ids[None, :] == np.arange(buckets)[:, None]).astype(np.float32)


def place():
    psg = lax.axis_index("psg")
    mp = lax.axis_index("mp")
    return psg // 8, (psg // 4) % 2, psg % 4, mp // 2, mp % 2


def psg_of(x, yl, z):
    return x * 8 + yl * 4 + z


def remote(src, dst, send_sem, recv_sem, device):
    return pltpu.make_async_remote_copy(
        src_ref=src,
        dst_ref=dst,
        send_sem=send_sem,
        recv_sem=recv_sem,
        device_id=device,
        device_id_type=MESH,
    )


def signal(device):
    pl.semaphore_signal(
        pltpu.get_barrier_semaphore(), inc=1, device_id=device, device_id_type=MESH
    )


def lookup_kernel(ids, lengths, assignment, retrieval, table, out, mask_add, claims, extra, rows, sems):
    copies = []
    held = []
    base = lax.axis_index("mp") * table.shape[0]
    for i in range(CLAIMS * POS):
        local = ids[i % POS, i // POS] - base
        inside = jnp.logical_and(local >= 0, local < table.shape[0])
        local = jnp.clip(local, 0, table.shape[0] - 1)
        start = pl.multiple_of((local // 16) * 16, 16)
        held.append(jnp.where(inside, local - start, -1))
        copies.append(
            pltpu.make_async_copy(table.at[pl.ds(start, 16), :], rows.at[i], sems.at[i])
        )
        copies[-1].start()
    slot = lax.broadcasted_iota(jnp.int32, (16, SEQ), 1)
    for p in range(4):
        add = jnp.where(slot < lengths[p], 0.0, MASKED)
        mask_add[p] = add[:8]
        extra[p] = add + retrieval[p]
        claims[p] = jnp.zeros((16, SEQ), jnp.int32) + assignment[p]
    at = lax.broadcasted_iota(jnp.int32, (16, 128), 0)
    for i in range(CLAIMS * POS):
        copies[i].wait()
        picked = jnp.where(at == held[i], rows[i].astype(jnp.float32), 0.0)
        out[pl.ds(i, 1), :] = jnp.sum(picked, axis=0, keepdims=True)


def lookup(ids, lengths, assignment, retrieval, table):
    smem = pl.BlockSpec(memory_space=pltpu.SMEM)
    f32 = jnp.float32
    return pl.pallas_call(
        lookup_kernel,
        out_shape=(
            jax.ShapeDtypeStruct((CLAIMS * POS, 128), f32),
            jax.ShapeDtypeStruct((4, 8, SEQ), f32),
            jax.ShapeDtypeStruct((4, 16, SEQ), jnp.int32),
            jax.ShapeDtypeStruct((4, 16, SEQ), f32),
        ),
        in_specs=[smem] * 4 + [ANY],
        out_specs=(VMEM,) * 4,
        scratch_shapes=[
            pltpu.VMEM((CLAIMS * POS, 16, 128), jnp.bfloat16),
            pltpu.SemaphoreType.DMA((CLAIMS * POS,)),
        ],
    )(ids, lengths, assignment, retrieval, table)


def split3(values):
    high = values.astype(jnp.bfloat16)
    rest = values - high.astype(jnp.float32)
    middle = rest.astype(jnp.bfloat16)
    low = (rest - middle.astype(jnp.float32)).astype(jnp.bfloat16)
    return jnp.concatenate([high, middle, low], axis=0)


def dot3(values, weights, contract=0):
    n = values.shape[0]
    parts = lax.dot_general(
        split3(values),
        weights,
        (((1,), (contract,)), ((), ())),
        preferred_element_type=jnp.float32,
    )
    return parts[:n] + parts[n : 2 * n] + parts[2 * n :]


ALL = slice(None)


def encoder_kernel(
    tokens,
    enc_gain,
    w_ref,
    bias_in,
    onehot,
    mask_add,
    enc_output,
    final_gain,
    found,
    dec_gain,
    cross_query,
    cross_keyval,
    cross_output,
    claims,
    extra,
    enc_out,
    dec_out,
    g_ref,
    normed,
    acc,
    qkv,
    e_ref,
    att,
    transit,
    bias,
    tok_here,
    block,
    mp_buf,
    x_buf,
    yz_buf,
    sc_src,
    sc_in,
    all_w,
    all_st,
    lhs,
    y_src,
    y_zin,
    st_z,
    y_one,
    y_ysrc,
    y_yin,
    st_one,
    st_yin,
    y_two,
    st_two,
    y_in,
    st_in,
    x_buf2,
    yz_buf2,
    mp_buf2,
    send_sem,
    recv_sem,
    own_sem,
):
    f32 = jnp.float32
    bf16 = jnp.bfloat16
    x, yl, z, yh, core = place()
    psg = lax.axis_index("psg")
    mp = lax.axis_index("mp")
    y = yh * 2 + yl
    y_dev = (psg_of(x, 1 - yl, z), mp)

    def dev(axis, step):
        if axis == "x":
            return (psg_of(lax.rem(x + step, 4), yl, z), mp)
        return (psg_of(x, yl, lax.rem(z + step, 4)), mp)

    def yz_dev(k):
        t = lax.rem(yl * 4 + z + k, 8)
        return (x * 8 + t, mp)

    def mp_dev(k):
        return (psg, lax.rem(mp + k, NMP))

    def y_step(step):
        t = lax.rem(y + step, 4)
        return (psg_of(x, lax.rem(t, 2), z), (t // 2) * 2 + core)

    other_core = (psg, yh * 2 + 1 - core)
    same_half = (x // 2) == yh
    yl_to = jnp.where(same_half, yl, 1 - yl)

    def block_to(k):
        return (psg_of(lax.rem(x + k, 4), yl_to, z), x)

    mine = x == mp

    load_tokens = pltpu.make_async_copy(tokens, normed, own_sem.at[0])
    load_tokens.start()
    own = pltpu.make_async_copy(
        w_ref, g_ref.at[:, x, z, pl.ds(pl.multiple_of(yl * 128, 128), 128), :], own_sem.at[1]
    )
    own.start()
    load_here = pltpu.make_async_copy(
        tokens.at[:, pl.ds(pl.multiple_of(mp * 1024, 128), 1024)], tok_here, own_sem.at[2]
    )
    load_here.start()
    load_block = pltpu.make_async_copy(enc_output, block.at[pl.ds(0, 512)], own_sem.at[3])
    load_block.start()

    for k in range(1, 4):
        signal(dev("x", k))
        signal(mp_dev(k))
    for k in range(1, 8):
        signal(yz_dev(k))
    signal(y_step(1))
    signal(y_step(3))
    for m in range(NMP):
        frm = psg_of(mp, jnp.where((m // 2) == yh, yl, 1 - yl), z)

        @pl.when(jnp.logical_not(jnp.logical_and(mine, m == mp)))
        def _():
            signal((frm, m))

    for k in range(4):
        frm = psg_of(lax.rem(x + k, 4), yl, z)
        if k == 0:
            pl.when(jnp.logical_not(mine))(functools.partial(signal, (frm, x)))
        else:
            signal((frm, x))

    def g(k, xs, zs, yls, cols=None):
        rows = ALL if yls is None else pl.ds(pl.multiple_of(yls * 128, 128), 128)
        c = ALL if cols is None else pl.ds(cols[0], cols[1])
        return g_ref.at[k, xs, zs, rows, c]

    def wide(c):
        return None if c is None else (c * 256, 256)

    def low_cols(c):
        return (0, 256) if c is None else (c * 128, 128)

    def high_cols(c):
        return (256, 256) if c is None else (256 + c * 128, 128)

    sent = []

    def send(t, src, dst, device):
        copy = remote(src, dst, send_sem.at[t], recv_sem.at[t], device)
        copy.start()
        sent.append(copy)
        return copy

    class Ring:
        def __init__(self, t, axis, piece, first=None):
            self.t, self.axis, self.piece = t, axis, piece
            self.at = x if axis == "x" else z
            src = piece(self.at) if first is None else first
            self.up = send(t, src, piece(self.at), dev(axis, 1))
            self.down = send(t + 1, src, piece(self.at), dev(axis, 3))

        def forward(self):
            below = lax.rem(self.at + 3, 4)
            above = lax.rem(self.at + 1, 4)
            self.up.wait_recv()
            up = self.piece(below, 0)
            self.f_up = send(self.t + 2, up, up, dev(self.axis, 1))
            self.down.wait_recv()
            down = self.piece(above, 1)
            self.f_down = send(self.t + 3, down, down, dev(self.axis, 3))

        def end(self):
            self.f_up.wait_recv()
            self.f_down.wait_recv()

    pl.semaphore_wait(pltpu.get_barrier_semaphore(), jnp.where(mine, 21, 23))

    yd = send(0, w_ref.at[0], g(0, x, z, yl), y_dev)
    ye = send(1, w_ref.at[1], g(1, x, z, yl), y_dev)
    a1 = Ring(
        4, "x", lambda v, c=None: g(2, v, z, yl, low_cols(c)), w_ref.at[2, :, pl.ds(0, 256)]
    )
    b1 = Ring(
        8, "z", lambda v, c=None: g(2, x, v, yl, high_cols(c)), w_ref.at[2, :, pl.ds(256, 256)]
    )
    mp_buf[mp] = found[...]
    mps = [send(52 + k, found, mp_buf.at[mp], mp_dev(k)) for k in range(1, 4)]
    own.wait()
    yd.wait_recv()
    d2 = Ring(20, "x", lambda v, c=None: g(0, v, z, None, wide(c)))
    ye.wait_recv()
    e2 = Ring(24, "z", lambda v, c=None: g(1, x, v, None, wide(c)))
    a1.forward()
    b1.forward()

    for copy in mps:
        copy.wait_recv()
    emb = mp_buf[0] + mp_buf[1] + mp_buf[2] + mp_buf[3]
    terms = dot3(emb * dec_gain[...], cross_query[...])
    squares = jnp.sum(emb * emb, axis=1, keepdims=True)
    x_buf[x, :, pl.ds(0, 512)] = terms
    x_buf[x, :, pl.ds(512, 128)] = jnp.broadcast_to(squares, (8, 128))
    xs = [send(56 + k, x_buf.at[x], x_buf.at[x], dev("x", k)) for k in range(1, 4)]

    a1.end()
    a2 = Ring(12, "z", lambda v, c=None: g(2, ALL, v, yl, low_cols(c)))
    b1.end()
    b2 = Ring(16, "x", lambda v, c=None: g(2, v, ALL, yl, high_cols(c)))

    load_tokens.wait()

    def norm_rows(first, count):
        def body(i, c):
            rows = pl.ds(pl.multiple_of(i * 16, 16), 16)
            values = normed[rows, :].astype(f32)
            mean = jnp.sum(values * values, axis=1, keepdims=True) / D
            inverse = lax.rsqrt(mean + EPSILON)
            scaled = (values * inverse * enc_gain[...]).astype(bf16)
            for p in range(NPSG):
                to = ((p // 8) * 4 + p % 4) * 2 + (p // 4) % 2
                normed[rows, pl.ds(to * 128, 128)] = scaled[:, p * 128 : (p + 1) * 128]
            return c

        lax.fori_loop(first, first + count, body, 0)

    norm_rows(0, 24)

    for copy in xs:
        copy.wait_recv()
    yz = yl * 4 + z
    yz_buf[yz] = x_buf[0] + x_buf[1] + x_buf[2] + x_buf[3]
    yzs = [send(60 + k, yz_buf.at[yz], yz_buf.at[yz], yz_dev(k)) for k in range(1, 8)]

    d2.forward()
    e2.forward()
    norm_rows(24, 20)
    d2.end()
    d3 = Ring(28, "z", lambda v, c=None: g(0, ALL, v, None, wide(c)))
    e2.end()
    e3 = Ring(32, "x", lambda v, c=None: g(1, v, ALL, None, wide(c)))
    a2.forward()
    b2.forward()
    norm_rows(44, 20)

    for copy in yzs:
        copy.wait_recv()
    joined = yz_buf[0]
    for k in range(1, 8):
        joined = joined + yz_buf[k]
    cquery = joined[:, :512] * lax.rsqrt(joined[:, 512:513] / D + EPSILON)
    spread_q = jnp.broadcast_to(cquery[:, None, :], (8, 8, 512)).reshape(64, 512)
    head_of_row = lax.rem(lax.broadcasted_iota(jnp.int32, (64, 512), 0), 8)
    head_of_lane = lax.broadcasted_iota(jnp.int32, (64, 512), 1) // HEAD_DIM
    spread_q = jnp.where(head_of_row == head_of_lane, spread_q, 0.0)
    folded = dot3(spread_q, cross_keyval[0], 1)
    folded = folded * final_gain[:, pl.ds(pl.multiple_of(psg * 128, 128), 128)]
    high = folded.astype(bf16)
    load_block.wait()
    block[pl.ds(512, 64), :] = high
    block[pl.ds(576, 64), :] = (folded - high.astype(f32)).astype(bf16)

    def e(ms, yls, zs):
        col = pl.multiple_of((yls * 4 + zs) * 128, 128)
        return e_ref.at[ms, :, pl.ds(col, 128)]

    def block_copy(k):
        return remote(block, e(mp, yl, z), send_sem.at[36 + k], recv_sem.at[40 + mp], block_to(k))

    keep = pltpu.make_async_copy(block, e(mp, yl, z), own_sem.at[4])

    @pl.when(mine)
    def _():
        keep.start()

    @pl.when(jnp.logical_not(mine))
    def _():
        block_copy(0).start()

    for k in range(1, 4):
        block_copy(k).start()

    a2.end()
    low = g(2, ALL, ALL, yl, low_cols(None))
    ya = send(2, low, low, y_dev)
    b2.end()
    hi = g(2, ALL, ALL, yl, high_cols(None))
    yb = send(3, hi, hi, y_dev)

    table = dot3(bias_in[...], onehot[...])
    for h in range(8):
        row = jnp.broadcast_to(table[h : h + 1], (SEQ, 512))
        bias[h] = pltpu.roll(row, 0, 1, stride=1, stride_axis=0)[:, :SEQ]

    for m in range(NMP):
        got = remote(block, e(m, yl, z), send_sem.at[36], recv_sem.at[40 + m], y_dev)
        pl.when(jnp.logical_not(jnp.logical_and(mine, m == mp)))(got.wait_recv)

    @pl.when(mine)
    def _():
        keep.wait()

    near = pl.ds(yh * 2, 2)
    far_half = pl.ds(2 - yh * 2, 2)
    y1 = send(44, e(near, yl, z), e(near, yl, z), y_dev)
    y2 = send(45, e(far_half, 1 - yl, z), e(far_half, 1 - yl, z), y_dev)

    d3.forward()
    e3.forward()

    def product(k, rows, xi, zi):
        at = pl.multiple_of((xi * 4 + zi) * 256, 256)
        return jnp.dot(
            normed[rows, pl.ds(at, 256)], g_ref[k, xi, zi], preferred_element_type=f32
        )

    def project(step):
        def body(i, c):
            step(pl.ds(pl.multiple_of(i * 256, 256), 256))
            return c

        lax.fori_loop(0, 4, body, 0)

    def first_q(rows):
        total = None
        for xi in range(4):
            for dz in (0, 1, 3):
                term = product(0, rows, xi, lax.rem(z + dz, 4))
                total = term if total is None else total + term
        acc[0, rows, :] = total

    def first_k(rows):
        total = None
        for zi in range(4):
            for dx in (0, 1, 3):
                term = product(1, rows, lax.rem(x + dx, 4), zi)
                total = term if total is None else total + term
        acc[1, rows, :] = total

    def all_v(rows):
        total = None
        for xi in range(4):
            for zi in range(4):
                term = product(2, rows, xi, zi)
                total = term if total is None else total + term
        qkv[2, rows, :] = total.astype(bf16)

    def last_q(rows):
        total = acc[0, rows, :]
        for xi in range(4):
            total = total + product(0, rows, xi, lax.rem(z + 2, 4))
        qkv[0, rows, :] = total.astype(bf16)

    def last_k(rows):
        total = acc[1, rows, :]
        for zi in range(4):
            total = total + product(1, rows, lax.rem(x + 2, 4), zi)
        qkv[1, rows, :] = total.astype(bf16)

    project(first_q)
    y1.wait_recv()
    y2.wait_recv()
    e_up = [send(46 + i, e(ALL, i, z), e(ALL, i, z), dev("z", 1)) for i in range(2)]
    e_down = [send(48 + i, e(ALL, i, z), e(ALL, i, z), dev("z", 3)) for i in (1, 0)]
    project(first_k)
    ya.wait_recv()
    yb.wait_recv()
    project(all_v)
    d3.end()
    project(last_q)
    e3.end()
    project(last_k)

    lane = lax.broadcasted_iota(jnp.int32, (SEQ, 128), 1)

    def attend(p):
        rows = pl.ds(p * SEQ, SEQ)

        def body(j, c):
            lanes = pl.ds(pl.multiple_of(j * 128, 128), 128)
            q2 = qkv[0, rows, lanes]
            k2 = qkv[1, rows, lanes]
            v2 = qkv[2, rows, lanes]
            outs = []
            for t in range(2):
                qt = jnp.where((lane // HEAD_DIM) == t, q2, jnp.zeros_like(q2))
                s = lax.dot_general(
                    qt, k2, (((1,), (1,)), ((), ())), preferred_element_type=f32
                )
                s = s + bias[2 * j + t] + mask_add[p, pl.ds(0, 1), :]
                wts = jnp.exp(s - jnp.max(s, axis=1, keepdims=True))
                scale = 1.0 / jnp.sum(wts, axis=1, keepdims=True)
                outs.append(
                    jnp.dot((wts * scale).astype(bf16), v2, preferred_element_type=f32)
                )
            att[mp, rows, lanes] = jnp.where(lane < HEAD_DIM, outs[0], outs[1]).astype(bf16)
            return c

        lax.fori_loop(0, 4, body, 0)

    hops, ends, cores, lasts = [], [], [], []
    far = (1 - yh) * 2 + core

    def hand_out(p):
        rows = pl.ds(p * SEQ, SEQ)
        cores.append(send(68 + p, att.at[mp, rows], att.at[mp, rows], other_core))
        hops.append(
            send(72 + p, att.at[mp, rows], transit.at[p], y_step(1 if p % 2 == 0 else 3))
        )

    def hand_on(p):
        rows = pl.ds(p * SEQ, SEQ)
        hops[p].wait_recv()
        frm = lax.rem(y + (3 if p % 2 == 0 else 1), 4)
        slot = (frm // 2) * 2 + core
        ends.append(
            send(76 + p, transit.at[p], att.at[slot, rows], y_step(1 if p % 2 == 0 else 3))
        )

    def hand_over(p):
        rows = pl.ds(p * SEQ, SEQ)
        ends[p].wait_recv()
        lasts.append(send(80 + p, att.at[far, rows], att.at[far, rows], other_core))

    attend(0)
    hand_out(0)
    attend(1)
    hand_out(1)
    hand_on(0)
    e_up[0].wait_recv()
    piece = e(ALL, 0, lax.rem(z + 3, 4))
    ef_up = send(50, piece, piece, dev("z", 1))
    e_down[0].wait_recv()
    piece = e(ALL, 1, lax.rem(z + 1, 4))
    ef_down = send(51, piece, piece, dev("z", 3))
    attend(2)
    hand_out(2)
    hand_on(1)
    hand_over(0)
    attend(3)
    hand_out(3)
    hand_on(2)
    hand_over(1)
    hand_on(3)
    load_here.wait()
    e_up[1].wait_recv()
    e_down[1].wait_recv()
    ef_up.wait_recv()
    ef_down.wait_recv()
    hand_over(2)
    hand_over(3)
    def out_project(p):
        rows = pl.ds(p * SEQ, SEQ)

        def out_cols(i, c):
            cols = pl.ds(pl.multiple_of(i * 512, 512), 512)
            total = None
            for m in range(NMP):
                term = jnp.dot(
                    att[m, rows, :], e_ref[m, pl.ds(0, 512), cols], preferred_element_type=f32
                ).astype(bf16).astype(f32)
                total = term if total is None else total + term
            enc_out[rows, cols] = (tok_here[rows, cols].astype(f32) + total).astype(bf16)
            return c

        lax.fori_loop(0, 2, out_cols, 0)

    def cross_scores(p):
        enc = enc_out[pl.ds(p * SEQ, SEQ), :]
        wide_enc = enc.astype(f32)
        squares = jnp.sum(wide_enc * wide_enc, axis=1, keepdims=True)
        squares = jnp.broadcast_to(squares, (SEQ, 128)).T[:8]
        for m in range(NMP):
            both = lax.dot_general(
                e_ref[m, pl.ds(512, 128), :], enc, (((1,), (1,)), ((), ())),
                preferred_element_type=f32,
            )
            both = both[:64] + both[64:]
            picked = jnp.zeros((16, SEQ), f32)
            for c in range(CLAIMS):
                picked = jnp.where(claims[p] == c, both[c * 16 : (c + 1) * 16], picked)
            sc_src[m, p, pl.ds(0, 16), :] = picked
            sc_src[m, p, pl.ds(16, 8), :] = squares
        out = []
        for k in range(1, 4):
            to = lax.rem(mp + k, NMP)
            out.append(
                send(84 + p * 3 + k - 1, sc_src.at[to, p], sc_in.at[mp, p], mp_dev(k))
            )
        sc_in[mp, p] = sc_src[mp, p]
        return out

    scs = []
    for p in range(4):
        cores[p].wait_recv()
        lasts[p].wait_recv()
        out_project(p)
        scs.append(cross_scores(p))

    crosses, inverses, maxima = [], [], []
    for p in range(4):
        for copy in scs[p]:
            copy.wait_recv()
        raw = sc_in[0, p] + sc_in[1, p] + sc_in[2, p] + sc_in[3, p]
        inverse = lax.rsqrt(raw[16:17] / D + EPSILON)
        cross = raw[:16] * inverse + extra[p]
        crosses.append(cross)
        inverses.append(inverse)
        maxima.append(jnp.broadcast_to(jnp.max(cross, axis=1, keepdims=True), (16, SEQ)))
    claim_max = []
    for c in range(CLAIMS):
        top = jnp.full((16, SEQ), MASKED, f32)
        for p in range(4):
            top = jnp.maximum(top, jnp.where(claims[p] == c, maxima[p], MASKED))
        claim_max.append(top)
    sums = []
    for p in range(4):
        chosen = claim_max[0]
        for c in range(1, CLAIMS):
            chosen = jnp.where(claims[p] == c, claim_max[c], chosen)
        wts = jnp.exp(crosses[p] - chosen)
        sums.append(jnp.broadcast_to(jnp.sum(wts, axis=1, keepdims=True), (16, SEQ)))
        all_w[mp, p] = (wts * inverses[p]).astype(bf16)
    totals = []
    for c in range(CLAIMS):
        total = jnp.zeros((16, SEQ), f32)
        for p in range(4):
            total = total + jnp.where(claims[p] == c, sums[p], 0.0)
        totals.append(total)
    first_row = lax.broadcasted_iota(jnp.int32, (8, 128), 0) == 0

    def lanes_of(parts, fill):
        column = jnp.concatenate([part[:, :128] for part in parts], axis=0)
        column = jnp.concatenate([column, jnp.full((64, 128), fill, f32)], axis=0)
        return column.T[:8]

    all_st[mp] = jnp.where(first_row, lanes_of(claim_max, MASKED), lanes_of(totals, 0.0))
    ws = [send(96 + k, all_w.at[mp], all_w.at[mp], mp_dev(k)) for k in range(3 + 1) if k]
    sts = [send(99 + k, all_st.at[mp], all_st.at[mp], mp_dev(k)) for k in range(3 + 1) if k]
    for copy in ws + sts:
        copy.wait_recv()

    for p in range(4):
        for m in range(NMP):
            w_mp = all_w[m, p].astype(f32)
            for c in range(CLAIMS):
                lhs[p, pl.ds(m * 64 + c * 16, 16), :] = jnp.where(
                    claims[p] == c, w_mp, 0.0
                ).astype(bf16)
    for i in range(2):
        total = None
        for p in range(4):
            term = jnp.dot(
                lhs[p], enc_out[pl.ds(p * SEQ, SEQ), pl.ds(i * 512, 512)],
                preferred_element_type=f32,
            )
            total = term if total is None else total + term
        for zt in range(4):
            y_src[zt, i] = total[:, zt * 128 : (zt + 1) * 128].astype(bf16)
    y_copies, st_copies = [], []
    for k in range(1, 4):
        tz = lax.rem(z + k, 4)
        y_copies.append(send(103 + k, y_src.at[tz], y_zin.at[z], dev("z", k)))
        st_copies.append(send(106 + k, all_st, st_z.at[z], dev("z", k)))
    y_zin[z] = y_src[z]
    st_z[z] = all_st[...]

    def merge(stats, rows):
        top = stats[0][0:1]
        for st in stats[1:]:
            top = jnp.maximum(top, st[0:1])
        total = jnp.zeros((1, 128), f32)
        results = [jnp.zeros((64, 128), f32) for _ in rows[0]]
        for st, these in zip(stats, rows):
            scale = jnp.exp(st[0:1] - top)
            total = total + scale * st[1:2]
            column = jnp.broadcast_to(scale, (128, 128)).T[:64]
            results = [r + column * t.astype(f32) for r, t in zip(results, these)]
        both = jnp.where(
            first_row, jnp.broadcast_to(top, (8, 128)), jnp.broadcast_to(total, (8, 128))
        )
        return both, results

    for copy in y_copies + st_copies:
        copy.wait_recv()
    for m in range(NMP):
        part = pl.ds(m * 64, 64)
        both, results = merge(
            [st_z[j, m] for j in range(4)],
            [[y_zin[j, i, part, :] for i in range(2)] for j in range(4)],
        )
        st_one[m] = both
        for i in range(2):
            y_one[i, m] = results[i]
    y_ysrc[...] = y_one[1 - yl].astype(bf16)
    yc = send(110, y_ysrc, y_yin, y_dev)
    ystc = send(111, st_one, st_yin, y_dev)
    yc.wait_recv()
    ystc.wait_recv()
    for m in range(NMP):
        both, results = merge([st_one[m], st_yin[m]], [[y_one[yl, m]], [y_yin[m]]])
        st_two[m] = both
        y_two[m] = results[0]

    def to_owner(k):
        m = lax.rem(mp + k, NMP)
        target = (psg_of(mp, yl, z), m)
        return (
            remote(y_two.at[m], y_in.at[x], send_sem.at[112 + k], recv_sem.at[112 + x], target),
            remote(st_two.at[m], st_in.at[x], send_sem.at[116 + k], recv_sem.at[116 + x], target),
        )

    def from_source(k):
        frm = lax.rem(x + k, 4)
        target = (psg_of(frm, yl, z), x)
        return (
            remote(y_two.at[0], y_in.at[frm], send_sem.at[112], recv_sem.at[112 + frm], target),
            remote(st_two.at[0], st_in.at[frm], send_sem.at[116], recv_sem.at[116 + frm], target),
        )

    @pl.when(mine)
    def _():
        y_in[x] = y_two[mp]
        st_in[x] = st_two[mp]

    @pl.when(jnp.logical_not(mine))
    def _():
        for copy in to_owner(0):
            copy.start()

    for k in range(1, 4):
        for copy in to_owner(k):
            copy.start()

    @pl.when(jnp.logical_not(mine))
    def _():
        for copy in from_source(0):
            copy.wait_recv()

    for k in range(1, 4):
        for copy in from_source(k):
            copy.wait_recv()
    both, results = merge([st_in[j] for j in range(4)], [[y_in[j]] for j in range(4)])
    total = jnp.broadcast_to(both[1:2], (128, 128)).T[:64]
    mean_rows = results[0] / total
    mean_rows = mean_rows * final_gain[:, pl.ds(pl.multiple_of(psg * 128, 128), 128)]

    products = dot3(mean_rows, cross_keyval[1])
    products = jnp.where(head_of_row == head_of_lane, products, 0.0)
    x_buf2[x] = jnp.sum(products.reshape(8, 8, 512), axis=1)
    xs = [send(120 + k, x_buf2.at[x], x_buf2.at[x], dev("x", k)) for k in range(1, 4)]
    for copy in xs:
        copy.wait_recv()
    yz_buf2[yz] = x_buf2[0] + x_buf2[1] + x_buf2[2] + x_buf2[3]
    yzs = [send(124 + k, yz_buf2.at[yz], yz_buf2.at[yz], yz_dev(k)) for k in range(1, 8)]
    for copy in yzs:
        copy.wait_recv()
    cross_attn = yz_buf2[0]
    for k in range(1, 8):
        cross_attn = cross_attn + yz_buf2[k]
    mp_buf2[mp] = dot3(cross_attn, cross_output[...])
    lasts = [send(132 + k, mp_buf2.at[mp], mp_buf2.at[mp], mp_dev(k)) for k in range(1, 4)]
    for copy in lasts:
        copy.wait_recv()
    final = (mp_buf2[0] + mp_buf2[1] + mp_buf2[2] + mp_buf2[3]) + (
        mp_buf[0] + mp_buf[1] + mp_buf[2] + mp_buf[3]
    )
    share = final[:, :32]
    for m in range(1, NMP):
        share = jnp.where(mp == m, final[:, m * 32 : (m + 1) * 32], share)
    dec_out[...] = share.astype(bf16)

    for copy in sent:
        copy.wait_send()
    for k in range(1, 4):
        block_copy(k).wait_send()
        for copy in to_owner(k):
            copy.wait_send()

    @pl.when(jnp.logical_not(mine))
    def _():
        block_copy(0).wait_send()
        for copy in to_owner(0):
            copy.wait_send()


def encoder(args):
    tok_rows = args[0].shape[0]
    bf16 = jnp.bfloat16
    f32 = jnp.float32
    return pl.pallas_call(
        encoder_kernel,
        out_shape=(
            jax.ShapeDtypeStruct((tok_rows, 1024), bf16),
            jax.ShapeDtypeStruct((CLAIMS * POS, 32), bf16),
        ),
        in_specs=[ANY, VMEM, ANY, VMEM, VMEM, VMEM, ANY] + [VMEM] * 8,
        out_specs=(VMEM, VMEM),
        scratch_shapes=[
            pltpu.VMEM((3, 4, 4, 256, 512), bf16),
            pltpu.VMEM((tok_rows, D), bf16),
            pltpu.VMEM((2, tok_rows, 512), jnp.float32),
            pltpu.VMEM((3, tok_rows, 512), bf16),
            pltpu.VMEM((NMP, 640, 1024), bf16),
            pltpu.VMEM((NMP, tok_rows, 512), bf16),
            pltpu.VMEM((4, SEQ, 512), bf16),
            pltpu.VMEM((8, SEQ, SEQ), jnp.float32),
            pltpu.VMEM((tok_rows, 1024), bf16),
            pltpu.VMEM((640, 128), bf16),
            pltpu.VMEM((NMP, 8, 128), jnp.float32),
            pltpu.VMEM((4, 8, 640), jnp.float32),
            pltpu.VMEM((8, 8, 640), f32),
            pltpu.VMEM((NMP, 4, 24, SEQ), f32),
            pltpu.VMEM((NMP, 4, 24, SEQ), f32),
            pltpu.VMEM((NMP, 4, 16, SEQ), bf16),
            pltpu.VMEM((NMP, 8, 128), f32),
            pltpu.VMEM((4, 256, SEQ), bf16),
            pltpu.VMEM((4, 2, 256, 128), bf16),
            pltpu.VMEM((4, 2, 256, 128), bf16),
            pltpu.VMEM((4, NMP, 8, 128), f32),
            pltpu.VMEM((2, NMP, 64, 128), f32),
            pltpu.VMEM((NMP, 64, 128), bf16),
            pltpu.VMEM((NMP, 64, 128), bf16),
            pltpu.VMEM((NMP, 8, 128), f32),
            pltpu.VMEM((NMP, 8, 128), f32),
            pltpu.VMEM((NMP, 64, 128), f32),
            pltpu.VMEM((NMP, 8, 128), f32),
            pltpu.VMEM((4, 64, 128), f32),
            pltpu.VMEM((4, 8, 128), f32),
            pltpu.VMEM((4, 8, 512), f32),
            pltpu.VMEM((8, 8, 512), f32),
            pltpu.VMEM((NMP, 8, 128), f32),
            pltpu.SemaphoreType.DMA((136,)),
            pltpu.SemaphoreType.DMA((136,)),
            pltpu.SemaphoreType.DMA((5,)),
        ],
        compiler_params=pltpu.CompilerParams(
            collective_id=1, has_side_effects=True, vmem_limit_bytes=58 << 20
        ),
    )(*args)


def shards(
    tokens,
    lengths,
    assignment,
    retrieval,
    enc_gain,
    enc_qkv,
    position_bias,
    enc_output,
    final_gain,
    embedding,
    dec_tokens,
    dec_gain,
    cross_query,
    cross_keyval,
    cross_output,
):
    found, mask_add, claims, extra = lookup(
        dec_tokens.T, lengths, assignment, retrieval, embedding
    )
    onehot = bucket_onehot(SEQ, BUCKETS, MAXDIST)
    onehot = np.concatenate([onehot[:, 255:], np.zeros((BUCKETS, 1)), onehot[:, :255]], axis=1)
    encoded, decoded = encoder(
        (
            tokens,
            enc_gain.reshape(1, D),
            enc_qkv,
            position_bias,
            jnp.asarray(onehot, jnp.bfloat16),
            mask_add,
            enc_output,
            final_gain.reshape(1, D),
            found,
            dec_gain.reshape(1, 128),
            cross_query,
            cross_keyval,
            cross_output,
            claims,
            extra,
        )
    )
    return (encoded, decoded.reshape(CLAIMS, POS, 32))


def solution(mesh):
    in_specs = (
        P("psg", None),
        P("psg"),
        P("psg"),
        P("psg"),
        P(),
        P(None, "psg", "mp"),
        P("mp", None),
        P("mp", "psg"),
        P(),
        P("mp", "psg"),
        P(),
        P("psg"),
        P("psg", "mp"),
        P(None, "psg", "mp"),
        P("mp", "psg"),
    )
    out_specs = (P("psg", "mp"), P(None, None, ("psg", "mp")))
    return jax.shard_map(shards, mesh=mesh, in_specs=in_specs, out_specs=out_specs, check_vma=False)
```

```python
import functools
import math

import jax
import jax.numpy as jnp
import numpy as np
from jax import lax
from jax.experimental import pallas as pl
from jax.experimental.pallas import tpu as pltpu
from jax.sharding import PartitionSpec as P

D = 4096
HEAD_DIM = 64
BUCKETS = 32
MAXDIST = 128
SEQ = 256
CLAIMS = 4
POS = 2
NPSG = 32
NMP = 4
EPSILON = 1e-06
MASKED = -1e30
MESH = pl.DeviceIdType.MESH
ANY = pl.BlockSpec(memory_space=pl.ANY)
VMEM = pl.BlockSpec(memory_space=pltpu.VMEM)


def bucket_onehot(length, buckets, max_distance):
    halfway = buckets // 2
    exact_max = halfway // 2
    relative_list = list(range(-(length - 1), length))
    beyond_list = [
        min(
            halfway - 1,
            exact_max
            + math.floor(
                math.log(max(abs(shift), 1) / exact_max)
                / math.log(max_distance / exact_max)
                * (halfway - exact_max)
            ),
        )
        for shift in relative_list
    ]
    relative = np.array(relative_list)
    beyond = np.array(beyond_list)
    distance = np.abs(relative)
    bucket_ids = np.where(relative > 0, halfway, 0) + np.where(
        distance < exact_max, distance, beyond
    )
    return (bucket_ids[None, :] == np.arange(buckets)[:, None]).astype(np.float32)


def place():
    psg = lax.axis_index("psg")
    mp = lax.axis_index("mp")
    return psg // 8, (psg // 4) % 2, psg % 4, mp // 2, mp % 2


def psg_of(x, yl, z):
    return x * 8 + yl * 4 + z


def remote(src, dst, send_sem, recv_sem, device):
    return pltpu.make_async_remote_copy(
        src_ref=src,
        dst_ref=dst,
        send_sem=send_sem,
        recv_sem=recv_sem,
        device_id=device,
        device_id_type=MESH,
    )


def signal(device):
    pl.semaphore_signal(
        pltpu.get_barrier_semaphore(), inc=1, device_id=device, device_id_type=MESH
    )


def lookup_kernel(ids, lengths, assignment, retrieval, table, out, mask_add, claims, extra, rows, sems):
    copies = []
    held = []
    base = lax.axis_index("mp") * table.shape[0]
    for i in range(CLAIMS * POS):
        local = ids[i % POS, i // POS] - base
        inside = jnp.logical_and(local >= 0, local < table.shape[0])
        local = jnp.clip(local, 0, table.shape[0] - 1)
        start = pl.multiple_of((local // 16) * 16, 16)
        held.append(jnp.where(inside, local - start, -1))
        copies.append(
            pltpu.make_async_copy(table.at[pl.ds(start, 16), :], rows.at[i], sems.at[i])
        )
        copies[-1].start()
    slot = lax.broadcasted_iota(jnp.int32, (16, SEQ), 1)
    for p in range(4):
        add = jnp.where(slot < lengths[p], 0.0, MASKED)
        mask_add[p] = add[:8]
        extra[p] = add + retrieval[p]
        claims[p] = jnp.zeros((16, SEQ), jnp.int32) + assignment[p]
    at = lax.broadcasted_iota(jnp.int32, (16, 128), 0)
    for i in range(CLAIMS * POS):
        copies[i].wait()
        picked = jnp.where(at == held[i], rows[i].astype(jnp.float32), 0.0)
        out[pl.ds(i, 1), :] = jnp.sum(picked, axis=0, keepdims=True)


def lookup(ids, lengths, assignment, retrieval, table):
    smem = pl.BlockSpec(memory_space=pltpu.SMEM)
    f32 = jnp.float32
    return pl.pallas_call(
        lookup_kernel,
        out_shape=(
            jax.ShapeDtypeStruct((CLAIMS * POS, 128), f32),
            jax.ShapeDtypeStruct((4, 8, SEQ), f32),
            jax.ShapeDtypeStruct((4, 16, SEQ), jnp.int32),
            jax.ShapeDtypeStruct((4, 16, SEQ), f32),
        ),
        in_specs=[smem] * 4 + [ANY],
        out_specs=(VMEM,) * 4,
        scratch_shapes=[
            pltpu.VMEM((CLAIMS * POS, 16, 128), jnp.bfloat16),
            pltpu.SemaphoreType.DMA((CLAIMS * POS,)),
        ],
    )(ids, lengths, assignment, retrieval, table)


def split3(values):
    high = values.astype(jnp.bfloat16)
    rest = values - high.astype(jnp.float32)
    middle = rest.astype(jnp.bfloat16)
    low = (rest - middle.astype(jnp.float32)).astype(jnp.bfloat16)
    return jnp.concatenate([high, middle, low], axis=0)


def dot3(values, weights, contract=0):
    n = values.shape[0]
    parts = lax.dot_general(
        split3(values),
        weights,
        (((1,), (contract,)), ((), ())),
        preferred_element_type=jnp.float32,
    )
    return parts[:n] + parts[n : 2 * n] + parts[2 * n :]


ALL = slice(None)


def encoder_kernel(
    tokens,
    enc_gain,
    w_ref,
    bias_in,
    onehot,
    mask_add,
    enc_output,
    final_gain,
    found,
    dec_gain,
    cross_query,
    cross_keyval,
    cross_output,
    claims,
    extra,
    enc_out,
    dec_out,
    g_ref,
    normed,
    acc,
    qkv,
    e_ref,
    u_ref,
    att,
    transit,
    bias,
    tok_here,
    block,
    mp_buf,
    x_buf,
    yz_buf,
    sc_src,
    sc_in,
    all_w,
    all_st,
    lhs,
    y_src,
    y_zin,
    st_z,
    y_one,
    y_ysrc,
    y_yin,
    st_one,
    st_yin,
    y_two,
    st_two,
    y_in,
    st_in,
    x_buf2,
    yz_buf2,
    mp_buf2,
    send_sem,
    recv_sem,
    own_sem,
):
    f32 = jnp.float32
    bf16 = jnp.bfloat16
    x, yl, z, yh, core = place()
    psg = lax.axis_index("psg")
    mp = lax.axis_index("mp")
    y = yh * 2 + yl
    y_dev = (psg_of(x, 1 - yl, z), mp)

    def dev(axis, step):
        if axis == "x":
            return (psg_of(lax.rem(x + step, 4), yl, z), mp)
        return (psg_of(x, yl, lax.rem(z + step, 4)), mp)

    def yz_dev(k):
        t = lax.rem(yl * 4 + z + k, 8)
        return (x * 8 + t, mp)

    def mp_dev(k):
        return (psg, lax.rem(mp + k, NMP))

    def y_step(step):
        t = lax.rem(y + step, 4)
        return (psg_of(x, lax.rem(t, 2), z), (t // 2) * 2 + core)

    other_core = (psg, yh * 2 + 1 - core)
    same_half = (x // 2) == yh
    yl_to = jnp.where(same_half, yl, 1 - yl)

    block_to = (psg_of(x, yl_to, z), x)
    mine = x == mp

    load_tokens = pltpu.make_async_copy(tokens, normed, own_sem.at[0])
    load_tokens.start()
    own = pltpu.make_async_copy(
        w_ref, g_ref.at[:, x, z, pl.ds(pl.multiple_of(yl * 128, 128), 128), :], own_sem.at[1]
    )
    own.start()
    load_here = pltpu.make_async_copy(
        tokens.at[:, pl.ds(pl.multiple_of(mp * 1024, 128), 1024)], tok_here, own_sem.at[2]
    )
    load_here.start()
    for k in range(1, 4):
        signal(dev("x", k))
        signal(mp_dev(k))
    for k in range(1, 8):
        signal(yz_dev(k))
    signal(y_step(1))
    signal(y_step(3))

    @pl.when(mine)
    def _():
        for k in range(1, 4):
            m = lax.rem(mp + k, NMP)
            signal((psg_of(x, jnp.where((m // 2) == yh, yl, 1 - yl), z), m))

    for k in range(4):
        frm = psg_of(lax.rem(x + k, 4), yl, z)
        if k == 0:
            pl.when(jnp.logical_not(mine))(functools.partial(signal, (frm, x)))
        else:
            signal((frm, x))

    def g(k, xs, zs, yls, cols=None):
        rows = ALL if yls is None else pl.ds(pl.multiple_of(yls * 128, 128), 128)
        c = ALL if cols is None else pl.ds(cols[0], cols[1])
        return g_ref.at[k, xs, zs, rows, c]

    def wide(c):
        return None if c is None else (c * 256, 256)

    def low_cols(c):
        return (0, 256) if c is None else (c * 128, 128)

    def high_cols(c):
        return (256, 256) if c is None else (256 + c * 128, 128)

    sent = []

    def send(t, src, dst, device):
        copy = remote(src, dst, send_sem.at[t], recv_sem.at[t], device)
        copy.start()
        sent.append(copy)
        return copy

    class Ring:
        def __init__(self, t, axis, piece, first=None):
            self.t, self.axis, self.piece = t, axis, piece
            self.at = x if axis == "x" else z
            src = piece(self.at) if first is None else first
            self.up = send(t, src, piece(self.at), dev(axis, 1))
            self.down = send(t + 1, src, piece(self.at), dev(axis, 3))

        def forward(self, then=None):
            below = lax.rem(self.at + 3, 4)
            above = lax.rem(self.at + 1, 4)
            self.up.wait_recv()
            up = self.piece(below, 0)
            self.f_up = send(self.t + 2, up, up, dev(self.axis, 1))
            if then is not None:
                then(1, below)
            self.down.wait_recv()
            down = self.piece(above, 1)
            self.f_down = send(self.t + 3, down, down, dev(self.axis, 3))
            if then is not None:
                then(2, above)

        def end(self, then=None):
            self.f_up.wait_recv()
            self.f_down.wait_recv()
            if then is not None:
                then(3, lax.rem(self.at + 2, 4))

    go_step = jnp.where(core == 1, 1, 3)
    go_on = lax.rem(mp + go_step, 4) == x
    near = pl.ds(yh * 2, 2)
    far_half = pl.ds(2 - yh * 2, 2)

    class Blocks:
        def __init__(self, t, src, ref, own_t):
            self.t, self.ref, self.src = t, ref, src
            first = self.at(mp, yl, z)
            self.block = remote(src, first, send_sem.at[t], recv_sem.at[t + 1 + mp], block_to)
            self.keep = pltpu.make_async_copy(src, first, own_sem.at[own_t])
            n, f = self.at(near, yl, z), self.at(far_half, 1 - yl, z)
            self.ys = [
                remote(n, n, send_sem.at[t + 5], recv_sem.at[t + 5], y_dev),
                remote(f, f, send_sem.at[t + 6], recv_sem.at[t + 6], y_dev),
            ]

        def at(self, ms, yls, zs):
            col = pl.multiple_of((yls * 4 + zs) * 128, 128)
            return self.ref.at[ms, :, pl.ds(col, 128)]

        def x_copy(self, c, step, t):
            part = self.at(ALL, c, z)
            return remote(
                part, part, send_sem.at[self.t + t], recv_sem.at[self.t + 13 + c], dev("x", step)
            )

        def start(self):
            pl.when(mine)(self.keep.start)
            pl.when(jnp.logical_not(mine))(self.block.start)

        def across(self):
            @pl.when(mine)
            def _():
                for k in range(1, 4):
                    m = lax.rem(mp + k, NMP)
                    remote(
                        self.src,
                        self.at(m, yl, z),
                        send_sem.at[self.t],
                        recv_sem.at[self.t + 1 + m],
                        y_dev,
                    ).wait_recv()
                self.keep.wait()
                for copy in self.ys:
                    copy.start()

        def along(self):
            @pl.when(mine)
            def _():
                for copy in self.ys:
                    copy.wait_recv()
                for c in range(2):
                    self.x_copy(c, 1, 7 + c).start()
                    self.x_copy(c, 3, 9 + c).start()

        def forward(self):
            @pl.when(go_on)
            def _():
                for c in range(2):
                    self.x_copy(c, 1, 7 + c).wait_recv()
                    self.x_copy(c, go_step, 11 + c).start()

        def arrive(self):
            @pl.when(jnp.logical_not(jnp.logical_or(mine, go_on)))
            def _():
                for c in range(2):
                    self.x_copy(c, 1, 7 + c).wait_recv()

        def ring(self):
            t = self.t
            parts = [self.at(ALL, i, z) for i in range(2)]
            self.up = [send(t + 15 + i, parts[i], parts[i], dev("z", 1)) for i in range(2)]
            self.down = [send(t + 17 + i, parts[i], parts[i], dev("z", 3)) for i in (1, 0)]

        def ring_forward(self):
            self.up[0].wait_recv()
            part = self.at(ALL, 0, lax.rem(z + 3, 4))
            self.f_up = send(self.t + 19, part, part, dev("z", 1))
            self.down[0].wait_recv()
            part = self.at(ALL, 1, lax.rem(z + 1, 4))
            self.f_down = send(self.t + 20, part, part, dev("z", 3))

        def ring_end(self):
            for copy in (self.up[1], self.down[1], self.f_up, self.f_down):
                copy.wait_recv()

        def finish(self):
            @pl.when(mine)
            def _():
                for copy in self.ys:
                    copy.wait_send()
                for c in range(2):
                    self.x_copy(c, 1, 7 + c).wait_send()
                    self.x_copy(c, 3, 9 + c).wait_send()

            pl.when(jnp.logical_not(mine))(self.block.wait_send)

            @pl.when(go_on)
            def _():
                for c in range(2):
                    self.x_copy(c, go_step, 11 + c).wait_send()

    e_blocks = Blocks(188, enc_output, e_ref, 3)
    u_blocks = Blocks(209, block, u_ref, 4)

    pl.semaphore_wait(pltpu.get_barrier_semaphore(), jnp.where(mine, 18, 20))

    yd = send(0, w_ref.at[0], g(0, x, z, yl), y_dev)
    ye = send(1, w_ref.at[1], g(1, x, z, yl), y_dev)
    a1 = Ring(
        4, "x", lambda v, c=None: g(2, v, z, yl, low_cols(c)), w_ref.at[2, :, pl.ds(0, 256)]
    )
    b1 = Ring(
        8, "z", lambda v, c=None: g(2, x, v, yl, high_cols(c)), w_ref.at[2, :, pl.ds(256, 256)]
    )
    mp_buf[mp] = found[...]
    mps = [send(52 + k, found, mp_buf.at[mp], mp_dev(k)) for k in range(1, 4)]
    e_blocks.start()
    own.wait()

    d3, e3, yas, ybs = [None] * 4, [None] * 4, [None] * 4, [None] * 4

    def start_d3(i, u):
        d3[i] = Ring(140 + 4 * i, "z", lambda v, c=None: g(0, u, v, None, wide(c)))

    def start_e3(i, u):
        e3[i] = Ring(156 + 4 * i, "x", lambda v, c=None: g(1, v, u, None, wide(c)))

    def start_ya(i, u):
        plane = g(2, ALL, u, yl, low_cols(None))
        yas[i] = send(172 + i, plane, plane, y_dev)

    def start_yb(i, u):
        plane = g(2, u, ALL, yl, high_cols(None))
        ybs[i] = send(176 + i, plane, plane, y_dev)

    a1.forward()
    b1.forward()
    yd.wait_recv()
    d2 = Ring(20, "x", lambda v, c=None: g(0, v, z, None, wide(c)))
    ye.wait_recv()
    e2 = Ring(24, "z", lambda v, c=None: g(1, x, v, None, wide(c)))
    a1.end()
    a2 = Ring(12, "z", lambda v, c=None: g(2, ALL, v, yl, low_cols(c)))
    start_ya(0, z)
    b1.end()
    b2 = Ring(16, "x", lambda v, c=None: g(2, v, ALL, yl, high_cols(c)))
    start_yb(0, x)
    start_d3(0, x)
    start_e3(0, z)
    e_blocks.across()

    for copy in mps:
        copy.wait_recv()
    emb = mp_buf[0] + mp_buf[1] + mp_buf[2] + mp_buf[3]
    terms = dot3(emb * dec_gain[...], cross_query[...])
    squares = jnp.sum(emb * emb, axis=1, keepdims=True)
    x_buf[x, :, pl.ds(0, 512)] = terms
    x_buf[x, :, pl.ds(512, 128)] = jnp.broadcast_to(squares, (8, 128))
    xs = [send(56 + k, x_buf.at[x], x_buf.at[x], dev("x", k)) for k in range(1, 4)]

    e_blocks.along()
    d2.forward(start_d3)
    e2.forward(start_e3)

    load_tokens.wait()

    def norm_rows(first, count):
        def body(i, c):
            rows = pl.ds(pl.multiple_of(i * 16, 16), 16)
            values = normed[rows, :].astype(f32)
            mean = jnp.sum(values * values, axis=1, keepdims=True) / D
            inverse = lax.rsqrt(mean + EPSILON)
            scaled = (values * inverse * enc_gain[...]).astype(bf16)
            for p in range(NPSG):
                to = ((p // 8) * 4 + p % 4) * 2 + (p // 4) % 2
                normed[rows, pl.ds(to * 128, 128)] = scaled[:, p * 128 : (p + 1) * 128]
            return c

        lax.fori_loop(first, first + count, body, 0)

    a2.forward(start_ya)
    b2.forward(start_yb)
    d2.end(start_d3)
    e2.end(start_e3)
    norm_rows(0, 16)
    d3[0].forward()
    e3[0].forward()
    a2.end(start_ya)
    b2.end(start_yb)
    for copy in xs:
        copy.wait_recv()
    yz = yl * 4 + z
    yz_buf[yz] = x_buf[0] + x_buf[1] + x_buf[2] + x_buf[3]
    yzs = [send(60 + k, yz_buf.at[yz], yz_buf.at[yz], yz_dev(k)) for k in range(1, 8)]
    norm_rows(16, 16)
    d3[1].forward()
    e3[1].forward()
    e_blocks.forward()
    norm_rows(32, 16)
    d3[2].forward()
    e3[2].forward()

    for copy in yzs:
        copy.wait_recv()
    joined = yz_buf[0]
    for k in range(1, 8):
        joined = joined + yz_buf[k]
    cquery = joined[:, :512] * lax.rsqrt(joined[:, 512:513] / D + EPSILON)
    spread_q = jnp.broadcast_to(cquery[:, None, :], (8, 8, 512)).reshape(64, 512)
    head_of_row = lax.rem(lax.broadcasted_iota(jnp.int32, (64, 512), 0), 8)
    head_of_lane = lax.broadcasted_iota(jnp.int32, (64, 512), 1) // HEAD_DIM
    spread_q = jnp.where(head_of_row == head_of_lane, spread_q, 0.0)
    folded = dot3(spread_q, cross_keyval[0], 1)
    folded = folded * final_gain[:, pl.ds(pl.multiple_of(psg * 128, 128), 128)]
    high = folded.astype(bf16)
    block[pl.ds(0, 64), :] = high
    block[pl.ds(64, 64), :] = (folded - high.astype(f32)).astype(bf16)

    u_blocks.start()
    norm_rows(48, 16)
    d3[3].forward()
    e3[3].forward()
    e_blocks.arrive()
    e_blocks.ring()
    u_blocks.across()

    table = dot3(bias_in[...], onehot[...])
    for h in range(8):
        row = jnp.broadcast_to(table[h : h + 1], (SEQ, 512))
        bias[h] = pltpu.roll(row, 0, 1, stride=1, stride_axis=0)[:, :SEQ]

    def product(k, rows, xi, zi):
        at = pl.multiple_of((xi * 4 + zi) * 256, 256)
        return jnp.dot(
            normed[rows, pl.ds(at, 256)], g_ref[k, xi, zi], preferred_element_type=f32
        )

    def project(step):
        def body(i, c):
            step(pl.ds(pl.multiple_of(i * 256, 256), 256))
            return c

        lax.fori_loop(0, 4, body, 0)

    def first_q(rows):
        total = None
        for xi in range(4):
            for dz in (0, 1, 3):
                term = product(0, rows, xi, lax.rem(z + dz, 4))
                total = term if total is None else total + term
        acc[0, rows, :] = total

    def first_k(rows):
        total = None
        for zi in range(4):
            for dx in (0, 1, 3):
                term = product(1, rows, lax.rem(x + dx, 4), zi)
                total = term if total is None else total + term
        acc[1, rows, :] = total

    def all_v(rows):
        total = None
        for xi in range(4):
            for zi in range(4):
                term = product(2, rows, xi, zi)
                total = term if total is None else total + term
        qkv[2, rows, :] = total.astype(bf16)

    def last_q(rows):
        total = acc[0, rows, :]
        for xi in range(4):
            total = total + product(0, rows, xi, lax.rem(z + 2, 4))
        qkv[0, rows, :] = total.astype(bf16)

    def last_k(rows):
        total = acc[1, rows, :]
        for zi in range(4):
            total = total + product(1, rows, lax.rem(x + 2, 4), zi)
        qkv[1, rows, :] = total.astype(bf16)

    project(first_q)
    u_blocks.along()
    project(first_k)
    u_blocks.forward()
    for copy in yas + ybs:
        copy.wait_recv()
    project(all_v)
    u_blocks.arrive()
    u_blocks.ring()
    for ring in d3:
        ring.end()
    project(last_q)
    for ring in e3:
        ring.end()
    project(last_k)

    lane = lax.broadcasted_iota(jnp.int32, (SEQ, 128), 1)

    def attend(p):
        rows = pl.ds(p * SEQ, SEQ)

        def body(j, c):
            lanes = pl.ds(pl.multiple_of(j * 128, 128), 128)
            q2 = qkv[0, rows, lanes]
            k2 = qkv[1, rows, lanes]
            v2 = qkv[2, rows, lanes]
            outs = []
            for t in range(2):
                qt = jnp.where((lane // HEAD_DIM) == t, q2, jnp.zeros_like(q2))
                s = lax.dot_general(
                    qt, k2, (((1,), (1,)), ((), ())), preferred_element_type=f32
                )
                s = s + bias[2 * j + t] + mask_add[p, pl.ds(0, 1), :]
                wts = jnp.exp(s - jnp.max(s, axis=1, keepdims=True))
                scale = 1.0 / jnp.sum(wts, axis=1, keepdims=True)
                outs.append(
                    jnp.dot((wts * scale).astype(bf16), v2, preferred_element_type=f32)
                )
            att[mp, rows, lanes] = jnp.where(lane < HEAD_DIM, outs[0], outs[1]).astype(bf16)
            return c

        lax.fori_loop(0, 4, body, 0)

    hops, ends, cores, lasts = [], [], [], []
    far = (1 - yh) * 2 + core

    def hand_out(p):
        rows = pl.ds(p * SEQ, SEQ)
        cores.append(send(68 + p, att.at[mp, rows], att.at[mp, rows], other_core))
        hops.append(
            send(72 + p, att.at[mp, rows], transit.at[p], y_step(1 if p % 2 == 0 else 3))
        )

    def hand_on(p):
        rows = pl.ds(p * SEQ, SEQ)
        hops[p].wait_recv()
        frm = lax.rem(y + (3 if p % 2 == 0 else 1), 4)
        slot = (frm // 2) * 2 + core
        ends.append(
            send(76 + p, transit.at[p], att.at[slot, rows], y_step(1 if p % 2 == 0 else 3))
        )

    def hand_over(p):
        rows = pl.ds(p * SEQ, SEQ)
        ends[p].wait_recv()
        lasts.append(send(80 + p, att.at[far, rows], att.at[far, rows], other_core))

    attend(0)
    hand_out(0)
    attend(1)
    hand_out(1)
    hand_on(0)
    e_blocks.ring_forward()
    u_blocks.ring_forward()
    attend(2)
    hand_out(2)
    hand_on(1)
    hand_over(0)
    attend(3)
    hand_out(3)
    hand_on(2)
    hand_over(1)
    hand_on(3)
    load_here.wait()
    e_blocks.ring_end()
    u_blocks.ring_end()
    hand_over(2)
    hand_over(3)
    def out_project(p):
        rows = pl.ds(p * SEQ, SEQ)

        def out_cols(i, c):
            cols = pl.ds(pl.multiple_of(i * 512, 512), 512)
            total = None
            for m in range(NMP):
                term = jnp.dot(
                    att[m, rows, :], e_ref[m, :, cols], preferred_element_type=f32
                ).astype(bf16).astype(f32)
                total = term if total is None else total + term
            enc_out[rows, cols] = (tok_here[rows, cols].astype(f32) + total).astype(bf16)
            return c

        lax.fori_loop(0, 2, out_cols, 0)

    def cross_scores(p):
        enc = enc_out[pl.ds(p * SEQ, SEQ), :]
        wide_enc = enc.astype(f32)
        squares = jnp.sum(wide_enc * wide_enc, axis=1, keepdims=True)
        squares = jnp.broadcast_to(squares, (SEQ, 128)).T[:8]
        for m in range(NMP):
            both = lax.dot_general(
                u_ref[m], enc, (((1,), (1,)), ((), ())),
                preferred_element_type=f32,
            )
            both = both[:64] + both[64:]
            picked = jnp.zeros((16, SEQ), f32)
            for c in range(CLAIMS):
                picked = jnp.where(claims[p] == c, both[c * 16 : (c + 1) * 16], picked)
            sc_src[m, p, pl.ds(0, 16), :] = picked
            sc_src[m, p, pl.ds(16, 8), :] = squares
        out = []
        for k in range(1, 4):
            to = lax.rem(mp + k, NMP)
            out.append(
                send(84 + p * 3 + k - 1, sc_src.at[to, p], sc_in.at[mp, p], mp_dev(k))
            )
        sc_in[mp, p] = sc_src[mp, p]
        return out

    scs = []
    for p in range(4):
        cores[p].wait_recv()
        lasts[p].wait_recv()
        out_project(p)
        scs.append(cross_scores(p))

    crosses, inverses, maxima = [], [], []
    for p in range(4):
        for copy in scs[p]:
            copy.wait_recv()
        raw = sc_in[0, p] + sc_in[1, p] + sc_in[2, p] + sc_in[3, p]
        inverse = lax.rsqrt(raw[16:17] / D + EPSILON)
        cross = raw[:16] * inverse + extra[p]
        crosses.append(cross)
        inverses.append(inverse)
        maxima.append(jnp.broadcast_to(jnp.max(cross, axis=1, keepdims=True), (16, SEQ)))
    claim_max = []
    for c in range(CLAIMS):
        top = jnp.full((16, SEQ), MASKED, f32)
        for p in range(4):
            top = jnp.maximum(top, jnp.where(claims[p] == c, maxima[p], MASKED))
        claim_max.append(top)
    sums = []
    for p in range(4):
        chosen = claim_max[0]
        for c in range(1, CLAIMS):
            chosen = jnp.where(claims[p] == c, claim_max[c], chosen)
        wts = jnp.exp(crosses[p] - chosen)
        sums.append(jnp.broadcast_to(jnp.sum(wts, axis=1, keepdims=True), (16, SEQ)))
        all_w[mp, p] = (wts * inverses[p]).astype(bf16)
    totals = []
    for c in range(CLAIMS):
        total = jnp.zeros((16, SEQ), f32)
        for p in range(4):
            total = total + jnp.where(claims[p] == c, sums[p], 0.0)
        totals.append(total)
    first_row = lax.broadcasted_iota(jnp.int32, (8, 128), 0) == 0

    def lanes_of(parts, fill):
        column = jnp.concatenate([part[:, :128] for part in parts], axis=0)
        column = jnp.concatenate([column, jnp.full((64, 128), fill, f32)], axis=0)
        return column.T[:8]

    all_st[mp] = jnp.where(first_row, lanes_of(claim_max, MASKED), lanes_of(totals, 0.0))
    ws = [send(96 + k, all_w.at[mp], all_w.at[mp], mp_dev(k)) for k in range(3 + 1) if k]
    sts = [send(99 + k, all_st.at[mp], all_st.at[mp], mp_dev(k)) for k in range(3 + 1) if k]
    for copy in ws + sts:
        copy.wait_recv()

    for p in range(4):
        for m in range(NMP):
            w_mp = all_w[m, p].astype(f32)
            for c in range(CLAIMS):
                lhs[p, pl.ds(m * 64 + c * 16, 16), :] = jnp.where(
                    claims[p] == c, w_mp, 0.0
                ).astype(bf16)
    for i in range(2):
        total = None
        for p in range(4):
            term = jnp.dot(
                lhs[p], enc_out[pl.ds(p * SEQ, SEQ), pl.ds(i * 512, 512)],
                preferred_element_type=f32,
            )
            total = term if total is None else total + term
        for zt in range(4):
            y_src[zt, i] = total[:, zt * 128 : (zt + 1) * 128].astype(bf16)
    y_copies, st_copies = [], []
    for k in range(1, 4):
        tz = lax.rem(z + k, 4)
        y_copies.append(send(103 + k, y_src.at[tz], y_zin.at[z], dev("z", k)))
        st_copies.append(send(106 + k, all_st, st_z.at[z], dev("z", k)))
    y_zin[z] = y_src[z]
    st_z[z] = all_st[...]

    def merge(stats, rows):
        top = stats[0][0:1]
        for st in stats[1:]:
            top = jnp.maximum(top, st[0:1])
        total = jnp.zeros((1, 128), f32)
        results = [jnp.zeros((64, 128), f32) for _ in rows[0]]
        for st, these in zip(stats, rows):
            scale = jnp.exp(st[0:1] - top)
            total = total + scale * st[1:2]
            column = jnp.broadcast_to(scale, (128, 128)).T[:64]
            results = [r + column * t.astype(f32) for r, t in zip(results, these)]
        both = jnp.where(
            first_row, jnp.broadcast_to(top, (8, 128)), jnp.broadcast_to(total, (8, 128))
        )
        return both, results

    for copy in y_copies + st_copies:
        copy.wait_recv()
    for m in range(NMP):
        part = pl.ds(m * 64, 64)
        both, results = merge(
            [st_z[j, m] for j in range(4)],
            [[y_zin[j, i, part, :] for i in range(2)] for j in range(4)],
        )
        st_one[m] = both
        for i in range(2):
            y_one[i, m] = results[i]
    y_ysrc[...] = y_one[1 - yl].astype(bf16)
    yc = send(110, y_ysrc, y_yin, y_dev)
    ystc = send(111, st_one, st_yin, y_dev)
    yc.wait_recv()
    ystc.wait_recv()
    for m in range(NMP):
        both, results = merge([st_one[m], st_yin[m]], [[y_one[yl, m]], [y_yin[m]]])
        st_two[m] = both
        y_two[m] = results[0]

    def to_owner(k):
        m = lax.rem(mp + k, NMP)
        target = (psg_of(mp, yl, z), m)
        return (
            remote(y_two.at[m], y_in.at[x], send_sem.at[112 + k], recv_sem.at[112 + x], target),
            remote(st_two.at[m], st_in.at[x], send_sem.at[116 + k], recv_sem.at[116 + x], target),
        )

    def from_source(k):
        frm = lax.rem(x + k, 4)
        target = (psg_of(frm, yl, z), x)
        return (
            remote(y_two.at[0], y_in.at[frm], send_sem.at[112], recv_sem.at[112 + frm], target),
            remote(st_two.at[0], st_in.at[frm], send_sem.at[116], recv_sem.at[116 + frm], target),
        )

    @pl.when(mine)
    def _():
        y_in[x] = y_two[mp]
        st_in[x] = st_two[mp]

    @pl.when(jnp.logical_not(mine))
    def _():
        for copy in to_owner(0):
            copy.start()

    for k in range(1, 4):
        for copy in to_owner(k):
            copy.start()

    @pl.when(jnp.logical_not(mine))
    def _():
        for copy in from_source(0):
            copy.wait_recv()

    for k in range(1, 4):
        for copy in from_source(k):
            copy.wait_recv()
    both, results = merge([st_in[j] for j in range(4)], [[y_in[j]] for j in range(4)])
    total = jnp.broadcast_to(both[1:2], (128, 128)).T[:64]
    mean_rows = results[0] / total
    mean_rows = mean_rows * final_gain[:, pl.ds(pl.multiple_of(psg * 128, 128), 128)]

    products = dot3(mean_rows, cross_keyval[1])
    products = jnp.where(head_of_row == head_of_lane, products, 0.0)
    x_buf2[x] = jnp.sum(products.reshape(8, 8, 512), axis=1)
    xs = [send(120 + k, x_buf2.at[x], x_buf2.at[x], dev("x", k)) for k in range(1, 4)]
    for copy in xs:
        copy.wait_recv()
    yz_buf2[yz] = x_buf2[0] + x_buf2[1] + x_buf2[2] + x_buf2[3]
    yzs = [send(124 + k, yz_buf2.at[yz], yz_buf2.at[yz], yz_dev(k)) for k in range(1, 8)]
    for copy in yzs:
        copy.wait_recv()
    cross_attn = yz_buf2[0]
    for k in range(1, 8):
        cross_attn = cross_attn + yz_buf2[k]
    mp_buf2[mp] = dot3(cross_attn, cross_output[...])
    lasts = [send(132 + k, mp_buf2.at[mp], mp_buf2.at[mp], mp_dev(k)) for k in range(1, 4)]
    for copy in lasts:
        copy.wait_recv()
    final = (mp_buf2[0] + mp_buf2[1] + mp_buf2[2] + mp_buf2[3]) + (
        mp_buf[0] + mp_buf[1] + mp_buf[2] + mp_buf[3]
    )
    share = final[:, :32]
    for m in range(1, NMP):
        share = jnp.where(mp == m, final[:, m * 32 : (m + 1) * 32], share)
    dec_out[...] = share.astype(bf16)

    for copy in sent:
        copy.wait_send()
    for k in range(1, 4):
        for copy in to_owner(k):
            copy.wait_send()

    @pl.when(jnp.logical_not(mine))
    def _():
        for copy in to_owner(0):
            copy.wait_send()

    e_blocks.finish()
    u_blocks.finish()


def encoder(args):
    tok_rows = args[0].shape[0]
    bf16 = jnp.bfloat16
    f32 = jnp.float32
    return pl.pallas_call(
        encoder_kernel,
        out_shape=(
            jax.ShapeDtypeStruct((tok_rows, 1024), bf16),
            jax.ShapeDtypeStruct((CLAIMS * POS, 32), bf16),
        ),
        in_specs=[ANY, VMEM, ANY, VMEM, VMEM, VMEM, ANY] + [VMEM] * 8,
        out_specs=(VMEM, VMEM),
        scratch_shapes=[
            pltpu.VMEM((3, 4, 4, 256, 512), bf16),
            pltpu.VMEM((tok_rows, D), bf16),
            pltpu.VMEM((2, tok_rows, 512), jnp.float32),
            pltpu.VMEM((3, tok_rows, 512), bf16),
            pltpu.VMEM((NMP, 512, 1024), bf16),
            pltpu.VMEM((NMP, 128, 1024), bf16),
            pltpu.VMEM((NMP, tok_rows, 512), bf16),
            pltpu.VMEM((4, SEQ, 512), bf16),
            pltpu.VMEM((8, SEQ, SEQ), jnp.float32),
            pltpu.VMEM((tok_rows, 1024), bf16),
            pltpu.VMEM((128, 128), bf16),
            pltpu.VMEM((NMP, 8, 128), jnp.float32),
            pltpu.VMEM((4, 8, 640), jnp.float32),
            pltpu.VMEM((8, 8, 640), f32),
            pltpu.VMEM((NMP, 4, 24, SEQ), f32),
            pltpu.VMEM((NMP, 4, 24, SEQ), f32),
            pltpu.VMEM((NMP, 4, 16, SEQ), bf16),
            pltpu.VMEM((NMP, 8, 128), f32),
            pltpu.VMEM((4, 256, SEQ), bf16),
            pltpu.VMEM((4, 2, 256, 128), bf16),
            pltpu.VMEM((4, 2, 256, 128), bf16),
            pltpu.VMEM((4, NMP, 8, 128), f32),
            pltpu.VMEM((2, NMP, 64, 128), f32),
            pltpu.VMEM((NMP, 64, 128), bf16),
            pltpu.VMEM((NMP, 64, 128), bf16),
            pltpu.VMEM((NMP, 8, 128), f32),
            pltpu.VMEM((NMP, 8, 128), f32),
            pltpu.VMEM((NMP, 64, 128), f32),
            pltpu.VMEM((NMP, 8, 128), f32),
            pltpu.VMEM((4, 64, 128), f32),
            pltpu.VMEM((4, 8, 128), f32),
            pltpu.VMEM((4, 8, 512), f32),
            pltpu.VMEM((8, 8, 512), f32),
            pltpu.VMEM((NMP, 8, 128), f32),
            pltpu.SemaphoreType.DMA((230,)),
            pltpu.SemaphoreType.DMA((230,)),
            pltpu.SemaphoreType.DMA((5,)),
        ],
        compiler_params=pltpu.CompilerParams(
            collective_id=1, has_side_effects=True, vmem_limit_bytes=58 << 20
        ),
    )(*args)


def shards(
    tokens,
    lengths,
    assignment,
    retrieval,
    enc_gain,
    enc_qkv,
    position_bias,
    enc_output,
    final_gain,
    embedding,
    dec_tokens,
    dec_gain,
    cross_query,
    cross_keyval,
    cross_output,
):
    found, mask_add, claims, extra = lookup(
        dec_tokens.T, lengths, assignment, retrieval, embedding
    )
    onehot = bucket_onehot(SEQ, BUCKETS, MAXDIST)
    onehot = np.concatenate([onehot[:, 255:], np.zeros((BUCKETS, 1)), onehot[:, :255]], axis=1)
    encoded, decoded = encoder(
        (
            tokens,
            enc_gain.reshape(1, D),
            enc_qkv,
            position_bias,
            jnp.asarray(onehot, jnp.bfloat16),
            mask_add,
            enc_output,
            final_gain.reshape(1, D),
            found,
            dec_gain.reshape(1, 128),
            cross_query,
            cross_keyval,
            cross_output,
            claims,
            extra,
        )
    )
    return (encoded, decoded.reshape(CLAIMS, POS, 32))


def solution(mesh):
    in_specs = (
        P("psg", None),
        P("psg"),
        P("psg"),
        P("psg"),
        P(),
        P(None, "psg", "mp"),
        P("mp", None),
        P("mp", "psg"),
        P(),
        P("mp", "psg"),
        P(),
        P("psg"),
        P("psg", "mp"),
        P(None, "psg", "mp"),
        P("mp", "psg"),
    )
    out_specs = (P("psg", "mp"), P(None, None, ("psg", "mp")))
    return jax.shard_map(shards, mesh=mesh, in_specs=in_specs, out_specs=out_specs, check_vma=False)
```

```python
import functools
import math

import jax
import jax.numpy as jnp
import numpy as np
from jax import lax
from jax.experimental import pallas as pl
from jax.experimental.pallas import tpu as pltpu
from jax.sharding import PartitionSpec as P

D = 4096
HEAD_DIM = 64
BUCKETS = 32
MAXDIST = 128
SEQ = 256
CLAIMS = 4
POS = 2
NPSG = 32
NMP = 4
EPSILON = 1e-06
MASKED = -1e30
MESH = pl.DeviceIdType.MESH
ANY = pl.BlockSpec(memory_space=pl.ANY)
VMEM = pl.BlockSpec(memory_space=pltpu.VMEM)


def bucket_onehot(length, buckets, max_distance):
    halfway = buckets // 2
    exact_max = halfway // 2
    relative_list = list(range(-(length - 1), length))
    beyond_list = [
        min(
            halfway - 1,
            exact_max
            + math.floor(
                math.log(max(abs(shift), 1) / exact_max)
                / math.log(max_distance / exact_max)
                * (halfway - exact_max)
            ),
        )
        for shift in relative_list
    ]
    relative = np.array(relative_list)
    beyond = np.array(beyond_list)
    distance = np.abs(relative)
    bucket_ids = np.where(relative > 0, halfway, 0) + np.where(
        distance < exact_max, distance, beyond
    )
    return (bucket_ids[None, :] == np.arange(buckets)[:, None]).astype(np.float32)


def place():
    psg = lax.axis_index("psg")
    mp = lax.axis_index("mp")
    return psg // 8, (psg // 4) % 2, psg % 4, mp // 2, mp % 2


def psg_of(x, yl, z):
    return x * 8 + yl * 4 + z


def remote(src, dst, send_sem, recv_sem, device):
    return pltpu.make_async_remote_copy(
        src_ref=src,
        dst_ref=dst,
        send_sem=send_sem,
        recv_sem=recv_sem,
        device_id=device,
        device_id_type=MESH,
    )


def signal(device):
    pl.semaphore_signal(
        pltpu.get_barrier_semaphore(), inc=1, device_id=device, device_id_type=MESH
    )


def lookup_kernel(ids, lengths, assignment, retrieval, table, out, mask_add, claims, extra, rows, sems):
    copies = []
    held = []
    base = lax.axis_index("mp") * table.shape[0]
    for i in range(CLAIMS * POS):
        local = ids[i % POS, i // POS] - base
        inside = jnp.logical_and(local >= 0, local < table.shape[0])
        local = jnp.clip(local, 0, table.shape[0] - 1)
        start = pl.multiple_of((local // 16) * 16, 16)
        held.append(jnp.where(inside, local - start, -1))
        copies.append(
            pltpu.make_async_copy(table.at[pl.ds(start, 16), :], rows.at[i], sems.at[i])
        )
        copies[-1].start()
    slot = lax.broadcasted_iota(jnp.int32, (16, SEQ), 1)
    for p in range(4):
        add = jnp.where(slot < lengths[p], 0.0, MASKED)
        mask_add[p] = add[:8]
        extra[p] = add + retrieval[p]
        claims[p] = jnp.zeros((16, SEQ), jnp.int32) + assignment[p]
    at = lax.broadcasted_iota(jnp.int32, (16, 128), 0)
    for i in range(CLAIMS * POS):
        copies[i].wait()
        picked = jnp.where(at == held[i], rows[i].astype(jnp.float32), 0.0)
        out[pl.ds(i, 1), :] = jnp.sum(picked, axis=0, keepdims=True)


def lookup(ids, lengths, assignment, retrieval, table):
    smem = pl.BlockSpec(memory_space=pltpu.SMEM)
    f32 = jnp.float32
    return pl.pallas_call(
        lookup_kernel,
        out_shape=(
            jax.ShapeDtypeStruct((CLAIMS * POS, 128), f32),
            jax.ShapeDtypeStruct((4, 8, SEQ), f32),
            jax.ShapeDtypeStruct((4, 16, SEQ), jnp.int32),
            jax.ShapeDtypeStruct((4, 16, SEQ), f32),
        ),
        in_specs=[smem] * 4 + [ANY],
        out_specs=(VMEM,) * 4,
        scratch_shapes=[
            pltpu.VMEM((CLAIMS * POS, 16, 128), jnp.bfloat16),
            pltpu.SemaphoreType.DMA((CLAIMS * POS,)),
        ],
    )(ids, lengths, assignment, retrieval, table)


def split3(values):
    high = values.astype(jnp.bfloat16)
    rest = values - high.astype(jnp.float32)
    middle = rest.astype(jnp.bfloat16)
    low = (rest - middle.astype(jnp.float32)).astype(jnp.bfloat16)
    return jnp.concatenate([high, middle, low], axis=0)


def dot3(values, weights, contract=0):
    n = values.shape[0]
    parts = lax.dot_general(
        split3(values),
        weights,
        (((1,), (contract,)), ((), ())),
        preferred_element_type=jnp.float32,
    )
    return parts[:n] + parts[n : 2 * n] + parts[2 * n :]


ALL = slice(None)


def encoder_kernel(
    tokens,
    enc_gain,
    w_ref,
    bias_in,
    onehot,
    mask_add,
    enc_output,
    final_gain,
    found,
    dec_gain,
    cross_query,
    cross_keyval,
    cross_output,
    claims,
    extra,
    enc_out,
    dec_out,
    g_ref,
    normed,
    acc,
    qkv,
    e_ref,
    u_ref,
    att,
    transit,
    bias,
    tok_here,
    block,
    mp_buf,
    x_buf,
    yz_buf,
    sc_src,
    sc_in,
    all_w,
    all_st,
    lhs,
    y_src,
    y_zin,
    st_z,
    y_one,
    st_one,
    y_in,
    st_in,
    x_buf2,
    yz_buf2,
    mp_buf2,
    send_sem,
    recv_sem,
    own_sem,
):
    f32 = jnp.float32
    bf16 = jnp.bfloat16
    x, yl, z, yh, core = place()
    psg = lax.axis_index("psg")
    mp = lax.axis_index("mp")
    y = yh * 2 + yl
    y_dev = (psg_of(x, 1 - yl, z), mp)

    def dev(axis, step):
        if axis == "x":
            return (psg_of(lax.rem(x + step, 4), yl, z), mp)
        return (psg_of(x, yl, lax.rem(z + step, 4)), mp)

    def yz_dev(k):
        t = lax.rem(yl * 4 + z + k, 8)
        return (x * 8 + t, mp)

    def mp_dev(k):
        return (psg, lax.rem(mp + k, NMP))

    def y_step(step):
        t = lax.rem(y + step, 4)
        return (psg_of(x, lax.rem(t, 2), z), (t // 2) * 2 + core)

    other_core = (psg, yh * 2 + 1 - core)
    same_half = (x // 2) == yh
    yl_to = jnp.where(same_half, yl, 1 - yl)

    block_to = (psg_of(x, yl_to, z), x)
    mine = x == mp

    load_tokens = pltpu.make_async_copy(tokens, normed, own_sem.at[0])
    load_tokens.start()
    own = pltpu.make_async_copy(
        w_ref, g_ref.at[:, x, z, pl.ds(pl.multiple_of(yl * 128, 128), 128), :], own_sem.at[1]
    )
    own.start()
    load_here = pltpu.make_async_copy(
        tokens.at[:, pl.ds(pl.multiple_of(mp * 1024, 128), 1024)], tok_here, own_sem.at[2]
    )
    load_here.start()
    for k in range(1, 4):
        signal(dev("x", k))
        signal(mp_dev(k))
    for k in range(1, 8):
        signal(yz_dev(k))
    signal(y_step(1))
    signal(y_step(3))

    @pl.when(mine)
    def _():
        for k in range(1, 4):
            m = lax.rem(mp + k, NMP)
            signal((psg_of(x, jnp.where((m // 2) == yh, yl, 1 - yl), z), m))

    for k in range(8):
        frm = psg_of(lax.rem(x + k, 4), lax.rem(yl + k // 4, 2), z)
        if k == 0:
            pl.when(jnp.logical_not(mine))(functools.partial(signal, (frm, x)))
        else:
            signal((frm, x))

    def g(k, xs, zs, yls, cols=None):
        rows = ALL if yls is None else pl.ds(pl.multiple_of(yls * 128, 128), 128)
        c = ALL if cols is None else pl.ds(cols[0], cols[1])
        return g_ref.at[k, xs, zs, rows, c]

    def wide(c):
        return None if c is None else (c * 256, 256)

    def low_cols(c):
        return (0, 256) if c is None else (c * 128, 128)

    def high_cols(c):
        return (256, 256) if c is None else (256 + c * 128, 128)

    sent = []

    def send(t, src, dst, device):
        copy = remote(src, dst, send_sem.at[t], recv_sem.at[t], device)
        copy.start()
        sent.append(copy)
        return copy

    class Ring:
        def __init__(self, t, axis, piece, first=None):
            self.t, self.axis, self.piece = t, axis, piece
            self.at = x if axis == "x" else z
            src = piece(self.at) if first is None else first
            self.up = send(t, src, piece(self.at), dev(axis, 1))
            self.down = send(t + 1, src, piece(self.at), dev(axis, 3))

        def forward(self, then=None):
            below = lax.rem(self.at + 3, 4)
            above = lax.rem(self.at + 1, 4)
            self.up.wait_recv()
            up = self.piece(below, 0)
            self.f_up = send(self.t + 2, up, up, dev(self.axis, 1))
            if then is not None:
                then(1, below)
            self.down.wait_recv()
            down = self.piece(above, 1)
            self.f_down = send(self.t + 3, down, down, dev(self.axis, 3))
            if then is not None:
                then(2, above)

        def end(self, then=None):
            self.f_up.wait_recv()
            self.f_down.wait_recv()
            if then is not None:
                then(3, lax.rem(self.at + 2, 4))

    go_step = jnp.where(core == 1, 1, 3)
    go_on = lax.rem(mp + go_step, 4) == x
    near = pl.ds(yh * 2, 2)
    far_half = pl.ds(2 - yh * 2, 2)

    class Blocks:
        def __init__(self, t, src, ref, own_t):
            self.t, self.ref, self.src = t, ref, src
            first = self.at(mp, yl, z)
            self.block = remote(src, first, send_sem.at[t], recv_sem.at[t + 1 + mp], block_to)
            self.keep = pltpu.make_async_copy(src, first, own_sem.at[own_t])
            n, f = self.at(near, yl, z), self.at(far_half, 1 - yl, z)
            self.ys = [
                remote(n, n, send_sem.at[t + 5], recv_sem.at[t + 5], y_dev),
                remote(f, f, send_sem.at[t + 6], recv_sem.at[t + 6], y_dev),
            ]

        def at(self, ms, yls, zs):
            col = pl.multiple_of((yls * 4 + zs) * 128, 128)
            return self.ref.at[ms, :, pl.ds(col, 128)]

        def x_copy(self, c, step, t):
            part = self.at(ALL, c, z)
            return remote(
                part, part, send_sem.at[self.t + t], recv_sem.at[self.t + 13 + c], dev("x", step)
            )

        def start(self):
            pl.when(mine)(self.keep.start)
            pl.when(jnp.logical_not(mine))(self.block.start)

        def across(self):
            @pl.when(mine)
            def _():
                for k in range(1, 4):
                    m = lax.rem(mp + k, NMP)
                    remote(
                        self.src,
                        self.at(m, yl, z),
                        send_sem.at[self.t],
                        recv_sem.at[self.t + 1 + m],
                        y_dev,
                    ).wait_recv()
                self.keep.wait()
                for copy in self.ys:
                    copy.start()

        def along(self):
            @pl.when(mine)
            def _():
                for copy in self.ys:
                    copy.wait_recv()
                for c in range(2):
                    self.x_copy(c, 1, 7 + c).start()
                    self.x_copy(c, 3, 9 + c).start()

        def forward(self):
            @pl.when(go_on)
            def _():
                for c in range(2):
                    self.x_copy(c, 1, 7 + c).wait_recv()
                    self.x_copy(c, go_step, 11 + c).start()

        def arrive(self):
            @pl.when(jnp.logical_not(jnp.logical_or(mine, go_on)))
            def _():
                for c in range(2):
                    self.x_copy(c, 1, 7 + c).wait_recv()

        def ring(self):
            t = self.t
            parts = [self.at(ALL, i, z) for i in range(2)]
            self.up = [send(t + 15 + i, parts[i], parts[i], dev("z", 1)) for i in range(2)]
            self.down = [send(t + 17 + i, parts[i], parts[i], dev("z", 3)) for i in (1, 0)]

        def ring_forward(self):
            self.up[0].wait_recv()
            part = self.at(ALL, 0, lax.rem(z + 3, 4))
            self.f_up = send(self.t + 19, part, part, dev("z", 1))
            self.down[0].wait_recv()
            part = self.at(ALL, 1, lax.rem(z + 1, 4))
            self.f_down = send(self.t + 20, part, part, dev("z", 3))

        def ring_end(self):
            for copy in (self.up[1], self.down[1], self.f_up, self.f_down):
                copy.wait_recv()

        def finish(self):
            @pl.when(mine)
            def _():
                for copy in self.ys:
                    copy.wait_send()
                for c in range(2):
                    self.x_copy(c, 1, 7 + c).wait_send()
                    self.x_copy(c, 3, 9 + c).wait_send()

            pl.when(jnp.logical_not(mine))(self.block.wait_send)

            @pl.when(go_on)
            def _():
                for c in range(2):
                    self.x_copy(c, go_step, 11 + c).wait_send()

    e_blocks = Blocks(188, enc_output, e_ref, 3)
    u_blocks = Blocks(209, block, u_ref, 4)

    pl.semaphore_wait(pltpu.get_barrier_semaphore(), jnp.where(mine, 22, 24))

    yd = send(0, w_ref.at[0], g(0, x, z, yl), y_dev)
    ye = send(1, w_ref.at[1], g(1, x, z, yl), y_dev)
    a1 = Ring(
        4, "x", lambda v, c=None: g(2, v, z, yl, low_cols(c)), w_ref.at[2, :, pl.ds(0, 256)]
    )
    b1 = Ring(
        8, "z", lambda v, c=None: g(2, x, v, yl, high_cols(c)), w_ref.at[2, :, pl.ds(256, 256)]
    )
    mp_buf[mp] = found[...]
    mps = [send(52 + k, found, mp_buf.at[mp], mp_dev(k)) for k in range(1, 4)]
    e_blocks.start()
    own.wait()

    d3, e3, yas, ybs = [None] * 4, [None] * 4, [None] * 4, [None] * 4

    def start_d3(i, u):
        d3[i] = Ring(140 + 4 * i, "z", lambda v, c=None: g(0, u, v, None, wide(c)))

    def start_e3(i, u):
        e3[i] = Ring(156 + 4 * i, "x", lambda v, c=None: g(1, v, u, None, wide(c)))

    def start_ya(i, u):
        plane = g(2, ALL, u, yl, low_cols(None))
        yas[i] = send(172 + i, plane, plane, y_dev)

    def start_yb(i, u):
        plane = g(2, u, ALL, yl, high_cols(None))
        ybs[i] = send(176 + i, plane, plane, y_dev)

    a1.forward()
    b1.forward()
    yd.wait_recv()
    d2 = Ring(20, "x", lambda v, c=None: g(0, v, z, None, wide(c)))
    ye.wait_recv()
    e2 = Ring(24, "z", lambda v, c=None: g(1, x, v, None, wide(c)))
    start_d3(0, x)
    start_e3(0, z)
    a1.end()
    a2 = Ring(12, "z", lambda v, c=None: g(2, ALL, v, yl, low_cols(c)))
    start_ya(0, z)
    b1.end()
    b2 = Ring(16, "x", lambda v, c=None: g(2, v, ALL, yl, high_cols(c)))
    start_yb(0, x)
    e_blocks.across()

    for copy in mps:
        copy.wait_recv()
    emb = mp_buf[0] + mp_buf[1] + mp_buf[2] + mp_buf[3]
    terms = dot3(emb * dec_gain[...], cross_query[...])
    squares = jnp.sum(emb * emb, axis=1, keepdims=True)
    x_buf[x, :, pl.ds(0, 512)] = terms
    x_buf[x, :, pl.ds(512, 128)] = jnp.broadcast_to(squares, (8, 128))
    xs = [send(56 + k, x_buf.at[x], x_buf.at[x], dev("x", k)) for k in range(1, 4)]

    e_blocks.along()
    load_tokens.wait()

    def norm_rows(first, count):
        def body(i, c):
            rows = pl.ds(pl.multiple_of(i * 16, 16), 16)
            values = normed[rows, :].astype(f32)
            mean = jnp.sum(values * values, axis=1, keepdims=True) / D
            inverse = lax.rsqrt(mean + EPSILON)
            scaled = (values * inverse * enc_gain[...]).astype(bf16)
            for p in range(NPSG):
                to = ((p // 8) * 4 + p % 4) * 2 + (p // 4) % 2
                normed[rows, pl.ds(to * 128, 128)] = scaled[:, p * 128 : (p + 1) * 128]
            return c

        lax.fori_loop(first, first + count, body, 0)

    norm_rows(0, 8)
    d2.forward(start_d3)
    e2.forward(start_e3)

    norm_rows(8, 8)
    a2.forward(start_ya)
    b2.forward(start_yb)
    d2.end(start_d3)
    e2.end(start_e3)
    d3[0].forward()
    e3[0].forward()
    a2.end(start_ya)
    b2.end(start_yb)
    for copy in xs:
        copy.wait_recv()
    yz = yl * 4 + z
    yz_buf[yz] = x_buf[0] + x_buf[1] + x_buf[2] + x_buf[3]
    yzs = [send(60 + k, yz_buf.at[yz], yz_buf.at[yz], yz_dev(k)) for k in range(1, 8)]
    norm_rows(16, 16)
    d3[1].forward()
    e3[1].forward()
    e_blocks.forward()
    norm_rows(32, 16)
    d3[2].forward()
    e3[2].forward()

    for copy in yzs:
        copy.wait_recv()
    joined = yz_buf[0]
    for k in range(1, 8):
        joined = joined + yz_buf[k]
    cquery = joined[:, :512] * lax.rsqrt(joined[:, 512:513] / D + EPSILON)
    spread_q = jnp.broadcast_to(cquery[:, None, :], (8, 8, 512)).reshape(64, 512)
    head_of_row = lax.rem(lax.broadcasted_iota(jnp.int32, (64, 512), 0), 8)
    head_of_lane = lax.broadcasted_iota(jnp.int32, (64, 512), 1) // HEAD_DIM
    spread_q = jnp.where(head_of_row == head_of_lane, spread_q, 0.0)
    folded = dot3(spread_q, cross_keyval[0], 1)
    folded = folded * final_gain[:, pl.ds(pl.multiple_of(psg * 128, 128), 128)]
    high = folded.astype(bf16)
    block[pl.ds(0, 64), :] = high
    block[pl.ds(64, 64), :] = (folded - high.astype(f32)).astype(bf16)

    u_blocks.start()
    norm_rows(48, 16)
    d3[3].forward()
    e3[3].forward()
    e_blocks.arrive()
    e_blocks.ring()

    table = dot3(bias_in[...], onehot[...])
    for h in range(8):
        row = jnp.broadcast_to(table[h : h + 1], (SEQ, 512))
        bias[h] = pltpu.roll(row, 0, 1, stride=1, stride_axis=0)[:, :SEQ]

    def product(k, rows, xi, zi):
        at = pl.multiple_of((xi * 4 + zi) * 256, 256)
        return jnp.dot(
            normed[rows, pl.ds(at, 256)], g_ref[k, xi, zi], preferred_element_type=f32
        )

    def project(step):
        def body(i, c):
            step(pl.ds(pl.multiple_of(i * 256, 256), 256))
            return c

        lax.fori_loop(0, 4, body, 0)

    def first_q(rows):
        total = None
        for xi in range(4):
            for dz in (0, 1, 3):
                term = product(0, rows, xi, lax.rem(z + dz, 4))
                total = term if total is None else total + term
        acc[0, rows, :] = total

    def first_k(rows):
        total = None
        for zi in range(4):
            for dx in (0, 1, 3):
                term = product(1, rows, lax.rem(x + dx, 4), zi)
                total = term if total is None else total + term
        acc[1, rows, :] = total

    def all_v(rows):
        total = None
        for xi in range(4):
            for zi in range(4):
                term = product(2, rows, xi, zi)
                total = term if total is None else total + term
        qkv[2, rows, :] = total.astype(bf16)

    def last_q(rows):
        total = acc[0, rows, :]
        for xi in range(4):
            total = total + product(0, rows, xi, lax.rem(z + 2, 4))
        qkv[0, rows, :] = total.astype(bf16)

    def last_k(rows):
        total = acc[1, rows, :]
        for zi in range(4):
            total = total + product(1, rows, lax.rem(x + 2, 4), zi)
        qkv[1, rows, :] = total.astype(bf16)

    project(first_q)
    u_blocks.across()
    project(first_k)
    u_blocks.along()
    for copy in yas + ybs:
        copy.wait_recv()
    project(all_v)
    u_blocks.forward()
    for ring in d3:
        ring.end()
    project(last_q)
    for ring in e3:
        ring.end()
    project(last_k)

    lane = lax.broadcasted_iota(jnp.int32, (SEQ, 128), 1)

    def attend(p):
        rows = pl.ds(p * SEQ, SEQ)

        def body(j, c):
            lanes = pl.ds(pl.multiple_of(j * 128, 128), 128)
            q2 = qkv[0, rows, lanes]
            k2 = qkv[1, rows, lanes]
            v2 = qkv[2, rows, lanes]
            outs = []
            for t in range(2):
                qt = jnp.where((lane // HEAD_DIM) == t, q2, jnp.zeros_like(q2))
                s = lax.dot_general(
                    qt, k2, (((1,), (1,)), ((), ())), preferred_element_type=f32
                )
                s = s + bias[2 * j + t] + mask_add[p, pl.ds(0, 1), :]
                wts = jnp.exp(s - jnp.max(s, axis=1, keepdims=True))
                scale = 1.0 / jnp.sum(wts, axis=1, keepdims=True)
                outs.append(
                    jnp.dot((wts * scale).astype(bf16), v2, preferred_element_type=f32)
                )
            att[mp, rows, lanes] = jnp.where(lane < HEAD_DIM, outs[0], outs[1]).astype(bf16)
            return c

        lax.fori_loop(0, 4, body, 0)

    hops, ends, cores, lasts = [], [], [], []
    far = (1 - yh) * 2 + core

    def hand_out(p):
        rows = pl.ds(p * SEQ, SEQ)
        cores.append(send(68 + p, att.at[mp, rows], att.at[mp, rows], other_core))
        hops.append(
            send(72 + p, att.at[mp, rows], transit.at[p], y_step(1 if p % 2 == 0 else 3))
        )

    def hand_on(p):
        rows = pl.ds(p * SEQ, SEQ)
        hops[p].wait_recv()
        frm = lax.rem(y + (3 if p % 2 == 0 else 1), 4)
        slot = (frm // 2) * 2 + core
        ends.append(
            send(76 + p, transit.at[p], att.at[slot, rows], y_step(1 if p % 2 == 0 else 3))
        )

    def hand_over(p):
        rows = pl.ds(p * SEQ, SEQ)
        ends[p].wait_recv()
        lasts.append(send(80 + p, att.at[far, rows], att.at[far, rows], other_core))

    attend(0)
    hand_out(0)
    u_blocks.arrive()
    u_blocks.ring()
    attend(1)
    hand_out(1)
    hand_on(0)
    e_blocks.ring_forward()
    attend(2)
    hand_out(2)
    hand_on(1)
    hand_over(0)
    u_blocks.ring_forward()
    attend(3)
    hand_out(3)
    hand_on(2)
    hand_over(1)
    hand_on(3)
    load_here.wait()
    e_blocks.ring_end()
    u_blocks.ring_end()
    hand_over(2)
    hand_over(3)
    def out_project(p):
        rows = pl.ds(p * SEQ, SEQ)

        def out_cols(i, c):
            cols = pl.ds(pl.multiple_of(i * 512, 512), 512)
            total = None
            for m in range(NMP):
                term = jnp.dot(
                    att[m, rows, :], e_ref[m, :, cols], preferred_element_type=f32
                ).astype(bf16).astype(f32)
                total = term if total is None else total + term
            enc_out[rows, cols] = (tok_here[rows, cols].astype(f32) + total).astype(bf16)
            return c

        lax.fori_loop(0, 2, out_cols, 0)

    def cross_scores(p):
        enc = enc_out[pl.ds(p * SEQ, SEQ), :]
        wide_enc = enc.astype(f32)
        squares = jnp.sum(wide_enc * wide_enc, axis=1, keepdims=True)
        squares = jnp.broadcast_to(squares, (SEQ, 128)).T[:8]
        for m in range(NMP):
            both = lax.dot_general(
                u_ref[m], enc, (((1,), (1,)), ((), ())),
                preferred_element_type=f32,
            )
            both = both[:64] + both[64:]
            picked = jnp.zeros((16, SEQ), f32)
            for c in range(CLAIMS):
                picked = jnp.where(claims[p] == c, both[c * 16 : (c + 1) * 16], picked)
            sc_src[m, p, pl.ds(0, 16), :] = picked
            sc_src[m, p, pl.ds(16, 8), :] = squares
        out = []
        for k in range(1, 4):
            to = lax.rem(mp + k, NMP)
            out.append(
                send(84 + p * 3 + k - 1, sc_src.at[to, p], sc_in.at[mp, p], mp_dev(k))
            )
        sc_in[mp, p] = sc_src[mp, p]
        return out

    scs = []
    for p in range(4):
        cores[p].wait_recv()
        lasts[p].wait_recv()
        out_project(p)
        scs.append(cross_scores(p))

    crosses, inverses, maxima = [], [], []
    for p in range(4):
        for copy in scs[p]:
            copy.wait_recv()
        raw = sc_in[0, p] + sc_in[1, p] + sc_in[2, p] + sc_in[3, p]
        inverse = lax.rsqrt(raw[16:17] / D + EPSILON)
        cross = raw[:16] * inverse + extra[p]
        crosses.append(cross)
        inverses.append(inverse)
        maxima.append(jnp.broadcast_to(jnp.max(cross, axis=1, keepdims=True), (16, SEQ)))
    claim_max = []
    for c in range(CLAIMS):
        top = jnp.full((16, SEQ), MASKED, f32)
        for p in range(4):
            top = jnp.maximum(top, jnp.where(claims[p] == c, maxima[p], MASKED))
        claim_max.append(top)
    sums = []
    for p in range(4):
        chosen = claim_max[0]
        for c in range(1, CLAIMS):
            chosen = jnp.where(claims[p] == c, claim_max[c], chosen)
        wts = jnp.exp(crosses[p] - chosen)
        sums.append(jnp.broadcast_to(jnp.sum(wts, axis=1, keepdims=True), (16, SEQ)))
        all_w[mp, p] = (wts * inverses[p]).astype(bf16)
    totals = []
    for c in range(CLAIMS):
        total = jnp.zeros((16, SEQ), f32)
        for p in range(4):
            total = total + jnp.where(claims[p] == c, sums[p], 0.0)
        totals.append(total)
    first_row = lax.broadcasted_iota(jnp.int32, (8, 128), 0) == 0

    def lanes_of(parts, fill):
        column = jnp.concatenate([part[:, :128] for part in parts], axis=0)
        column = jnp.concatenate([column, jnp.full((64, 128), fill, f32)], axis=0)
        return column.T[:8]

    all_st[mp] = jnp.where(first_row, lanes_of(claim_max, MASKED), lanes_of(totals, 0.0))
    ws = [send(96 + k, all_w.at[mp], all_w.at[mp], mp_dev(k)) for k in range(3 + 1) if k]
    sts = [send(99 + k, all_st.at[mp], all_st.at[mp], mp_dev(k)) for k in range(3 + 1) if k]
    for copy in ws + sts:
        copy.wait_recv()

    for p in range(4):
        for m in range(NMP):
            w_mp = all_w[m, p].astype(f32)
            for c in range(CLAIMS):
                lhs[p, pl.ds(m * 64 + c * 16, 16), :] = jnp.where(
                    claims[p] == c, w_mp, 0.0
                ).astype(bf16)
    for i in range(2):
        total = None
        for p in range(4):
            term = jnp.dot(
                lhs[p], enc_out[pl.ds(p * SEQ, SEQ), pl.ds(i * 512, 512)],
                preferred_element_type=f32,
            )
            total = term if total is None else total + term
        for zt in range(4):
            y_src[zt, i] = total[:, zt * 128 : (zt + 1) * 128].astype(bf16)
    y_copies, st_copies = [], []
    for k in range(1, 4):
        tz = lax.rem(z + k, 4)
        y_copies.append(send(103 + k, y_src.at[tz], y_zin.at[z], dev("z", k)))
        st_copies.append(send(106 + k, all_st, st_z.at[z], dev("z", k)))
    y_zin[z] = y_src[z]
    st_z[z] = all_st[...]

    def merge(stats, rows):
        top = stats[0][0:1]
        for st in stats[1:]:
            top = jnp.maximum(top, st[0:1])
        total = jnp.zeros((1, 128), f32)
        results = [jnp.zeros((64, 128), f32) for _ in rows[0]]
        for st, these in zip(stats, rows):
            scale = jnp.exp(st[0:1] - top)
            total = total + scale * st[1:2]
            column = jnp.broadcast_to(scale, (128, 128)).T[:64]
            results = [r + column * t.astype(f32) for r, t in zip(results, these)]
        both = jnp.where(
            first_row, jnp.broadcast_to(top, (8, 128)), jnp.broadcast_to(total, (8, 128))
        )
        return both, results

    for copy in y_copies + st_copies:
        copy.wait_recv()
    for m in range(NMP):
        part = pl.ds(m * 64, 64)
        both, results = merge(
            [st_z[j, m] for j in range(4)],
            [[y_zin[j, i, part, :] for i in range(2)] for j in range(4)],
        )
        st_one[m] = both
        for i in range(2):
            y_one[i, m] = results[i].astype(bf16)
    def to_owner(k):
        to_yl, m = lax.rem(yl + k // 4, 2), lax.rem(mp + k % 4, NMP)
        target = (psg_of(mp, to_yl, z), m)
        slot = x * 2 + yl
        return (
            remote(
                y_one.at[to_yl, m], y_in.at[slot], send_sem.at[230 + k], recv_sem.at[230 + slot], target
            ),
            remote(
                st_one.at[m], st_in.at[slot], send_sem.at[238 + k], recv_sem.at[238 + slot], target
            ),
        )

    def from_source(k):
        frm, frm_yl = lax.rem(x + k, 4), lax.rem(yl + k // 4, 2)
        target = (psg_of(frm, frm_yl, z), x)
        slot = frm * 2 + frm_yl
        return (
            remote(
                y_one.at[0, 0], y_in.at[slot], send_sem.at[230], recv_sem.at[230 + slot], target
            ),
            remote(st_one.at[0], st_in.at[slot], send_sem.at[238], recv_sem.at[238 + slot], target),
        )

    @pl.when(mine)
    def _():
        y_in[x * 2 + yl] = y_one[yl, mp]
        st_in[x * 2 + yl] = st_one[mp]

    @pl.when(jnp.logical_not(mine))
    def _():
        for copy in to_owner(0):
            copy.start()

    for k in range(1, 8):
        for copy in to_owner(k):
            copy.start()

    @pl.when(jnp.logical_not(mine))
    def _():
        for copy in from_source(0):
            copy.wait_recv()

    for k in range(1, 8):
        for copy in from_source(k):
            copy.wait_recv()
    both, results = merge([st_in[j] for j in range(8)], [[y_in[j]] for j in range(8)])
    total = jnp.broadcast_to(both[1:2], (128, 128)).T[:64]
    mean_rows = results[0] / total
    mean_rows = mean_rows * final_gain[:, pl.ds(pl.multiple_of(psg * 128, 128), 128)]

    products = dot3(mean_rows, cross_keyval[1])
    products = jnp.where(head_of_row == head_of_lane, products, 0.0)
    x_buf2[x] = jnp.sum(products.reshape(8, 8, 512), axis=1)
    xs = [send(120 + k, x_buf2.at[x], x_buf2.at[x], dev("x", k)) for k in range(1, 4)]
    for copy in xs:
        copy.wait_recv()
    yz_buf2[yz] = x_buf2[0] + x_buf2[1] + x_buf2[2] + x_buf2[3]
    yzs = [send(124 + k, yz_buf2.at[yz], yz_buf2.at[yz], yz_dev(k)) for k in range(1, 8)]
    for copy in yzs:
        copy.wait_recv()
    cross_attn = yz_buf2[0]
    for k in range(1, 8):
        cross_attn = cross_attn + yz_buf2[k]
    mp_buf2[mp] = dot3(cross_attn, cross_output[...])
    lasts = [send(132 + k, mp_buf2.at[mp], mp_buf2.at[mp], mp_dev(k)) for k in range(1, 4)]
    for copy in lasts:
        copy.wait_recv()
    final = (mp_buf2[0] + mp_buf2[1] + mp_buf2[2] + mp_buf2[3]) + (
        mp_buf[0] + mp_buf[1] + mp_buf[2] + mp_buf[3]
    )
    share = final[:, :32]
    for m in range(1, NMP):
        share = jnp.where(mp == m, final[:, m * 32 : (m + 1) * 32], share)
    dec_out[...] = share.astype(bf16)

    for copy in sent:
        copy.wait_send()
    for k in range(1, 8):
        for copy in to_owner(k):
            copy.wait_send()

    @pl.when(jnp.logical_not(mine))
    def _():
        for copy in to_owner(0):
            copy.wait_send()

    e_blocks.finish()
    u_blocks.finish()


def encoder(args):
    tok_rows = args[0].shape[0]
    bf16 = jnp.bfloat16
    f32 = jnp.float32
    return pl.pallas_call(
        encoder_kernel,
        out_shape=(
            jax.ShapeDtypeStruct((tok_rows, 1024), bf16),
            jax.ShapeDtypeStruct((CLAIMS * POS, 32), bf16),
        ),
        in_specs=[ANY, VMEM, ANY, VMEM, VMEM, VMEM, ANY] + [VMEM] * 8,
        out_specs=(VMEM, VMEM),
        scratch_shapes=[
            pltpu.VMEM((3, 4, 4, 256, 512), bf16),
            pltpu.VMEM((tok_rows, D), bf16),
            pltpu.VMEM((2, tok_rows, 512), jnp.float32),
            pltpu.VMEM((3, tok_rows, 512), bf16),
            pltpu.VMEM((NMP, 512, 1024), bf16),
            pltpu.VMEM((NMP, 128, 1024), bf16),
            pltpu.VMEM((NMP, tok_rows, 512), bf16),
            pltpu.VMEM((4, SEQ, 512), bf16),
            pltpu.VMEM((8, SEQ, SEQ), jnp.float32),
            pltpu.VMEM((tok_rows, 1024), bf16),
            pltpu.VMEM((128, 128), bf16),
            pltpu.VMEM((NMP, 8, 128), jnp.float32),
            pltpu.VMEM((4, 8, 640), jnp.float32),
            pltpu.VMEM((8, 8, 640), f32),
            pltpu.VMEM((NMP, 4, 24, SEQ), f32),
            pltpu.VMEM((NMP, 4, 24, SEQ), f32),
            pltpu.VMEM((NMP, 4, 16, SEQ), bf16),
            pltpu.VMEM((NMP, 8, 128), f32),
            pltpu.VMEM((4, 256, SEQ), bf16),
            pltpu.VMEM((4, 2, 256, 128), bf16),
            pltpu.VMEM((4, 2, 256, 128), bf16),
            pltpu.VMEM((4, NMP, 8, 128), f32),
            pltpu.VMEM((2, NMP, 64, 128), bf16),
            pltpu.VMEM((NMP, 8, 128), f32),
            pltpu.VMEM((8, 64, 128), bf16),
            pltpu.VMEM((8, 8, 128), f32),
            pltpu.VMEM((4, 8, 512), f32),
            pltpu.VMEM((8, 8, 512), f32),
            pltpu.VMEM((NMP, 8, 128), f32),
            pltpu.SemaphoreType.DMA((246,)),
            pltpu.SemaphoreType.DMA((246,)),
            pltpu.SemaphoreType.DMA((5,)),
        ],
        compiler_params=pltpu.CompilerParams(
            collective_id=1, has_side_effects=True, vmem_limit_bytes=58 << 20
        ),
    )(*args)


def shards(
    tokens,
    lengths,
    assignment,
    retrieval,
    enc_gain,
    enc_qkv,
    position_bias,
    enc_output,
    final_gain,
    embedding,
    dec_tokens,
    dec_gain,
    cross_query,
    cross_keyval,
    cross_output,
):
    found, mask_add, claims, extra = lookup(
        dec_tokens.T, lengths, assignment, retrieval, embedding
    )
    onehot = bucket_onehot(SEQ, BUCKETS, MAXDIST)
    onehot = np.concatenate([onehot[:, 255:], np.zeros((BUCKETS, 1)), onehot[:, :255]], axis=1)
    encoded, decoded = encoder(
        (
            tokens,
            enc_gain.reshape(1, D),
            enc_qkv,
            position_bias,
            jnp.asarray(onehot, jnp.bfloat16),
            mask_add,
            enc_output,
            final_gain.reshape(1, D),
            found,
            dec_gain.reshape(1, 128),
            cross_query,
            cross_keyval,
            cross_output,
            claims,
            extra,
        )
    )
    return (encoded, decoded.reshape(CLAIMS, POS, 32))


def solution(mesh):
    in_specs = (
        P("psg", None),
        P("psg"),
        P("psg"),
        P("psg"),
        P(),
        P(None, "psg", "mp"),
        P("mp", None),
        P("mp", "psg"),
        P(),
        P("mp", "psg"),
        P(),
        P("psg"),
        P("psg", "mp"),
        P(None, "psg", "mp"),
        P("mp", "psg"),
    )
    out_specs = (P("psg", "mp"), P(None, None, ("psg", "mp")))
    return jax.shard_map(shards, mesh=mesh, in_specs=in_specs, out_specs=out_specs, check_vma=False)
```

```python
import functools
import math

import jax
import jax.numpy as jnp
import numpy as np
from jax import lax
from jax.experimental import pallas as pl
from jax.experimental.pallas import tpu as pltpu
from jax.sharding import PartitionSpec as P

D = 4096
HEAD_DIM = 64
BUCKETS = 32
MAXDIST = 128
SEQ = 256
CLAIMS = 4
POS = 2
NPSG = 32
NMP = 4
EPSILON = 1e-06
MASKED = -1e30
MESH = pl.DeviceIdType.MESH
ANY = pl.BlockSpec(memory_space=pl.ANY)
VMEM = pl.BlockSpec(memory_space=pltpu.VMEM)


def bucket_onehot(length, buckets, max_distance):
    halfway = buckets // 2
    exact_max = halfway // 2
    relative_list = list(range(-(length - 1), length))
    beyond_list = [
        min(
            halfway - 1,
            exact_max
            + math.floor(
                math.log(max(abs(shift), 1) / exact_max)
                / math.log(max_distance / exact_max)
                * (halfway - exact_max)
            ),
        )
        for shift in relative_list
    ]
    relative = np.array(relative_list)
    beyond = np.array(beyond_list)
    distance = np.abs(relative)
    bucket_ids = np.where(relative > 0, halfway, 0) + np.where(
        distance < exact_max, distance, beyond
    )
    return (bucket_ids[None, :] == np.arange(buckets)[:, None]).astype(np.float32)


def place():
    psg = lax.axis_index("psg")
    mp = lax.axis_index("mp")
    return psg // 8, (psg // 4) % 2, psg % 4, mp // 2, mp % 2


def psg_of(x, yl, z):
    return x * 8 + yl * 4 + z


def remote(src, dst, send_sem, recv_sem, device):
    return pltpu.make_async_remote_copy(
        src_ref=src,
        dst_ref=dst,
        send_sem=send_sem,
        recv_sem=recv_sem,
        device_id=device,
        device_id_type=MESH,
    )


def signal(device):
    pl.semaphore_signal(
        pltpu.get_barrier_semaphore(), inc=1, device_id=device, device_id_type=MESH
    )


def lookup_kernel(ids, lengths, assignment, retrieval, table, out, mask_add, claims, extra, rows, sems):
    copies = []
    held = []
    base = lax.axis_index("mp") * table.shape[0]
    for i in range(CLAIMS * POS):
        local = ids[i % POS, i // POS] - base
        inside = jnp.logical_and(local >= 0, local < table.shape[0])
        local = jnp.clip(local, 0, table.shape[0] - 1)
        start = pl.multiple_of((local // 16) * 16, 16)
        held.append(jnp.where(inside, local - start, -1))
        copies.append(
            pltpu.make_async_copy(table.at[pl.ds(start, 16), :], rows.at[i], sems.at[i])
        )
        copies[-1].start()
    slot = lax.broadcasted_iota(jnp.int32, (16, SEQ), 1)
    for p in range(4):
        add = jnp.where(slot < lengths[p], 0.0, MASKED)
        mask_add[p] = add[:8]
        extra[p] = add + retrieval[p]
        claims[p] = jnp.zeros((16, SEQ), jnp.int32) + assignment[p]
    at = lax.broadcasted_iota(jnp.int32, (16, 128), 0)
    for i in range(CLAIMS * POS):
        copies[i].wait()
        picked = jnp.where(at == held[i], rows[i].astype(jnp.float32), 0.0)
        out[pl.ds(i, 1), :] = jnp.sum(picked, axis=0, keepdims=True)


def lookup(ids, lengths, assignment, retrieval, table):
    smem = pl.BlockSpec(memory_space=pltpu.SMEM)
    f32 = jnp.float32
    return pl.pallas_call(
        lookup_kernel,
        out_shape=(
            jax.ShapeDtypeStruct((CLAIMS * POS, 128), f32),
            jax.ShapeDtypeStruct((4, 8, SEQ), f32),
            jax.ShapeDtypeStruct((4, 16, SEQ), jnp.int32),
            jax.ShapeDtypeStruct((4, 16, SEQ), f32),
        ),
        in_specs=[smem] * 4 + [ANY],
        out_specs=(VMEM,) * 4,
        scratch_shapes=[
            pltpu.VMEM((CLAIMS * POS, 16, 128), jnp.bfloat16),
            pltpu.SemaphoreType.DMA((CLAIMS * POS,)),
        ],
    )(ids, lengths, assignment, retrieval, table)


def split3(values):
    high = values.astype(jnp.bfloat16)
    rest = values - high.astype(jnp.float32)
    middle = rest.astype(jnp.bfloat16)
    low = (rest - middle.astype(jnp.float32)).astype(jnp.bfloat16)
    return jnp.concatenate([high, middle, low], axis=0)


def dot3(values, weights, contract=0):
    n = values.shape[0]
    parts = lax.dot_general(
        split3(values),
        weights,
        (((1,), (contract,)), ((), ())),
        preferred_element_type=jnp.float32,
    )
    return parts[:n] + parts[n : 2 * n] + parts[2 * n :]


ALL = slice(None)


def encoder_kernel(
    tokens,
    enc_gain,
    w_ref,
    bias_in,
    onehot,
    mask_add,
    enc_output,
    final_gain,
    found,
    dec_gain,
    cross_query,
    cross_keyval,
    cross_output,
    claims,
    extra,
    enc_hbm,
    dec_out,
    enc_out,
    g_ref,
    normed,
    acc,
    qkv,
    e_ref,
    u_ref,
    att,
    transit,
    bias,
    tok_here,
    block,
    mp_buf,
    x_buf,
    yz_buf,
    sc_src,
    sc_in,
    all_w,
    all_st,
    lhs,
    y_src,
    y_zin,
    st_z,
    y_one,
    st_one,
    y_in,
    st_in,
    x_buf2,
    yz_buf2,
    mp_buf2,
    send_sem,
    recv_sem,
    own_sem,
):
    f32 = jnp.float32
    bf16 = jnp.bfloat16
    x, yl, z, yh, core = place()
    psg = lax.axis_index("psg")
    mp = lax.axis_index("mp")
    y = yh * 2 + yl
    y_dev = (psg_of(x, 1 - yl, z), mp)

    def dev(axis, step):
        if axis == "x":
            return (psg_of(lax.rem(x + step, 4), yl, z), mp)
        return (psg_of(x, yl, lax.rem(z + step, 4)), mp)

    def yz_dev(k):
        t = lax.rem(yl * 4 + z + k, 8)
        return (x * 8 + t, mp)

    def mp_dev(k):
        return (psg, lax.rem(mp + k, NMP))

    def y_step(step):
        t = lax.rem(y + step, 4)
        return (psg_of(x, lax.rem(t, 2), z), (t // 2) * 2 + core)

    other_core = (psg, yh * 2 + 1 - core)
    same_half = (x // 2) == yh
    yl_to = jnp.where(same_half, yl, 1 - yl)

    block_to = (psg_of(x, yl_to, z), x)
    mine = x == mp

    load_tokens = pltpu.make_async_copy(tokens, normed, own_sem.at[0])
    load_tokens.start()
    own = pltpu.make_async_copy(
        w_ref, g_ref.at[:, x, z, pl.ds(pl.multiple_of(yl * 128, 128), 128), :], own_sem.at[1]
    )
    own.start()
    load_here = pltpu.make_async_copy(
        tokens.at[:, pl.ds(pl.multiple_of(mp * 1024, 128), 1024)], tok_here, own_sem.at[2]
    )
    load_here.start()
    for k in range(1, 4):
        signal(dev("x", k))
        signal(mp_dev(k))
    for k in range(1, 8):
        signal(yz_dev(k))
    signal(y_step(1))
    signal(y_step(3))

    @pl.when(mine)
    def _():
        for k in range(1, 4):
            m = lax.rem(mp + k, NMP)
            signal((psg_of(x, jnp.where((m // 2) == yh, yl, 1 - yl), z), m))

    for k in range(8):
        frm = psg_of(lax.rem(x + k, 4), lax.rem(yl + k // 4, 2), z)
        if k == 0:
            pl.when(jnp.logical_not(mine))(functools.partial(signal, (frm, x)))
        else:
            signal((frm, x))

    def g(k, xs, zs, yls, cols=None):
        rows = ALL if yls is None else pl.ds(pl.multiple_of(yls * 128, 128), 128)
        c = ALL if cols is None else pl.ds(cols[0], cols[1])
        return g_ref.at[k, xs, zs, rows, c]

    def wide(c):
        return None if c is None else (c * 256, 256)

    def low_cols(c):
        return (0, 256) if c is None else (c * 128, 128)

    def high_cols(c):
        return (256, 256) if c is None else (256 + c * 128, 128)

    sent = []

    def send(t, src, dst, device):
        copy = remote(src, dst, send_sem.at[t], recv_sem.at[t], device)
        copy.start()
        sent.append(copy)
        return copy

    class Ring:
        def __init__(self, t, axis, piece, first=None):
            self.t, self.axis, self.piece = t, axis, piece
            self.at = x if axis == "x" else z
            src = piece(self.at) if first is None else first
            self.up = send(t, src, piece(self.at), dev(axis, 1))
            self.down = send(t + 1, src, piece(self.at), dev(axis, 3))

        def forward(self, then=None):
            below = lax.rem(self.at + 3, 4)
            above = lax.rem(self.at + 1, 4)
            self.up.wait_recv()
            up = self.piece(below, 0)
            self.f_up = send(self.t + 2, up, up, dev(self.axis, 1))
            if then is not None:
                then(1, below)
            self.down.wait_recv()
            down = self.piece(above, 1)
            self.f_down = send(self.t + 3, down, down, dev(self.axis, 3))
            if then is not None:
                then(2, above)

        def end(self, then=None):
            self.f_up.wait_recv()
            self.f_down.wait_recv()
            if then is not None:
                then(3, lax.rem(self.at + 2, 4))

    go_step = jnp.where(core == 1, 1, 3)
    go_on = lax.rem(mp + go_step, 4) == x
    near = pl.ds(yh * 2, 2)
    far_half = pl.ds(2 - yh * 2, 2)

    class Blocks:
        def __init__(self, t, src, ref, own_t):
            self.t, self.ref, self.src = t, ref, src
            first = self.at(mp, yl, z)
            self.block = remote(src, first, send_sem.at[t], recv_sem.at[t + 1 + mp], block_to)
            self.keep = pltpu.make_async_copy(src, first, own_sem.at[own_t])
            n, f = self.at(near, yl, z), self.at(far_half, 1 - yl, z)
            self.ys = [
                remote(n, n, send_sem.at[t + 5], recv_sem.at[t + 5], y_dev),
                remote(f, f, send_sem.at[t + 6], recv_sem.at[t + 6], y_dev),
            ]

        def at(self, ms, yls, zs):
            col = pl.multiple_of((yls * 4 + zs) * 128, 128)
            return self.ref.at[ms, :, pl.ds(col, 128)]

        def x_copy(self, c, step, t):
            part = self.at(ALL, c, z)
            return remote(
                part, part, send_sem.at[self.t + t], recv_sem.at[self.t + 13 + c], dev("x", step)
            )

        def start(self):
            pl.when(mine)(self.keep.start)
            pl.when(jnp.logical_not(mine))(self.block.start)

        def across(self):
            @pl.when(mine)
            def _():
                for k in range(1, 4):
                    m = lax.rem(mp + k, NMP)
                    remote(
                        self.src,
                        self.at(m, yl, z),
                        send_sem.at[self.t],
                        recv_sem.at[self.t + 1 + m],
                        y_dev,
                    ).wait_recv()
                self.keep.wait()
                for copy in self.ys:
                    copy.start()

        def along(self):
            @pl.when(mine)
            def _():
                for copy in self.ys:
                    copy.wait_recv()
                for c in range(2):
                    self.x_copy(c, 1, 7 + c).start()
                    self.x_copy(c, 3, 9 + c).start()

        def forward(self):
            @pl.when(go_on)
            def _():
                for c in range(2):
                    self.x_copy(c, 1, 7 + c).wait_recv()
                    self.x_copy(c, go_step, 11 + c).start()

        def arrive(self):
            @pl.when(jnp.logical_not(jnp.logical_or(mine, go_on)))
            def _():
                for c in range(2):
                    self.x_copy(c, 1, 7 + c).wait_recv()

        def ring(self):
            t = self.t
            parts = [self.at(ALL, i, z) for i in range(2)]
            self.up = [send(t + 15 + i, parts[i], parts[i], dev("z", 1)) for i in range(2)]
            self.down = [send(t + 17 + i, parts[i], parts[i], dev("z", 3)) for i in (1, 0)]

        def ring_forward(self):
            self.up[0].wait_recv()
            part = self.at(ALL, 0, lax.rem(z + 3, 4))
            self.f_up = send(self.t + 19, part, part, dev("z", 1))
            self.down[0].wait_recv()
            part = self.at(ALL, 1, lax.rem(z + 1, 4))
            self.f_down = send(self.t + 20, part, part, dev("z", 3))

        def ring_end(self):
            for copy in (self.up[1], self.down[1], self.f_up, self.f_down):
                copy.wait_recv()

        def finish(self):
            @pl.when(mine)
            def _():
                for copy in self.ys:
                    copy.wait_send()
                for c in range(2):
                    self.x_copy(c, 1, 7 + c).wait_send()
                    self.x_copy(c, 3, 9 + c).wait_send()

            pl.when(jnp.logical_not(mine))(self.block.wait_send)

            @pl.when(go_on)
            def _():
                for c in range(2):
                    self.x_copy(c, go_step, 11 + c).wait_send()

    e_blocks = Blocks(188, enc_output, e_ref, 3)
    u_blocks = Blocks(209, block, u_ref, 4)

    pl.semaphore_wait(pltpu.get_barrier_semaphore(), jnp.where(mine, 22, 24))

    yd = send(0, w_ref.at[0], g(0, x, z, yl), y_dev)
    ye = send(1, w_ref.at[1], g(1, x, z, yl), y_dev)
    a1 = Ring(
        4, "x", lambda v, c=None: g(2, v, z, yl, low_cols(c)), w_ref.at[2, :, pl.ds(0, 256)]
    )
    b1 = Ring(
        8, "z", lambda v, c=None: g(2, x, v, yl, high_cols(c)), w_ref.at[2, :, pl.ds(256, 256)]
    )
    mp_buf[mp] = found[...]
    mps = [send(52 + k, found, mp_buf.at[mp], mp_dev(k)) for k in range(1, 4)]
    e_blocks.start()
    own.wait()

    d3, e3, yas, ybs = [None] * 4, [None] * 4, [None] * 4, [None] * 4

    def start_d3(i, u):
        d3[i] = Ring(140 + 4 * i, "z", lambda v, c=None: g(0, u, v, None, wide(c)))

    def start_e3(i, u):
        e3[i] = Ring(156 + 4 * i, "x", lambda v, c=None: g(1, v, u, None, wide(c)))

    def start_ya(i, u):
        plane = g(2, ALL, u, yl, low_cols(None))
        yas[i] = send(172 + i, plane, plane, y_dev)

    def start_yb(i, u):
        plane = g(2, u, ALL, yl, high_cols(None))
        ybs[i] = send(176 + i, plane, plane, y_dev)

    a1.forward()
    b1.forward()
    yd.wait_recv()
    d2 = Ring(20, "x", lambda v, c=None: g(0, v, z, None, wide(c)))
    ye.wait_recv()
    e2 = Ring(24, "z", lambda v, c=None: g(1, x, v, None, wide(c)))
    start_d3(0, x)
    start_e3(0, z)
    a1.end()
    a2 = Ring(12, "z", lambda v, c=None: g(2, ALL, v, yl, low_cols(c)))
    start_ya(0, z)
    b1.end()
    b2 = Ring(16, "x", lambda v, c=None: g(2, v, ALL, yl, high_cols(c)))
    start_yb(0, x)
    e_blocks.across()

    for copy in mps:
        copy.wait_recv()
    emb = mp_buf[0] + mp_buf[1] + mp_buf[2] + mp_buf[3]
    terms = dot3(emb * dec_gain[...], cross_query[...])
    squares = jnp.sum(emb * emb, axis=1, keepdims=True)
    x_buf[x, :, pl.ds(0, 512)] = terms
    x_buf[x, :, pl.ds(512, 128)] = jnp.broadcast_to(squares, (8, 128))
    xs = [send(56 + k, x_buf.at[x], x_buf.at[x], dev("x", k)) for k in range(1, 4)]

    e_blocks.along()
    load_tokens.wait()

    def norm_rows(first, count):
        def body(i, c):
            rows = pl.ds(pl.multiple_of(i * 16, 16), 16)
            values = normed[rows, :].astype(f32)
            mean = jnp.sum(values * values, axis=1, keepdims=True) / D
            inverse = lax.rsqrt(mean + EPSILON)
            scaled = (values * inverse * enc_gain[...]).astype(bf16)
            for p in range(NPSG):
                to = ((p // 8) * 4 + p % 4) * 2 + (p // 4) % 2
                normed[rows, pl.ds(to * 128, 128)] = scaled[:, p * 128 : (p + 1) * 128]
            return c

        lax.fori_loop(first, first + count, body, 0)

    norm_rows(0, 8)
    d2.forward(start_d3)
    e2.forward(start_e3)

    norm_rows(8, 8)
    a2.forward(start_ya)
    b2.forward(start_yb)
    d2.end(start_d3)
    e2.end(start_e3)
    d3[0].forward()
    e3[0].forward()
    a2.end(start_ya)
    b2.end(start_yb)
    for copy in xs:
        copy.wait_recv()
    yz = yl * 4 + z
    yz_buf[yz] = x_buf[0] + x_buf[1] + x_buf[2] + x_buf[3]
    yzs = [send(60 + k, yz_buf.at[yz], yz_buf.at[yz], yz_dev(k)) for k in range(1, 8)]
    norm_rows(16, 16)
    d3[1].forward()
    e3[1].forward()
    e_blocks.forward()
    norm_rows(32, 16)
    d3[2].forward()
    e3[2].forward()

    for copy in yzs:
        copy.wait_recv()
    joined = yz_buf[0]
    for k in range(1, 8):
        joined = joined + yz_buf[k]
    cquery = joined[:, :512] * lax.rsqrt(joined[:, 512:513] / D + EPSILON)
    spread_q = jnp.broadcast_to(cquery[:, None, :], (8, 8, 512)).reshape(64, 512)
    head_of_row = lax.rem(lax.broadcasted_iota(jnp.int32, (64, 512), 0), 8)
    head_of_lane = lax.broadcasted_iota(jnp.int32, (64, 512), 1) // HEAD_DIM
    spread_q = jnp.where(head_of_row == head_of_lane, spread_q, 0.0)
    folded = dot3(spread_q, cross_keyval[0], 1)
    folded = folded * final_gain[:, pl.ds(pl.multiple_of(psg * 128, 128), 128)]
    high = folded.astype(bf16)
    block[pl.ds(0, 64), :] = high
    block[pl.ds(64, 64), :] = (folded - high.astype(f32)).astype(bf16)

    u_blocks.start()
    norm_rows(48, 16)
    d3[3].forward()
    e3[3].forward()
    e_blocks.arrive()
    e_blocks.ring()

    table = dot3(bias_in[...], onehot[...])
    for h in range(8):
        row = jnp.broadcast_to(table[h : h + 1], (SEQ, 512))
        bias[h] = pltpu.roll(row, 0, 1, stride=1, stride_axis=0)[:, :SEQ]

    def product(k, rows, xi, zi):
        at = pl.multiple_of((xi * 4 + zi) * 256, 256)
        return jnp.dot(
            normed[rows, pl.ds(at, 256)], g_ref[k, xi, zi], preferred_element_type=f32
        )

    def project(step):
        def body(i, c):
            step(pl.ds(pl.multiple_of(i * 256, 256), 256))
            return c

        lax.fori_loop(0, 4, body, 0)

    def first_q(rows):
        total = None
        for xi in range(4):
            for dz in (0, 1, 3):
                term = product(0, rows, xi, lax.rem(z + dz, 4))
                total = term if total is None else total + term
        acc[0, rows, :] = total

    def first_k(rows):
        total = None
        for zi in range(4):
            for dx in (0, 1, 3):
                term = product(1, rows, lax.rem(x + dx, 4), zi)
                total = term if total is None else total + term
        acc[1, rows, :] = total

    def all_v(rows):
        total = None
        for xi in range(4):
            for zi in range(4):
                term = product(2, rows, xi, zi)
                total = term if total is None else total + term
        qkv[2, rows, :] = total.astype(bf16)

    def last_q(rows):
        total = acc[0, rows, :]
        for xi in range(4):
            total = total + product(0, rows, xi, lax.rem(z + 2, 4))
        qkv[0, rows, :] = total.astype(bf16)

    def last_k(rows):
        total = acc[1, rows, :]
        for zi in range(4):
            total = total + product(1, rows, lax.rem(x + 2, 4), zi)
        qkv[1, rows, :] = total.astype(bf16)

    project(first_q)
    u_blocks.across()
    project(first_k)
    u_blocks.along()
    for copy in yas + ybs:
        copy.wait_recv()
    project(all_v)
    u_blocks.forward()
    for ring in d3:
        ring.end()
    project(last_q)
    for ring in e3:
        ring.end()
    project(last_k)

    lane = lax.broadcasted_iota(jnp.int32, (SEQ, 128), 1)

    def attend(p):
        rows = pl.ds(p * SEQ, SEQ)

        def body(j, c):
            lanes = pl.ds(pl.multiple_of(j * 128, 128), 128)
            q2 = qkv[0, rows, lanes]
            k2 = qkv[1, rows, lanes]
            v2 = qkv[2, rows, lanes]
            outs = []
            for t in range(2):
                qt = jnp.where((lane // HEAD_DIM) == t, q2, jnp.zeros_like(q2))
                s = lax.dot_general(
                    qt, k2, (((1,), (1,)), ((), ())), preferred_element_type=f32
                )
                s = s + bias[2 * j + t] + mask_add[p, pl.ds(0, 1), :]
                wts = jnp.exp(s - jnp.max(s, axis=1, keepdims=True))
                scale = 1.0 / jnp.sum(wts, axis=1, keepdims=True)
                outs.append(
                    jnp.dot((wts * scale).astype(bf16), v2, preferred_element_type=f32)
                )
            att[mp, rows, lanes] = jnp.where(lane < HEAD_DIM, outs[0], outs[1]).astype(bf16)
            return c

        lax.fori_loop(0, 4, body, 0)

    hops, ends, cores, lasts = [], [], [], []
    far = (1 - yh) * 2 + core

    def hand_out(p):
        rows = pl.ds(p * SEQ, SEQ)
        cores.append(send(68 + p, att.at[mp, rows], att.at[mp, rows], other_core))
        hops.append(
            send(72 + p, att.at[mp, rows], transit.at[p], y_step(1 if p % 2 == 0 else 3))
        )

    def hand_on(p):
        rows = pl.ds(p * SEQ, SEQ)
        hops[p].wait_recv()
        frm = lax.rem(y + (3 if p % 2 == 0 else 1), 4)
        slot = (frm // 2) * 2 + core
        ends.append(
            send(76 + p, transit.at[p], att.at[slot, rows], y_step(1 if p % 2 == 0 else 3))
        )

    def hand_over(p):
        rows = pl.ds(p * SEQ, SEQ)
        ends[p].wait_recv()
        lasts.append(send(80 + p, att.at[far, rows], att.at[far, rows], other_core))

    attend(0)
    hand_out(0)
    u_blocks.arrive()
    u_blocks.ring()
    attend(1)
    hand_out(1)
    hand_on(0)
    e_blocks.ring_forward()
    attend(2)
    hand_out(2)
    hand_on(1)
    hand_over(0)
    u_blocks.ring_forward()
    attend(3)
    hand_out(3)
    hand_on(2)
    hand_over(1)
    hand_on(3)
    load_here.wait()
    e_blocks.ring_end()
    u_blocks.ring_end()
    hand_over(2)
    hand_over(3)
    def out_project(p):
        rows = pl.ds(p * SEQ, SEQ)

        def out_cols(i, c):
            cols = pl.ds(pl.multiple_of(i * 512, 512), 512)
            total = None
            for m in range(NMP):
                term = jnp.dot(
                    att[m, rows, :], e_ref[m, :, cols], preferred_element_type=f32
                ).astype(bf16).astype(f32)
                total = term if total is None else total + term
            enc_out[rows, cols] = (tok_here[rows, cols].astype(f32) + total).astype(bf16)
            return c

        lax.fori_loop(0, 2, out_cols, 0)

    def cross_scores(p):
        enc = enc_out[pl.ds(p * SEQ, SEQ), :]
        wide_enc = enc.astype(f32)
        squares = jnp.sum(wide_enc * wide_enc, axis=1, keepdims=True)
        squares = jnp.broadcast_to(squares, (SEQ, 128)).T[:8]
        for m in range(NMP):
            both = lax.dot_general(
                u_ref[m], enc, (((1,), (1,)), ((), ())),
                preferred_element_type=f32,
            )
            both = both[:64] + both[64:]
            picked = jnp.zeros((16, SEQ), f32)
            for c in range(CLAIMS):
                picked = jnp.where(claims[p] == c, both[c * 16 : (c + 1) * 16], picked)
            sc_src[m, p, pl.ds(0, 16), :] = picked
            sc_src[m, p, pl.ds(16, 8), :] = squares
        out = []
        for k in range(1, 4):
            to = lax.rem(mp + k, NMP)
            out.append(
                send(84 + p * 3 + k - 1, sc_src.at[to, p], sc_in.at[mp, p], mp_dev(k))
            )
        sc_in[mp, p] = sc_src[mp, p]
        return out

    scs, leave = [], []
    for p in range(4):
        cores[p].wait_recv()
        lasts[p].wait_recv()
        out_project(p)
        scs.append(cross_scores(p))
        rows = pl.ds(p * SEQ, SEQ)
        leave.append(pltpu.make_async_copy(enc_out.at[rows], enc_hbm.at[rows], own_sem.at[5 + p]))
        leave[-1].start()

    crosses, inverses, maxima = [], [], []
    for p in range(4):
        for copy in scs[p]:
            copy.wait_recv()
        raw = sc_in[0, p] + sc_in[1, p] + sc_in[2, p] + sc_in[3, p]
        inverse = lax.rsqrt(raw[16:17] / D + EPSILON)
        cross = raw[:16] * inverse + extra[p]
        crosses.append(cross)
        inverses.append(inverse)
        maxima.append(jnp.broadcast_to(jnp.max(cross, axis=1, keepdims=True), (16, SEQ)))
    claim_max = []
    for c in range(CLAIMS):
        top = jnp.full((16, SEQ), MASKED, f32)
        for p in range(4):
            top = jnp.maximum(top, jnp.where(claims[p] == c, maxima[p], MASKED))
        claim_max.append(top)
    sums = []
    for p in range(4):
        chosen = claim_max[0]
        for c in range(1, CLAIMS):
            chosen = jnp.where(claims[p] == c, claim_max[c], chosen)
        wts = jnp.exp(crosses[p] - chosen)
        sums.append(jnp.broadcast_to(jnp.sum(wts, axis=1, keepdims=True), (16, SEQ)))
        all_w[mp, p] = (wts * inverses[p]).astype(bf16)
    totals = []
    for c in range(CLAIMS):
        total = jnp.zeros((16, SEQ), f32)
        for p in range(4):
            total = total + jnp.where(claims[p] == c, sums[p], 0.0)
        totals.append(total)
    first_row = lax.broadcasted_iota(jnp.int32, (8, 128), 0) == 0

    def lanes_of(parts, fill):
        column = jnp.concatenate([part[:, :128] for part in parts], axis=0)
        column = jnp.concatenate([column, jnp.full((64, 128), fill, f32)], axis=0)
        return column.T[:8]

    all_st[mp] = jnp.where(first_row, lanes_of(claim_max, MASKED), lanes_of(totals, 0.0))
    ws = [send(96 + k, all_w.at[mp], all_w.at[mp], mp_dev(k)) for k in range(3 + 1) if k]
    sts = [send(99 + k, all_st.at[mp], all_st.at[mp], mp_dev(k)) for k in range(3 + 1) if k]
    for copy in ws + sts:
        copy.wait_recv()

    for p in range(4):
        for m in range(NMP):
            w_mp = all_w[m, p].astype(f32)
            for c in range(CLAIMS):
                lhs[p, pl.ds(m * 64 + c * 16, 16), :] = jnp.where(
                    claims[p] == c, w_mp, 0.0
                ).astype(bf16)
    for i in range(2):
        total = None
        for p in range(4):
            term = jnp.dot(
                lhs[p], enc_out[pl.ds(p * SEQ, SEQ), pl.ds(i * 512, 512)],
                preferred_element_type=f32,
            )
            total = term if total is None else total + term
        for zt in range(4):
            y_src[zt, i] = total[:, zt * 128 : (zt + 1) * 128].astype(bf16)
    y_copies, st_copies = [], []
    for k in range(1, 4):
        tz = lax.rem(z + k, 4)
        y_copies.append(send(103 + k, y_src.at[tz], y_zin.at[z], dev("z", k)))
        st_copies.append(send(106 + k, all_st, st_z.at[z], dev("z", k)))
    y_zin[z] = y_src[z]
    st_z[z] = all_st[...]

    def merge(stats, rows):
        top = stats[0][0:1]
        for st in stats[1:]:
            top = jnp.maximum(top, st[0:1])
        total = jnp.zeros((1, 128), f32)
        results = [jnp.zeros((64, 128), f32) for _ in rows[0]]
        for st, these in zip(stats, rows):
            scale = jnp.exp(st[0:1] - top)
            total = total + scale * st[1:2]
            column = jnp.broadcast_to(scale, (128, 128)).T[:64]
            results = [r + column * t.astype(f32) for r, t in zip(results, these)]
        both = jnp.where(
            first_row, jnp.broadcast_to(top, (8, 128)), jnp.broadcast_to(total, (8, 128))
        )
        return both, results

    for copy in y_copies + st_copies:
        copy.wait_recv()
    for m in range(NMP):
        part = pl.ds(m * 64, 64)
        both, results = merge(
            [st_z[j, m] for j in range(4)],
            [[y_zin[j, i, part, :] for i in range(2)] for j in range(4)],
        )
        st_one[m] = both
        for i in range(2):
            y_one[i, m] = results[i].astype(bf16)
    def to_owner(k):
        to_yl, m = lax.rem(yl + k // 4, 2), lax.rem(mp + k % 4, NMP)
        target = (psg_of(mp, to_yl, z), m)
        slot = x * 2 + yl
        return (
            remote(
                y_one.at[to_yl, m], y_in.at[slot], send_sem.at[230 + k], recv_sem.at[230 + slot], target
            ),
            remote(
                st_one.at[m], st_in.at[slot], send_sem.at[238 + k], recv_sem.at[238 + slot], target
            ),
        )

    def from_source(k):
        frm, frm_yl = lax.rem(x + k, 4), lax.rem(yl + k // 4, 2)
        target = (psg_of(frm, frm_yl, z), x)
        slot = frm * 2 + frm_yl
        return (
            remote(
                y_one.at[0, 0], y_in.at[slot], send_sem.at[230], recv_sem.at[230 + slot], target
            ),
            remote(st_one.at[0], st_in.at[slot], send_sem.at[238], recv_sem.at[238 + slot], target),
        )

    @pl.when(mine)
    def _():
        y_in[x * 2 + yl] = y_one[yl, mp]
        st_in[x * 2 + yl] = st_one[mp]

    @pl.when(jnp.logical_not(mine))
    def _():
        for copy in to_owner(0):
            copy.start()

    for k in range(1, 8):
        for copy in to_owner(k):
            copy.start()

    @pl.when(jnp.logical_not(mine))
    def _():
        for copy in from_source(0):
            copy.wait_recv()

    for k in range(1, 8):
        for copy in from_source(k):
            copy.wait_recv()
    both, results = merge([st_in[j] for j in range(8)], [[y_in[j]] for j in range(8)])
    total = jnp.broadcast_to(both[1:2], (128, 128)).T[:64]
    mean_rows = results[0] / total
    mean_rows = mean_rows * final_gain[:, pl.ds(pl.multiple_of(psg * 128, 128), 128)]

    products = dot3(mean_rows, cross_keyval[1])
    products = jnp.where(head_of_row == head_of_lane, products, 0.0)
    x_buf2[x] = jnp.sum(products.reshape(8, 8, 512), axis=1)
    xs = [send(120 + k, x_buf2.at[x], x_buf2.at[x], dev("x", k)) for k in range(1, 4)]
    for copy in xs:
        copy.wait_recv()
    yz_buf2[yz] = x_buf2[0] + x_buf2[1] + x_buf2[2] + x_buf2[3]
    yzs = [send(124 + k, yz_buf2.at[yz], yz_buf2.at[yz], yz_dev(k)) for k in range(1, 8)]
    for copy in yzs:
        copy.wait_recv()
    cross_attn = yz_buf2[0]
    for k in range(1, 8):
        cross_attn = cross_attn + yz_buf2[k]
    mp_buf2[mp] = dot3(cross_attn, cross_output[...])
    lasts = [send(132 + k, mp_buf2.at[mp], mp_buf2.at[mp], mp_dev(k)) for k in range(1, 4)]
    for copy in lasts:
        copy.wait_recv()
    final = (mp_buf2[0] + mp_buf2[1] + mp_buf2[2] + mp_buf2[3]) + (
        mp_buf[0] + mp_buf[1] + mp_buf[2] + mp_buf[3]
    )
    share = final[:, :32]
    for m in range(1, NMP):
        share = jnp.where(mp == m, final[:, m * 32 : (m + 1) * 32], share)
    dec_out[...] = share.astype(bf16)

    for copy in sent:
        copy.wait_send()
    for copy in leave:
        copy.wait()
    for k in range(1, 8):
        for copy in to_owner(k):
            copy.wait_send()

    @pl.when(jnp.logical_not(mine))
    def _():
        for copy in to_owner(0):
            copy.wait_send()

    e_blocks.finish()
    u_blocks.finish()


def encoder(args):
    tok_rows = args[0].shape[0]
    bf16 = jnp.bfloat16
    f32 = jnp.float32
    return pl.pallas_call(
        encoder_kernel,
        out_shape=(
            jax.ShapeDtypeStruct((tok_rows, 1024), bf16),
            jax.ShapeDtypeStruct((CLAIMS * POS, 32), bf16),
        ),
        in_specs=[ANY, VMEM, ANY, VMEM, VMEM, VMEM, ANY] + [VMEM] * 8,
        out_specs=(ANY, VMEM),
        scratch_shapes=[
            pltpu.VMEM((tok_rows, 1024), bf16),
            pltpu.VMEM((3, 4, 4, 256, 512), bf16),
            pltpu.VMEM((tok_rows, D), bf16),
            pltpu.VMEM((2, tok_rows, 512), jnp.float32),
            pltpu.VMEM((3, tok_rows, 512), bf16),
            pltpu.VMEM((NMP, 512, 1024), bf16),
            pltpu.VMEM((NMP, 128, 1024), bf16),
            pltpu.VMEM((NMP, tok_rows, 512), bf16),
            pltpu.VMEM((4, SEQ, 512), bf16),
            pltpu.VMEM((8, SEQ, SEQ), jnp.float32),
            pltpu.VMEM((tok_rows, 1024), bf16),
            pltpu.VMEM((128, 128), bf16),
            pltpu.VMEM((NMP, 8, 128), jnp.float32),
            pltpu.VMEM((4, 8, 640), jnp.float32),
            pltpu.VMEM((8, 8, 640), f32),
            pltpu.VMEM((NMP, 4, 24, SEQ), f32),
            pltpu.VMEM((NMP, 4, 24, SEQ), f32),
            pltpu.VMEM((NMP, 4, 16, SEQ), bf16),
            pltpu.VMEM((NMP, 8, 128), f32),
            pltpu.VMEM((4, 256, SEQ), bf16),
            pltpu.VMEM((4, 2, 256, 128), bf16),
            pltpu.VMEM((4, 2, 256, 128), bf16),
            pltpu.VMEM((4, NMP, 8, 128), f32),
            pltpu.VMEM((2, NMP, 64, 128), bf16),
            pltpu.VMEM((NMP, 8, 128), f32),
            pltpu.VMEM((8, 64, 128), bf16),
            pltpu.VMEM((8, 8, 128), f32),
            pltpu.VMEM((4, 8, 512), f32),
            pltpu.VMEM((8, 8, 512), f32),
            pltpu.VMEM((NMP, 8, 128), f32),
            pltpu.SemaphoreType.DMA((246,)),
            pltpu.SemaphoreType.DMA((246,)),
            pltpu.SemaphoreType.DMA((9,)),
        ],
        compiler_params=pltpu.CompilerParams(
            collective_id=1, has_side_effects=True, vmem_limit_bytes=58 << 20
        ),
    )(*args)


def shards(
    tokens,
    lengths,
    assignment,
    retrieval,
    enc_gain,
    enc_qkv,
    position_bias,
    enc_output,
    final_gain,
    embedding,
    dec_tokens,
    dec_gain,
    cross_query,
    cross_keyval,
    cross_output,
):
    found, mask_add, claims, extra = lookup(
        dec_tokens.T, lengths, assignment, retrieval, embedding
    )
    onehot = bucket_onehot(SEQ, BUCKETS, MAXDIST)
    onehot = np.concatenate([onehot[:, 255:], np.zeros((BUCKETS, 1)), onehot[:, :255]], axis=1)
    encoded, decoded = encoder(
        (
            tokens,
            enc_gain.reshape(1, D),
            enc_qkv,
            position_bias,
            jnp.asarray(onehot, jnp.bfloat16),
            mask_add,
            enc_output,
            final_gain.reshape(1, D),
            found,
            dec_gain.reshape(1, 128),
            cross_query,
            cross_keyval,
            cross_output,
            claims,
            extra,
        )
    )
    return (encoded, decoded.reshape(CLAIMS, POS, 32))


def solution(mesh):
    in_specs = (
        P("psg", None),
        P("psg"),
        P("psg"),
        P("psg"),
        P(),
        P(None, "psg", "mp"),
        P("mp", None),
        P("mp", "psg"),
        P(),
        P("mp", "psg"),
        P(),
        P("psg"),
        P("psg", "mp"),
        P(None, "psg", "mp"),
        P("mp", "psg"),
    )
    out_specs = (P("psg", "mp"), P(None, None, ("psg", "mp")))
    return jax.shard_map(shards, mesh=mesh, in_specs=in_specs, out_specs=out_specs, check_vma=False)
```

```python
import functools
import math

import jax
import jax.numpy as jnp
import numpy as np
from jax import lax
from jax.experimental import pallas as pl
from jax.experimental.pallas import tpu as pltpu
from jax.sharding import PartitionSpec as P

D = 4096
HEAD_DIM = 64
BUCKETS = 32
MAXDIST = 128
SEQ = 256
CLAIMS = 4
POS = 2
NPSG = 32
NMP = 4
EPSILON = 1e-06
MASKED = -1e30
MESH = pl.DeviceIdType.MESH
ANY = pl.BlockSpec(memory_space=pl.ANY)
VMEM = pl.BlockSpec(memory_space=pltpu.VMEM)


def bucket_onehot(length, buckets, max_distance):
    halfway = buckets // 2
    exact_max = halfway // 2
    relative_list = list(range(-(length - 1), length))
    beyond_list = [
        min(
            halfway - 1,
            exact_max
            + math.floor(
                math.log(max(abs(shift), 1) / exact_max)
                / math.log(max_distance / exact_max)
                * (halfway - exact_max)
            ),
        )
        for shift in relative_list
    ]
    relative = np.array(relative_list)
    beyond = np.array(beyond_list)
    distance = np.abs(relative)
    bucket_ids = np.where(relative > 0, halfway, 0) + np.where(
        distance < exact_max, distance, beyond
    )
    return (bucket_ids[None, :] == np.arange(buckets)[:, None]).astype(np.float32)


def place():
    psg = lax.axis_index("psg")
    mp = lax.axis_index("mp")
    return psg // 8, (psg // 4) % 2, psg % 4, mp // 2, mp % 2


def psg_of(x, yl, z):
    return x * 8 + yl * 4 + z


def remote(src, dst, send_sem, recv_sem, device):
    return pltpu.make_async_remote_copy(
        src_ref=src,
        dst_ref=dst,
        send_sem=send_sem,
        recv_sem=recv_sem,
        device_id=device,
        device_id_type=MESH,
    )


def signal(device):
    pl.semaphore_signal(
        pltpu.get_barrier_semaphore(), inc=1, device_id=device, device_id_type=MESH
    )


def lookup_kernel(ids, lengths, assignment, retrieval, table, out, mask_add, claims, extra, rows, sems):
    copies = []
    held = []
    base = lax.axis_index("mp") * table.shape[0]
    for i in range(CLAIMS * POS):
        local = ids[i % POS, i // POS] - base
        inside = jnp.logical_and(local >= 0, local < table.shape[0])
        local = jnp.clip(local, 0, table.shape[0] - 1)
        start = pl.multiple_of((local // 16) * 16, 16)
        held.append(jnp.where(inside, local - start, -1))
        copies.append(
            pltpu.make_async_copy(table.at[pl.ds(start, 16), :], rows.at[i], sems.at[i])
        )
        copies[-1].start()
    slot = lax.broadcasted_iota(jnp.int32, (16, SEQ), 1)
    for p in range(4):
        add = jnp.where(slot < lengths[p], 0.0, MASKED)
        mask_add[p] = add[:8]
        extra[p] = add + retrieval[p]
        claims[p] = jnp.zeros((16, SEQ), jnp.int32) + assignment[p]
    at = lax.broadcasted_iota(jnp.int32, (16, 128), 0)
    for i in range(CLAIMS * POS):
        copies[i].wait()
        picked = jnp.where(at == held[i], rows[i].astype(jnp.float32), 0.0)
        out[pl.ds(i, 1), :] = jnp.sum(picked, axis=0, keepdims=True)


def lookup(ids, lengths, assignment, retrieval, table):
    smem = pl.BlockSpec(memory_space=pltpu.SMEM)
    f32 = jnp.float32
    return pl.pallas_call(
        lookup_kernel,
        out_shape=(
            jax.ShapeDtypeStruct((CLAIMS * POS, 128), f32),
            jax.ShapeDtypeStruct((4, 8, SEQ), f32),
            jax.ShapeDtypeStruct((4, 16, SEQ), jnp.int32),
            jax.ShapeDtypeStruct((4, 16, SEQ), f32),
        ),
        in_specs=[smem] * 4 + [ANY],
        out_specs=(VMEM,) * 4,
        scratch_shapes=[
            pltpu.VMEM((CLAIMS * POS, 16, 128), jnp.bfloat16),
            pltpu.SemaphoreType.DMA((CLAIMS * POS,)),
        ],
    )(ids, lengths, assignment, retrieval, table)


def split3(values):
    high = values.astype(jnp.bfloat16)
    rest = values - high.astype(jnp.float32)
    middle = rest.astype(jnp.bfloat16)
    low = (rest - middle.astype(jnp.float32)).astype(jnp.bfloat16)
    return jnp.concatenate([high, middle, low], axis=0)


def dot3(values, weights, contract=0):
    n = values.shape[0]
    parts = lax.dot_general(
        split3(values),
        weights,
        (((1,), (contract,)), ((), ())),
        preferred_element_type=jnp.float32,
    )
    return parts[:n] + parts[n : 2 * n] + parts[2 * n :]


ALL = slice(None)


def encoder_kernel(
    tokens,
    enc_gain,
    w_ref,
    bias_in,
    onehot,
    mask_add,
    enc_output,
    final_gain,
    found,
    dec_gain,
    cross_query,
    cross_keyval,
    cross_output,
    claims,
    extra,
    enc_hbm,
    dec_out,
    enc_out,
    g_ref,
    normed,
    acc,
    qkv,
    e_ref,
    u_ref,
    att,
    transit,
    bias,
    tok_here,
    block,
    mp_buf,
    x_buf,
    yz_buf,
    sc_src,
    sc_in,
    all_w,
    all_st,
    lhs,
    y_src,
    y_zin,
    st_z,
    y_one,
    st_one,
    y_in,
    st_in,
    x_buf2,
    yz_buf2,
    mp_buf2,
    send_sem,
    recv_sem,
    own_sem,
):
    f32 = jnp.float32
    bf16 = jnp.bfloat16
    x, yl, z, yh, core = place()
    psg = lax.axis_index("psg")
    mp = lax.axis_index("mp")
    y = yh * 2 + yl
    y_dev = (psg_of(x, 1 - yl, z), mp)

    def dev(axis, step):
        if axis == "x":
            return (psg_of(lax.rem(x + step, 4), yl, z), mp)
        return (psg_of(x, yl, lax.rem(z + step, 4)), mp)

    def yz_dev(k):
        t = lax.rem(yl * 4 + z + k, 8)
        return (x * 8 + t, mp)

    def mp_dev(k):
        return (psg, lax.rem(mp + k, NMP))

    def y_step(step):
        t = lax.rem(y + step, 4)
        return (psg_of(x, lax.rem(t, 2), z), (t // 2) * 2 + core)

    other_core = (psg, yh * 2 + 1 - core)
    same_half = (x // 2) == yh
    yl_to = jnp.where(same_half, yl, 1 - yl)

    block_to = (psg_of(x, yl_to, z), x)
    mine = x == mp

    load_tokens = pltpu.make_async_copy(tokens, normed, own_sem.at[0])
    load_tokens.start()
    own = pltpu.make_async_copy(
        w_ref, g_ref.at[:, x, z, pl.ds(pl.multiple_of(yl * 128, 128), 128), :], own_sem.at[1]
    )
    own.start()
    load_here = pltpu.make_async_copy(
        tokens.at[:, pl.ds(pl.multiple_of(mp * 1024, 128), 1024)], tok_here, own_sem.at[2]
    )
    load_here.start()
    for k in range(1, 4):
        signal(dev("x", k))
        signal(mp_dev(k))
    for k in range(1, 8):
        signal(yz_dev(k))
    signal(y_step(1))
    signal(y_step(3))

    @pl.when(mine)
    def _():
        for k in range(1, 4):
            m = lax.rem(mp + k, NMP)
            signal((psg_of(x, jnp.where((m // 2) == yh, yl, 1 - yl), z), m))

    for k in range(8):
        frm = psg_of(lax.rem(x + k, 4), lax.rem(yl + k // 4, 2), z)
        if k == 0:
            pl.when(jnp.logical_not(mine))(functools.partial(signal, (frm, x)))
        else:
            signal((frm, x))

    def g(k, xs, zs, yls, cols=None):
        rows = ALL if yls is None else pl.ds(pl.multiple_of(yls * 128, 128), 128)
        c = ALL if cols is None else pl.ds(cols[0], cols[1])
        return g_ref.at[k, xs, zs, rows, c]

    def wide(c):
        return None if c is None else (c * 256, 256)

    def low_cols(c):
        return (0, 256) if c is None else (c * 128, 128)

    def high_cols(c):
        return (256, 256) if c is None else (256 + c * 128, 128)

    sent = []

    def send(t, src, dst, device):
        copy = remote(src, dst, send_sem.at[t], recv_sem.at[t], device)
        copy.start()
        sent.append(copy)
        return copy

    class Ring:
        def __init__(self, t, axis, piece, first=None):
            self.t, self.axis, self.piece = t, axis, piece
            self.at = x if axis == "x" else z
            src = piece(self.at) if first is None else first
            self.up = send(t, src, piece(self.at), dev(axis, 1))
            self.down = send(t + 1, src, piece(self.at), dev(axis, 3))

        def forward(self, then=None):
            below = lax.rem(self.at + 3, 4)
            above = lax.rem(self.at + 1, 4)
            self.up.wait_recv()
            up = self.piece(below, 0)
            self.f_up = send(self.t + 2, up, up, dev(self.axis, 1))
            if then is not None:
                then(1, below)
            self.down.wait_recv()
            down = self.piece(above, 1)
            self.f_down = send(self.t + 3, down, down, dev(self.axis, 3))
            if then is not None:
                then(2, above)

        def end(self, then=None):
            self.f_up.wait_recv()
            self.f_down.wait_recv()
            if then is not None:
                then(3, lax.rem(self.at + 2, 4))

    go_step = jnp.where(core == 1, 1, 3)
    go_on = lax.rem(mp + go_step, 4) == x
    near = pl.ds(yh * 2, 2)
    far_half = pl.ds(2 - yh * 2, 2)

    class Blocks:
        def __init__(self, t, src, ref, own_t):
            self.t, self.ref, self.src = t, ref, src
            first = self.at(mp, yl, z)
            self.block = remote(src, first, send_sem.at[t], recv_sem.at[t + 1 + mp], block_to)
            self.keep = pltpu.make_async_copy(src, first, own_sem.at[own_t])
            n, f = self.at(near, yl, z), self.at(far_half, 1 - yl, z)
            self.ys = [
                remote(n, n, send_sem.at[t + 5], recv_sem.at[t + 5], y_dev),
                remote(f, f, send_sem.at[t + 6], recv_sem.at[t + 6], y_dev),
            ]

        def at(self, ms, yls, zs):
            col = pl.multiple_of((yls * 4 + zs) * 128, 128)
            return self.ref.at[ms, :, pl.ds(col, 128)]

        def x_copy(self, c, step, t):
            part = self.at(ALL, c, z)
            return remote(
                part, part, send_sem.at[self.t + t], recv_sem.at[self.t + 13 + c], dev("x", step)
            )

        def start(self):
            pl.when(mine)(self.keep.start)
            pl.when(jnp.logical_not(mine))(self.block.start)

        def across(self):
            @pl.when(mine)
            def _():
                for k in range(1, 4):
                    m = lax.rem(mp + k, NMP)
                    remote(
                        self.src,
                        self.at(m, yl, z),
                        send_sem.at[self.t],
                        recv_sem.at[self.t + 1 + m],
                        y_dev,
                    ).wait_recv()
                self.keep.wait()
                for copy in self.ys:
                    copy.start()

        def along(self):
            @pl.when(mine)
            def _():
                for copy in self.ys:
                    copy.wait_recv()
                for c in range(2):
                    self.x_copy(c, 1, 7 + c).start()
                    self.x_copy(c, 3, 9 + c).start()

        def forward(self):
            @pl.when(go_on)
            def _():
                for c in range(2):
                    self.x_copy(c, 1, 7 + c).wait_recv()
                    self.x_copy(c, go_step, 11 + c).start()

        def arrive(self):
            @pl.when(jnp.logical_not(jnp.logical_or(mine, go_on)))
            def _():
                for c in range(2):
                    self.x_copy(c, 1, 7 + c).wait_recv()

        def ring(self):
            t = self.t
            parts = [self.at(ALL, i, z) for i in range(2)]
            self.up = [send(t + 15 + i, parts[i], parts[i], dev("z", 1)) for i in range(2)]
            self.down = [send(t + 17 + i, parts[i], parts[i], dev("z", 3)) for i in (1, 0)]

        def ring_forward(self):
            self.up[0].wait_recv()
            part = self.at(ALL, 0, lax.rem(z + 3, 4))
            self.f_up = send(self.t + 19, part, part, dev("z", 1))
            self.down[0].wait_recv()
            part = self.at(ALL, 1, lax.rem(z + 1, 4))
            self.f_down = send(self.t + 20, part, part, dev("z", 3))

        def ring_end(self):
            for copy in (self.up[1], self.down[1], self.f_up, self.f_down):
                copy.wait_recv()

        def finish(self):
            @pl.when(mine)
            def _():
                for copy in self.ys:
                    copy.wait_send()
                for c in range(2):
                    self.x_copy(c, 1, 7 + c).wait_send()
                    self.x_copy(c, 3, 9 + c).wait_send()

            pl.when(jnp.logical_not(mine))(self.block.wait_send)

            @pl.when(go_on)
            def _():
                for c in range(2):
                    self.x_copy(c, go_step, 11 + c).wait_send()

    e_blocks = Blocks(188, enc_output, e_ref, 3)
    u_blocks = Blocks(209, block, u_ref, 4)

    pl.semaphore_wait(pltpu.get_barrier_semaphore(), jnp.where(mine, 22, 24))

    yd = send(0, w_ref.at[0], g(0, x, z, yl), y_dev)
    ye = send(1, w_ref.at[1], g(1, x, z, yl), y_dev)
    a1 = Ring(
        4, "x", lambda v, c=None: g(2, v, z, yl, low_cols(c)), w_ref.at[2, :, pl.ds(0, 256)]
    )
    b1 = Ring(
        8, "z", lambda v, c=None: g(2, x, v, yl, high_cols(c)), w_ref.at[2, :, pl.ds(256, 256)]
    )
    mp_buf[mp] = found[...]
    mps = [send(52 + k, found, mp_buf.at[mp], mp_dev(k)) for k in range(1, 4)]
    e_blocks.start()
    own.wait()

    d3, e3, yas, ybs = [None] * 4, [None] * 4, [None] * 4, [None] * 4

    def start_d3(i, u):
        d3[i] = Ring(140 + 4 * i, "z", lambda v, c=None: g(0, u, v, None, wide(c)))

    def start_e3(i, u):
        e3[i] = Ring(156 + 4 * i, "x", lambda v, c=None: g(1, v, u, None, wide(c)))

    def start_ya(i, u):
        plane = g(2, ALL, u, yl, low_cols(None))
        yas[i] = send(172 + i, plane, plane, y_dev)

    def start_yb(i, u):
        plane = g(2, u, ALL, yl, high_cols(None))
        ybs[i] = send(176 + i, plane, plane, y_dev)

    a1.forward()
    b1.forward()
    yd.wait_recv()
    d2 = Ring(20, "x", lambda v, c=None: g(0, v, z, None, wide(c)))
    ye.wait_recv()
    e2 = Ring(24, "z", lambda v, c=None: g(1, x, v, None, wide(c)))
    start_d3(0, x)
    start_e3(0, z)
    a1.end()
    a2 = Ring(12, "z", lambda v, c=None: g(2, ALL, v, yl, low_cols(c)))
    start_ya(0, z)
    b1.end()
    b2 = Ring(16, "x", lambda v, c=None: g(2, v, ALL, yl, high_cols(c)))
    start_yb(0, x)
    e_blocks.across()

    for copy in mps:
        copy.wait_recv()
    emb = mp_buf[0] + mp_buf[1] + mp_buf[2] + mp_buf[3]
    terms = dot3(emb * dec_gain[...], cross_query[...])
    squares = jnp.sum(emb * emb, axis=1, keepdims=True)
    x_buf[x, :, pl.ds(0, 512)] = terms
    x_buf[x, :, pl.ds(512, 128)] = jnp.broadcast_to(squares, (8, 128))
    xs = [send(56 + k, x_buf.at[x], x_buf.at[x], dev("x", k)) for k in range(1, 4)]

    e_blocks.along()
    load_tokens.wait()

    def norm_rows(first, count):
        def body(i, c):
            rows = pl.ds(pl.multiple_of(i * 16, 16), 16)
            values = normed[rows, :].astype(f32)
            mean = jnp.sum(values * values, axis=1, keepdims=True) / D
            inverse = lax.rsqrt(mean + EPSILON)
            scaled = (values * inverse * enc_gain[...]).astype(bf16)
            for p in range(NPSG):
                to = ((p // 8) * 4 + p % 4) * 2 + (p // 4) % 2
                normed[rows, pl.ds(to * 128, 128)] = scaled[:, p * 128 : (p + 1) * 128]
            return c

        lax.fori_loop(first, first + count, body, 0)

    norm_rows(0, 8)
    d2.forward(start_d3)
    e2.forward(start_e3)

    norm_rows(8, 8)
    a2.forward(start_ya)
    b2.forward(start_yb)
    d2.end(start_d3)
    e2.end(start_e3)
    d3[0].forward()
    e3[0].forward()
    a2.end(start_ya)
    b2.end(start_yb)
    for copy in xs:
        copy.wait_recv()
    yz = yl * 4 + z
    yz_buf[yz] = x_buf[0] + x_buf[1] + x_buf[2] + x_buf[3]
    yzs = [send(60 + k, yz_buf.at[yz], yz_buf.at[yz], yz_dev(k)) for k in range(1, 8)]
    norm_rows(16, 16)
    d3[1].forward()
    e3[1].forward()
    e_blocks.forward()
    norm_rows(32, 16)
    d3[2].forward()
    e3[2].forward()

    for copy in yzs:
        copy.wait_recv()
    joined = yz_buf[0]
    for k in range(1, 8):
        joined = joined + yz_buf[k]
    cquery = joined[:, :512] * lax.rsqrt(joined[:, 512:513] / D + EPSILON)
    spread_q = jnp.broadcast_to(cquery[:, None, :], (8, 8, 512)).reshape(64, 512)
    head_of_row = lax.rem(lax.broadcasted_iota(jnp.int32, (64, 512), 0), 8)
    head_of_lane = lax.broadcasted_iota(jnp.int32, (64, 512), 1) // HEAD_DIM
    spread_q = jnp.where(head_of_row == head_of_lane, spread_q, 0.0)
    folded = dot3(spread_q, cross_keyval[0], 1)
    folded = folded * final_gain[:, pl.ds(pl.multiple_of(psg * 128, 128), 128)]
    high = folded.astype(bf16)
    block[pl.ds(0, 64), :] = high
    block[pl.ds(64, 64), :] = (folded - high.astype(f32)).astype(bf16)

    u_blocks.start()
    norm_rows(48, 16)
    d3[3].forward()
    e3[3].forward()
    e_blocks.arrive()
    e_blocks.ring()

    table = dot3(bias_in[...], onehot[...])
    for h in range(8):
        row = jnp.broadcast_to(table[h : h + 1], (SEQ, 512))
        bias[h] = pltpu.roll(row, 0, 1, stride=1, stride_axis=0)[:, :SEQ]

    def product(k, rows, xi, zi):
        at = pl.multiple_of((xi * 4 + zi) * 256, 256)
        return jnp.dot(
            normed[rows, pl.ds(at, 256)], g_ref[k, xi, zi], preferred_element_type=f32
        )

    def project(step):
        def body(i, c):
            step(pl.ds(pl.multiple_of(i * 256, 256), 256))
            return c

        lax.fori_loop(0, 4, body, 0)

    def first_q(rows):
        total = None
        for xi in range(4):
            for dz in (0, 1, 3):
                term = product(0, rows, xi, lax.rem(z + dz, 4))
                total = term if total is None else total + term
        acc[0, rows, :] = total

    def first_k(rows):
        total = None
        for zi in range(4):
            for dx in (0, 1, 3):
                term = product(1, rows, lax.rem(x + dx, 4), zi)
                total = term if total is None else total + term
        acc[1, rows, :] = total

    def all_v(rows):
        total = None
        for xi in range(4):
            for zi in range(4):
                term = product(2, rows, xi, zi)
                total = term if total is None else total + term
        qkv[2, rows, :] = total.astype(bf16)

    def last_q(rows):
        total = acc[0, rows, :]
        for xi in range(4):
            total = total + product(0, rows, xi, lax.rem(z + 2, 4))
        qkv[0, rows, :] = total.astype(bf16)

    def last_k(rows):
        total = acc[1, rows, :]
        for zi in range(4):
            total = total + product(1, rows, lax.rem(x + 2, 4), zi)
        qkv[1, rows, :] = total.astype(bf16)

    project(first_q)
    u_blocks.across()
    project(first_k)
    u_blocks.along()
    for copy in yas + ybs:
        copy.wait_recv()
    project(all_v)
    u_blocks.forward()
    for ring in d3:
        ring.end()
    project(last_q)
    for ring in e3:
        ring.end()
    project(last_k)

    lane = lax.broadcasted_iota(jnp.int32, (SEQ, 128), 1)

    def attend(p):
        rows = pl.ds(p * SEQ, SEQ)

        def body(j, c):
            lanes = pl.ds(pl.multiple_of(j * 128, 128), 128)
            q2 = qkv[0, rows, lanes]
            k2 = qkv[1, rows, lanes]
            v2 = qkv[2, rows, lanes]
            outs = []
            for t in range(2):
                qt = jnp.where((lane // HEAD_DIM) == t, q2, jnp.zeros_like(q2))
                s = lax.dot_general(
                    qt, k2, (((1,), (1,)), ((), ())), preferred_element_type=f32
                )
                s = s + bias[2 * j + t] + mask_add[p, pl.ds(0, 1), :]
                wts = jnp.exp(s - jnp.max(s, axis=1, keepdims=True))
                scale = 1.0 / jnp.sum(wts, axis=1, keepdims=True)
                outs.append(
                    jnp.dot((wts * scale).astype(bf16), v2, preferred_element_type=f32)
                )
            att[mp, rows, lanes] = jnp.where(lane < HEAD_DIM, outs[0], outs[1]).astype(bf16)
            return c

        lax.fori_loop(0, 4, body, 0)

    hops, ends, cores, lasts = [], [], [], []
    far = (1 - yh) * 2 + core

    def hand_out(p):
        rows = pl.ds(p * SEQ, SEQ)
        cores.append(send(68 + p, att.at[mp, rows], att.at[mp, rows], other_core))
        hops.append(
            send(72 + p, att.at[mp, rows], transit.at[p], y_step(1 if p % 2 == 0 else 3))
        )

    def hand_on(p):
        rows = pl.ds(p * SEQ, SEQ)
        hops[p].wait_recv()
        frm = lax.rem(y + (3 if p % 2 == 0 else 1), 4)
        slot = (frm // 2) * 2 + core
        ends.append(
            send(76 + p, transit.at[p], att.at[slot, rows], y_step(1 if p % 2 == 0 else 3))
        )

    def hand_over(p):
        rows = pl.ds(p * SEQ, SEQ)
        ends[p].wait_recv()
        lasts.append(send(80 + p, att.at[far, rows], att.at[far, rows], other_core))

    attend(0)
    hand_out(0)
    u_blocks.arrive()
    u_blocks.ring()
    attend(1)
    hand_out(1)
    hand_on(0)
    e_blocks.ring_forward()
    attend(2)
    hand_out(2)
    hand_on(1)
    hand_over(0)
    u_blocks.ring_forward()
    attend(3)
    hand_out(3)
    hand_on(2)
    hand_over(1)
    hand_on(3)
    load_here.wait()
    e_blocks.ring_end()
    u_blocks.ring_end()
    hand_over(2)
    hand_over(3)
    def out_project(p):
        rows = pl.ds(p * SEQ, SEQ)

        def out_cols(i, c):
            cols = pl.ds(pl.multiple_of(i * 512, 512), 512)
            total = None
            for m in range(NMP):
                term = jnp.dot(
                    att[m, rows, :], e_ref[m, :, cols], preferred_element_type=f32
                ).astype(bf16).astype(f32)
                total = term if total is None else total + term
            enc_out[rows, cols] = (tok_here[rows, cols].astype(f32) + total).astype(bf16)
            return c

        lax.fori_loop(0, 2, out_cols, 0)

    def cross_scores(p):
        enc = enc_out[pl.ds(p * SEQ, SEQ), :]
        wide_enc = enc.astype(f32)
        squares = jnp.sum(wide_enc * wide_enc, axis=1, keepdims=True)
        squares = jnp.broadcast_to(squares, (SEQ, 128)).T[:8]
        for m in range(NMP):
            both = lax.dot_general(
                u_ref[m], enc, (((1,), (1,)), ((), ())),
                preferred_element_type=f32,
            )
            both = both[:64] + both[64:]
            picked = jnp.zeros((16, SEQ), f32)
            for c in range(CLAIMS):
                picked = jnp.where(claims[p] == c, both[c * 16 : (c + 1) * 16], picked)
            sc_src[m, p, pl.ds(0, 16), :] = picked
            sc_src[m, p, pl.ds(16, 8), :] = squares
        out = []
        for k in range(1, 4):
            to = lax.rem(mp + k, NMP)
            out.append(
                send(84 + p * 3 + k - 1, sc_src.at[to, p], sc_in.at[mp, p], mp_dev(k))
            )
        sc_in[mp, p] = sc_src[mp, p]
        return out

    scs, leave = [], []
    for p in range(4):
        cores[p].wait_recv()
        lasts[p].wait_recv()
        out_project(p)
        scs.append(cross_scores(p))
        rows = pl.ds(p * SEQ, SEQ)
        leave.append(pltpu.make_async_copy(enc_out.at[rows], enc_hbm.at[rows], own_sem.at[5 + p]))
        leave[-1].start()

    crosses, inverses, maxima = [], [], []
    for p in range(4):
        for copy in scs[p]:
            copy.wait_recv()
        raw = sc_in[0, p] + sc_in[1, p] + sc_in[2, p] + sc_in[3, p]
        inverse = lax.rsqrt(raw[16:17] / D + EPSILON)
        cross = raw[:16] * inverse + extra[p]
        crosses.append(cross)
        inverses.append(inverse)
        maxima.append(jnp.broadcast_to(jnp.max(cross, axis=1, keepdims=True), (16, SEQ)))
    claim_max = []
    for c in range(CLAIMS):
        top = jnp.full((16, SEQ), MASKED, f32)
        for p in range(4):
            top = jnp.maximum(top, jnp.where(claims[p] == c, maxima[p], MASKED))
        claim_max.append(top)
    sums = []
    for p in range(4):
        chosen = claim_max[0]
        for c in range(1, CLAIMS):
            chosen = jnp.where(claims[p] == c, claim_max[c], chosen)
        wts = jnp.exp(crosses[p] - chosen)
        sums.append(jnp.broadcast_to(jnp.sum(wts, axis=1, keepdims=True), (16, SEQ)))
        all_w[mp, p] = (wts * inverses[p]).astype(bf16)
    totals = []
    for c in range(CLAIMS):
        total = jnp.zeros((16, SEQ), f32)
        for p in range(4):
            total = total + jnp.where(claims[p] == c, sums[p], 0.0)
        totals.append(total)
    first_row = lax.broadcasted_iota(jnp.int32, (8, 128), 0) == 0

    def lanes_of(parts, fill):
        column = jnp.concatenate([part[:, :128] for part in parts], axis=0)
        column = jnp.concatenate([column, jnp.full((64, 128), fill, f32)], axis=0)
        return column.T[:8]

    all_st[mp] = jnp.where(first_row, lanes_of(claim_max, MASKED), lanes_of(totals, 0.0))
    ws = [send(96 + k, all_w.at[mp], all_w.at[mp], mp_dev(k)) for k in range(3 + 1) if k]
    sts = [send(99 + k, all_st.at[mp], all_st.at[mp], mp_dev(k)) for k in range(3 + 1) if k]
    for copy in ws + sts:
        copy.wait_recv()

    for p in range(4):
        for m in range(NMP):
            w_mp = all_w[m, p].astype(f32)
            for c in range(CLAIMS):
                lhs[p, pl.ds(m * 64 + c * 16, 16), :] = jnp.where(
                    claims[p] == c, w_mp, 0.0
                ).astype(bf16)
    y_copies = []
    st_copies = [send(106 + k, all_st, st_z.at[z], dev("z", k)) for k in range(1, 4)]
    for i in range(2):
        total = None
        for p in range(4):
            term = jnp.dot(
                lhs[p], enc_out[pl.ds(p * SEQ, SEQ), pl.ds(i * 512, 512)],
                preferred_element_type=f32,
            )
            total = term if total is None else total + term
        for zt in range(4):
            y_src[zt, i] = total[:, zt * 128 : (zt + 1) * 128].astype(bf16)
        for k in range(1, 4):
            tz = lax.rem(z + k, 4)
            y_copies.append(
                send((103, 110)[i] + k, y_src.at[tz, i], y_zin.at[z, i], dev("z", k))
            )
    y_zin[z] = y_src[z]
    st_z[z] = all_st[...]

    def merge(stats, rows):
        top = stats[0][0:1]
        for st in stats[1:]:
            top = jnp.maximum(top, st[0:1])
        total = jnp.zeros((1, 128), f32)
        results = [jnp.zeros((64, 128), f32) for _ in rows[0]]
        for st, these in zip(stats, rows):
            scale = jnp.exp(st[0:1] - top)
            total = total + scale * st[1:2]
            column = jnp.broadcast_to(scale, (128, 128)).T[:64]
            results = [r + column * t.astype(f32) for r, t in zip(results, these)]
        both = jnp.where(
            first_row, jnp.broadcast_to(top, (8, 128)), jnp.broadcast_to(total, (8, 128))
        )
        return both, results

    for copy in y_copies + st_copies:
        copy.wait_recv()
    for m in range(NMP):
        part = pl.ds(m * 64, 64)
        both, results = merge(
            [st_z[j, m] for j in range(4)],
            [[y_zin[j, i, part, :] for i in range(2)] for j in range(4)],
        )
        st_one[m] = both
        for i in range(2):
            y_one[i, m] = results[i].astype(bf16)
    def to_owner(k):
        to_yl, m = lax.rem(yl + k // 4, 2), lax.rem(mp + k % 4, NMP)
        target = (psg_of(mp, to_yl, z), m)
        slot = x * 2 + yl
        return (
            remote(
                y_one.at[to_yl, m], y_in.at[slot], send_sem.at[230 + k], recv_sem.at[230 + slot], target
            ),
            remote(
                st_one.at[m], st_in.at[slot], send_sem.at[238 + k], recv_sem.at[238 + slot], target
            ),
        )

    def from_source(k):
        frm, frm_yl = lax.rem(x + k, 4), lax.rem(yl + k // 4, 2)
        target = (psg_of(frm, frm_yl, z), x)
        slot = frm * 2 + frm_yl
        return (
            remote(
                y_one.at[0, 0], y_in.at[slot], send_sem.at[230], recv_sem.at[230 + slot], target
            ),
            remote(st_one.at[0], st_in.at[slot], send_sem.at[238], recv_sem.at[238 + slot], target),
        )

    @pl.when(mine)
    def _():
        y_in[x * 2 + yl] = y_one[yl, mp]
        st_in[x * 2 + yl] = st_one[mp]

    @pl.when(jnp.logical_not(mine))
    def _():
        for copy in to_owner(0):
            copy.start()

    for k in range(1, 8):
        for copy in to_owner(k):
            copy.start()

    @pl.when(jnp.logical_not(mine))
    def _():
        for copy in from_source(0):
            copy.wait_recv()

    for k in range(1, 8):
        for copy in from_source(k):
            copy.wait_recv()
    both, results = merge([st_in[j] for j in range(8)], [[y_in[j]] for j in range(8)])
    total = jnp.broadcast_to(both[1:2], (128, 128)).T[:64]
    mean_rows = results[0] / total
    mean_rows = mean_rows * final_gain[:, pl.ds(pl.multiple_of(psg * 128, 128), 128)]

    products = dot3(mean_rows, cross_keyval[1])
    products = jnp.where(head_of_row == head_of_lane, products, 0.0)
    x_buf2[x] = jnp.sum(products.reshape(8, 8, 512), axis=1)
    xs = [send(120 + k, x_buf2.at[x], x_buf2.at[x], dev("x", k)) for k in range(1, 4)]
    for copy in xs:
        copy.wait_recv()
    yz_buf2[yz] = x_buf2[0] + x_buf2[1] + x_buf2[2] + x_buf2[3]
    yzs = [send(124 + k, yz_buf2.at[yz], yz_buf2.at[yz], yz_dev(k)) for k in range(1, 8)]
    for copy in yzs:
        copy.wait_recv()
    cross_attn = yz_buf2[0]
    for k in range(1, 8):
        cross_attn = cross_attn + yz_buf2[k]
    mp_buf2[mp] = dot3(cross_attn, cross_output[...])
    lasts = [send(132 + k, mp_buf2.at[mp], mp_buf2.at[mp], mp_dev(k)) for k in range(1, 4)]
    for copy in lasts:
        copy.wait_recv()
    final = (mp_buf2[0] + mp_buf2[1] + mp_buf2[2] + mp_buf2[3]) + (
        mp_buf[0] + mp_buf[1] + mp_buf[2] + mp_buf[3]
    )
    share = final[:, :32]
    for m in range(1, NMP):
        share = jnp.where(mp == m, final[:, m * 32 : (m + 1) * 32], share)
    dec_out[...] = share.astype(bf16)

    for copy in sent:
        copy.wait_send()
    for copy in leave:
        copy.wait()
    for k in range(1, 8):
        for copy in to_owner(k):
            copy.wait_send()

    @pl.when(jnp.logical_not(mine))
    def _():
        for copy in to_owner(0):
            copy.wait_send()

    e_blocks.finish()
    u_blocks.finish()


def encoder(args):
    tok_rows = args[0].shape[0]
    bf16 = jnp.bfloat16
    f32 = jnp.float32
    return pl.pallas_call(
        encoder_kernel,
        out_shape=(
            jax.ShapeDtypeStruct((tok_rows, 1024), bf16),
            jax.ShapeDtypeStruct((CLAIMS * POS, 32), bf16),
        ),
        in_specs=[ANY, VMEM, ANY, VMEM, VMEM, VMEM, ANY] + [VMEM] * 8,
        out_specs=(ANY, VMEM),
        scratch_shapes=[
            pltpu.VMEM((tok_rows, 1024), bf16),
            pltpu.VMEM((3, 4, 4, 256, 512), bf16),
            pltpu.VMEM((tok_rows, D), bf16),
            pltpu.VMEM((2, tok_rows, 512), jnp.float32),
            pltpu.VMEM((3, tok_rows, 512), bf16),
            pltpu.VMEM((NMP, 512, 1024), bf16),
            pltpu.VMEM((NMP, 128, 1024), bf16),
            pltpu.VMEM((NMP, tok_rows, 512), bf16),
            pltpu.VMEM((4, SEQ, 512), bf16),
            pltpu.VMEM((8, SEQ, SEQ), jnp.float32),
            pltpu.VMEM((tok_rows, 1024), bf16),
            pltpu.VMEM((128, 128), bf16),
            pltpu.VMEM((NMP, 8, 128), jnp.float32),
            pltpu.VMEM((4, 8, 640), jnp.float32),
            pltpu.VMEM((8, 8, 640), f32),
            pltpu.VMEM((NMP, 4, 24, SEQ), f32),
            pltpu.VMEM((NMP, 4, 24, SEQ), f32),
            pltpu.VMEM((NMP, 4, 16, SEQ), bf16),
            pltpu.VMEM((NMP, 8, 128), f32),
            pltpu.VMEM((4, 256, SEQ), bf16),
            pltpu.VMEM((4, 2, 256, 128), bf16),
            pltpu.VMEM((4, 2, 256, 128), bf16),
            pltpu.VMEM((4, NMP, 8, 128), f32),
            pltpu.VMEM((2, NMP, 64, 128), bf16),
            pltpu.VMEM((NMP, 8, 128), f32),
            pltpu.VMEM((8, 64, 128), bf16),
            pltpu.VMEM((8, 8, 128), f32),
            pltpu.VMEM((4, 8, 512), f32),
            pltpu.VMEM((8, 8, 512), f32),
            pltpu.VMEM((NMP, 8, 128), f32),
            pltpu.SemaphoreType.DMA((246,)),
            pltpu.SemaphoreType.DMA((246,)),
            pltpu.SemaphoreType.DMA((9,)),
        ],
        compiler_params=pltpu.CompilerParams(
            collective_id=1, has_side_effects=True, vmem_limit_bytes=58 << 20
        ),
    )(*args)


def shards(
    tokens,
    lengths,
    assignment,
    retrieval,
    enc_gain,
    enc_qkv,
    position_bias,
    enc_output,
    final_gain,
    embedding,
    dec_tokens,
    dec_gain,
    cross_query,
    cross_keyval,
    cross_output,
):
    found, mask_add, claims, extra = lookup(
        dec_tokens.T, lengths, assignment, retrieval, embedding
    )
    onehot = bucket_onehot(SEQ, BUCKETS, MAXDIST)
    onehot = np.concatenate([onehot[:, 255:], np.zeros((BUCKETS, 1)), onehot[:, :255]], axis=1)
    encoded, decoded = encoder(
        (
            tokens,
            enc_gain.reshape(1, D),
            enc_qkv,
            position_bias,
            jnp.asarray(onehot, jnp.bfloat16),
            mask_add,
            enc_output,
            final_gain.reshape(1, D),
            found,
            dec_gain.reshape(1, 128),
            cross_query,
            cross_keyval,
            cross_output,
            claims,
            extra,
        )
    )
    return (encoded, decoded.reshape(CLAIMS, POS, 32))


def solution(mesh):
    in_specs = (
        P("psg", None),
        P("psg"),
        P("psg"),
        P("psg"),
        P(),
        P(None, "psg", "mp"),
        P("mp", None),
        P("mp", "psg"),
        P(),
        P("mp", "psg"),
        P(),
        P("psg"),
        P("psg", "mp"),
        P(None, "psg", "mp"),
        P("mp", "psg"),
    )
    out_specs = (P("psg", "mp"), P(None, None, ("psg", "mp")))
    return jax.shard_map(shards, mesh=mesh, in_specs=in_specs, out_specs=out_specs, check_vma=False)
```
